32 devices in a mesh: rep: 4 (over y, x), fsdp: 8 (over z, core).
Axes of the slice: x: 2, y: 2, z: 4, core: 2. Of those that a mesh axis runs over, the one named last changes fastest.
Arguments:
- language: float32 [2560, 768], P(('rep', 'fsdp')), may hold values from -6 to 6
- vision: float32 [4608, 768], P(('rep', 'fsdp')), may hold values from -6 to 6
- lengths: int32 [128], P(('rep', 'fsdp')), may hold values from 5 to 20
- attn_weights: bfloat16 [3, 4, 768, 768], P(None, None, 'fsdp'), may hold values from -0.21875 to 0.21875
- attn_vectors: bfloat16 [3, 5, 768], P(None, None, 'fsdp'), may hold values from -1 to 1
- ffn_up: bfloat16 [2, 768, 3072], P(None, 'fsdp'), may hold values from -0.21875 to 0.21875
- ffn_up_bias: bfloat16 [2, 3072], P(None, 'fsdp'), may hold values from -1 to 1
- ffn_down: bfloat16 [2, 3072, 768], P(None, 'fsdp'), may hold values from -0.109375 to 0.109375
- ffn_vectors: bfloat16 [2, 3, 768], P(None, None, 'fsdp'), may hold values from -1 to 1
- language_cot: float32 [2560, 768], P(('rep', 'fsdp')), may hold values from -6 to 6
- vision_cot: float32 [4608, 768], P(('rep', 'fsdp')), may hold values from -6 to 6
Outputs:
- language_out: float32 [2560, 768], P(('rep', 'fsdp'))
- vision_out: float32 [4608, 768], P(('rep', 'fsdp'))
- language_grad: float32 [2560, 768], P(('rep', 'fsdp'))
- vision_grad: float32 [4608, 768], P(('rep', 'fsdp'))
- grad_attn_weights: float32 [3, 4, 768, 768], P(None, None, 'fsdp')
- grad_attn_vectors: float32 [3, 5, 768], P(None, None, 'fsdp')
- grad_ffn_up: float32 [2, 768, 3072], P(None, 'fsdp')
- grad_ffn_up_bias: float32 [2, 3072], P(None, 'fsdp')
- grad_ffn_down: float32 [2, 3072, 768], P(None, 'fsdp')
- grad_ffn_vectors: float32 [2, 3, 768], P(None, None, 'fsdp')
The draws below stay inside these ranges and needn't reach their ends.
Inputs may be any that keep to these rules, and one draw needn't show every extreme that they name: lengths[i] is the number of real words of item i; its word slots from lengths[i] on are padding.
All inputs are finite; a program needn't handle non-finite values.
Results may differ from the reference program's by a relative error of at most 0.018.
Values may be sent and summed in bfloat16 or wider, within the bound.
A program may use at most 256 MiB of HBM per device.

```python
import math
import jax
import jax.numpy as jnp
from jax import lax

D = 768
HEADS = 12
FF = 3072
WORDS = 20
REGIONS = 36
ITEMS = 128


def touch_ends(result, rng, least, top_value):
    extent = result.shape
    spot = [jax.random.randint(jax.random.fold_in(rng, axis), (), 0, extent[axis]) for axis in range(len(extent))]
    result = result.at[tuple(spot)].set(least)
    longest = extent.index(max(extent))
    spot[longest] = (spot[longest] + 1) % extent[longest]
    return result.at[tuple(spot)].set(top_value)


def with_spikes(array, key, source, target, blocks, factor):
    def block_of(position):
        return (jnp.arange(array.shape[position]) // (array.shape[position] // blocks)).reshape((-1,) + (1,) * (array.ndim - 1 - position))

    one_side = jax.random.permutation(key, blocks)[block_of(target)]
    far = (block_of(target) + blocks // 2) % blocks
    return jnp.where((block_of(source) == one_side) | (block_of(source) == far), factor * array, array)


def level_of(own_key, dims, shards, low, high):
    level = 1.0
    for axis_at, blocks in shards:
        heights = jax.random.uniform(jax.random.fold_in(jax.random.fold_in(own_key, 6), axis_at), (blocks,), jnp.float32, low / len(shards), high / len(shards))
        level = level * jnp.repeat(jnp.exp(heights), dims[axis_at] // blocks).reshape((-1,) + (1,) * (len(dims) - 1 - axis_at))
    return level


def bell_draw(own_key, shape, width, bound, cuts=(), kind=jnp.bfloat16):
    level = level_of(own_key, shape, cuts, -0.22, 0.18) if cuts else 1.0
    result = jax.random.normal(own_key, shape, jnp.float32) * width * level
    return jnp.minimum(jnp.maximum(result, -bound), bound).astype(kind)


def gaussian_with(stream_key, extent, width, reach, pieces, heavy, kind=jnp.bfloat16):
    array = width * jax.random.normal(stream_key, extent, jnp.float32)
    if pieces:
        array = array * level_of(stream_key, extent, pieces, -0.22, 0.18)
    return jnp.clip(with_spikes(array, jax.random.fold_in(stream_key, 3), *heavy), -reach, reach).astype(kind)


def setup_inputs(seed: int = 0) -> dict:
    key_list = jax.random.split(jax.random.key(seed), 12)
    language = bell_draw(key_list[0], (ITEMS * WORDS, D), 1.0, 6.0, ((0, 32),), jnp.float32)
    vision = bell_draw(key_list[1], (ITEMS * REGIONS, D), 1.0, 6.0, ((0, 32),), jnp.float32)
    lengths = touch_ends(jax.random.randint(key_list[2], (ITEMS,), 5, WORDS + 1), jax.random.fold_in(key_list[2], 1), 5, WORDS).astype(jnp.int32)
    attn_weights = bell_draw(key_list[3], (3, 4, D, D), D ** -0.5, 0.21875, ((2, 8),))
    attn_vectors = bell_draw(key_list[4], (3, 5, D), 0.2, 1.0, ((2, 8),))
    ffn_up = bell_draw(key_list[5], (2, D, FF), D ** -0.5, 0.21875, ((1, 8),))
    ffn_up_bias = bell_draw(key_list[6], (2, FF), 0.2, 1.0, ((1, 8),))
    ffn_down = bell_draw(key_list[7], (2, FF, D), FF ** -0.5, 0.109375, ((1, 8),))
    ffn_vectors = bell_draw(key_list[8], (2, 3, D), 0.2, 1.0, ((2, 8),))
    language_cot = gaussian_with(key_list[9], (ITEMS * WORDS, D), 1.0, 6.0, ((0, 32),), (0, 1, 32, 2.75), jnp.float32)
    vision_cot = gaussian_with(key_list[10], (ITEMS * REGIONS, D), 1.0, 6.0, ((0, 32),), (0, 1, 32, 2.75), jnp.float32)
    return dict(language=language, vision=vision, lengths=lengths, attn_weights=attn_weights, attn_vectors=attn_vectors, ffn_up=ffn_up, ffn_up_bias=ffn_up_bias, ffn_down=ffn_down, ffn_vectors=ffn_vectors, language_cot=language_cot, vision_cot=vision_cot)


@jax.custom_vjp
def low(v):
    return lax.optimization_barrier(v.astype(jnp.bfloat16)).astype(jnp.float32)

@jax.custom_vjp
def low_back(v):
    return v

def low_keep(v):
    return (low(v), None)

def low_pass(kept, grad):
    return (grad,)

def back_keep(v):
    return (v, None)

def back_low(kept, grad):
    return (low(grad),)
low.defvjp(low_keep, low_pass)
low_back.defvjp(back_keep, back_low)

def layer_norm(values, gain, shift):
    mean = lax.optimization_barrier(jnp.mean(values, axis=-1, keepdims=True))
    centred = values - mean
    spread = lax.optimization_barrier(jnp.mean(centred * centred, axis=-1, keepdims=True))
    return centred * lax.rsqrt(spread + 1e-06) * (1.0 + gain) + shift

def project(inputs, matrix):
    return jnp.einsum('isd,de->ise', inputs, matrix, precision=lax.Precision.HIGHEST)

def attend(residual, query_low, key_low, weights, vector, key_bias):
    item_count, query_len, model_width = residual.shape
    key_len = key_low.shape[1]
    head_size = model_width // HEADS
    queries = low(low_back(project(query_low, weights[0]) + vector[0]))
    key_heads = low(low_back(project(key_low, weights[1])))
    values = low(low_back(project(key_low, weights[2]) + vector[1]))
    queries = queries.reshape(item_count, query_len, HEADS, head_size)
    key_heads = key_heads.reshape(item_count, key_len, HEADS, head_size)
    values = values.reshape(item_count, key_len, HEADS, head_size)
    scores = jnp.einsum('iqhd,ikhd->ihqk', queries, key_heads, precision=lax.Precision.HIGHEST) / math.sqrt(head_size)
    scores = low_back(scores + key_bias[:, None, None, :])
    attn_probs = low(jax.nn.softmax(scores, axis=-1))
    mixed_heads = jnp.einsum('ihqk,ikhd->iqhd', attn_probs, values, precision=lax.Precision.HIGHEST)
    mixed_heads = low(low_back(mixed_heads.reshape(item_count, query_len, model_width)))
    branch = low_back(project(mixed_heads, weights[3]) + vector[2])
    return layer_norm(residual + branch, vector[3], vector[4])

def feed_forward(residual, up_weight, up_bias, down_weight, vector):
    hidden = low_back(project(low(residual), up_weight) + up_bias)
    active = low(jax.nn.gelu(hidden, approximate=False))
    branch = low_back(project(active, down_weight) + vector[0])
    return layer_norm(residual + branch, vector[1], vector[2])

def cross_layer(language, vision, word_bias, attn_weights, attn_vectors, ffn_up, ffn_up_bias, ffn_down, ffn_vectors):
    region_bias = jnp.zeros(vision.shape[:2], jnp.float32)
    lang_low = low(language)
    visn_low = low(vision)
    lang_one = attend(language, lang_low, visn_low, attn_weights[0], attn_vectors[0], region_bias)
    visn_one = attend(vision, visn_low, lang_low, attn_weights[0], attn_vectors[0], word_bias)
    lang_one_low = low(lang_one)
    lang_two = attend(lang_one, lang_one_low, lang_one_low, attn_weights[1], attn_vectors[1], word_bias)
    visn_one_low = low(visn_one)
    visn_two = attend(visn_one, visn_one_low, visn_one_low, attn_weights[2], attn_vectors[2], region_bias)
    lang_three = feed_forward(lang_two, ffn_up[0], ffn_up_bias[0], ffn_down[0], ffn_vectors[0])
    visn_three = feed_forward(visn_two, ffn_up[1], ffn_up_bias[1], ffn_down[1], ffn_vectors[1])
    return (lang_three, visn_three)

def reference(language, vision, lengths, attn_weights, attn_vectors, ffn_up, ffn_up_bias, ffn_down, ffn_vectors, language_cot, vision_cot):
    block_items = 32
    block_count = ITEMS // block_items
    params = (attn_weights.astype(jnp.float32), attn_vectors.astype(jnp.float32), ffn_up.astype(jnp.float32), ffn_up_bias.astype(jnp.float32), ffn_down.astype(jnp.float32), ffn_vectors.astype(jnp.float32))
    blocks = (language.reshape(block_count, block_items, WORDS, D), vision.reshape(block_count, block_items, REGIONS, D), lengths.reshape(block_count, block_items), language_cot.reshape(block_count, block_items, WORDS, D), vision_cot.reshape(block_count, block_items, REGIONS, D))

    def group_step(totals, block):
        lang_block, visn_block, len_block, lang_cot_block, visn_cot_block = block
        word_bias = jnp.where(jnp.arange(WORDS)[None, :] < len_block[:, None], 0.0, -1000000000.0).astype(jnp.float32)

        def forward(lang_input, visn_input, *weights):
            return cross_layer(lang_input, visn_input, word_bias, *weights)
        outputs, pull_back = jax.vjp(forward, lang_block, visn_block, *params)
        grads = pull_back((lang_cot_block, visn_cot_block))
        totals = tuple((total + grad for total, grad in zip(totals, grads[2:])))
        return (totals, (outputs[0], outputs[1], grads[0], grads[1]))
    initial = tuple((jnp.zeros_like(param) for param in params))
    summed, results = lax.scan(group_step, initial, blocks)
    return (results[0].reshape(ITEMS * WORDS, D), results[1].reshape(ITEMS * REGIONS, D), results[2].reshape(ITEMS * WORDS, D), results[3].reshape(ITEMS * REGIONS, D), summed[0], summed[1], summed[2], summed[3], summed[4], summed[5])
```

```python
import functools
import math

import jax
import jax.numpy as jnp
from jax import lax
from jax.experimental import pallas as pl
from jax.experimental.pallas import tpu as pltpu
from jax.sharding import PartitionSpec as P

HEADS = 12
LOW = jnp.bfloat16
FULL = jnp.float32
VMEM_BYTES = 58 * 1024 * 1024
HBM = pl.BlockSpec(memory_space=pl.ANY)
ONCHIP = pl.BlockSpec(memory_space=pltpu.VMEM)


D = 768
WORDS_HERE = 80
REGIONS_HERE = 144
ROWS = WORDS_HERE + REGIONS_HERE
LANG = slice(0, WORDS_HERE)
VISN = slice(WORDS_HERE, ROWS)
EVERY = slice(0, ROWS)
ITEMS_HERE = 4
FF = 3072
PART = 384
SHARD = 96
Z = 4


def copy_to(src, dst, send, recv, device):
    return pltpu.make_async_remote_copy(
        src_ref=src,
        dst_ref=dst,
        send_sem=send,
        recv_sem=recv,
        device_id=device,
        device_id_type=pl.DeviceIdType.MESH,
    )


class Place:
    def __init__(self):
        rep, spot = lax.axis_index("rep"), lax.axis_index("fsdp")
        z = lax.div(spot, 2)
        core = spot - 2 * z
        y = lax.div(rep, 2)
        x = rep - 2 * y
        self.rep, self.spot, self.z, self.core, self.other = rep, spot, z, core, 1 - core
        along_x, along_y = (1 - x) + 2 * y, x + 2 * (1 - y)
        turn = core * (along_y - along_x)
        self.peers = [along_x + turn, along_y - turn, (1 - x) + 2 * (1 - y)]
        self.sibling = (rep, 2 * z + (1 - core))

    def peer(self, p):
        return (self.peers[p], self.spot)

    def above(self):
        return (self.rep, self.spot + 2)

    def below(self):
        return (self.rep, self.spot - 2)

    def column(self, s):
        return (self.rep, 2 * s + self.core)

    def enter(self, line):
        barrier = pltpu.get_barrier_semaphore()

        def greet(device):
            pl.semaphore_signal(
                barrier, inc=1, device_id=device, device_id_type=pl.DeviceIdType.MESH
            )

        for p in range(3):
            greet(self.peer(p))
        greet(self.sibling)
        number = 4
        if line == 1:

            @pl.when(self.z > 0)
            def _():
                greet(self.below())

            @pl.when(self.z < Z - 1)
            def _():
                greet(self.above())

            number = 4 + jnp.minimum(self.z, 1) + jnp.minimum(Z - 1 - self.z, 1)
        if line == 2:
            for s in range(Z):

                @pl.when(s != self.z)
                def _():
                    greet(self.column(s))

            number = 4 + Z - 1
        pl.semaphore_wait(barrier, number)


class Chain:
    def __init__(self, at, units, slot, own, send, recv):
        self.at, self.units, self.slot, self.own = at, units, slot, own
        self.send, self.recv = send, recv

    def copy(self, index, s, source, upward):
        return copy_to(
            source, self.slot(self.units[index], s),
            self.send.at[index, s, 0 if upward else 1], self.recv.at[index, s],
            self.at.above() if upward else self.at.below(),
        )

    def send_step(self, index, k):
        z, unit = self.at.z, self.units[index]

        @pl.when((z - k >= 0) & (z < Z - 1))
        def _():
            source = self.own(unit) if k == 0 else self.slot(unit, z - k)
            self.copy(index, z - k, source, True).start()

        @pl.when((z + k <= Z - 1) & (z > 0))
        def _():
            source = self.own(unit) if k == 0 else self.slot(unit, z + k)
            self.copy(index, z + k, source, False).start()

    def come(self, k):
        z = self.at.z
        return ((z - 1 - k, z - 1 - k >= 0), (z + 1 + k, z + 1 + k <= Z - 1))

    def wait_step(self, index, k):
        for upward, (s, there) in zip((True, False), self.come(k)):

            @pl.when(there)
            def _():
                ref = self.slot(self.units[index], s)
                self.copy(index, s, ref, not upward).wait_recv()

    def finish(self):
        z = self.at.z
        for index, unit in enumerate(self.units):
            for s in range(Z):

                @pl.when((s <= z) & (z < Z - 1))
                def _():
                    self.copy(index, s, self.slot(unit, s), True).wait_send()

                @pl.when((s >= z) & (z > 0))
                def _():
                    self.copy(index, s, self.slot(unit, s), False).wait_send()


class FeedWeights:
    def __init__(self, at, up, down, ust, dst, uf, df, sems):
        self.at, self.up, self.down = at, up, down
        self.ust, self.dst, self.uf, self.df = ust, dst, uf, df
        self.usend, self.urecv, self.dsend, self.drecv, self.ulocal, self.dlocal = sems
        self.columns = pl.multiple_of(D * at.rep, D)
        self.rows = self.quarter(at.rep)

    def quarter(self, rep):
        return pl.ds(pl.multiple_of(SHARD * rep, SHARD), SHARD)

    def slot(self, kind, s):
        return self.ust.at[s] if kind == "u" else self.dst.at[s]

    def own(self, kind):
        return self.up.at[:, pl.ds(self.columns, D)] if kind == "u" else self.down.at[self.rows]

    def halves(self, s, source, offset):
        core, other = self.at.core, self.at.other
        target = self.uf.at[2 * s + core]
        there = copy_to(
            source.at[:, pl.ds(pl.multiple_of(offset + PART * other, PART), PART)],
            target, self.usend.at[s], self.urecv.at[s], self.at.sibling,
        )
        here = pltpu.make_async_copy(
            source.at[:, pl.ds(pl.multiple_of(offset + PART * core, PART), PART)],
            target, self.ulocal.at[s],
        )
        return there, here

    def down_there(self, s, source):
        return copy_to(
            source, self.df.at[self.rows],
            self.dsend.at[s], self.drecv.at[self.at.rep], (s, self.at.spot),
        )

    def down_here(self, source):
        return pltpu.make_async_copy(source, self.df.at[self.rows], self.dlocal)

    def pass_on(self, kind, s, source):
        if kind == "u":
            for copy in self.halves(s, source, 0):
                copy.start()
        else:

            @pl.when(s != self.at.rep)
            def _():
                self.down_there(s, source).start()

            @pl.when(s == self.at.rep)
            def _():
                self.down_here(source).start()

    def own_start(self, kind):
        if kind == "u":
            for copy in self.halves(self.at.z, self.up, self.columns):
                copy.start()
        else:
            self.pass_on(kind, self.at.z, self.own(kind))

    def finish(self):
        for s in range(Z):
            there, here = self.halves(s, self.ust.at[s], 0)
            there.wait()
            here.wait()

            @pl.when(s != self.at.rep)
            def _():
                self.down_there(s, self.dst.at[s]).wait_send()

        for p in range(3):
            there = self.at.peers[p]
            copy_to(
                self.dst.at[0], self.df.at[self.quarter(there)],
                self.dsend.at[0], self.drecv.at[there], self.at.peer(p),
            ).wait_recv()
        self.down_here(self.dst.at[0]).wait()


def feed_sems():
    dma = pltpu.SemaphoreType.DMA
    return [dma((Z,)), dma((Z,)), dma((Z,)), dma((Z,)), dma((Z,)), dma]


UNITS = [("a", 0), ("s", 0), ("a", 1), ("a", 2), ("u", 1), ("d", 1)]


def gather_kernel(
    aw, up, down, small, language, vision, lengths,
    wf, uf, df, ax, vec, ub, onelow, two, q0, k0, v0, z0, q1, k1, v1, m1, z1,
    wv, ust, dst, sf, x, one, xlow, m0,
    zsend, zrecv, psend, precv, asend, arecv, ssend, srecv,
    alocal, slocal, wlocal, xlocal, osend, orecv, olocal, *fsems,
):
    at = Place()
    rep, z, core = at.rep, at.z, at.core
    rows_in = [
        pltpu.make_async_copy(ref, x.at[rows], xlocal.at[i])
        for i, (ref, rows) in enumerate(
            ((language, pl.ds(0, WORDS_HERE)), (vision, pl.ds(WORDS_HERE, REGIONS_HERE)))
        )
    ]
    for copy in rows_in:
        copy.start()
    at.enter(1)
    feed_weights = FeedWeights(at, up.at[1], down.at[1], ust, dst, uf, df, fsems)

    def slot(unit, s):
        kind, i = unit
        if kind == "a":
            return wv.at[i, rep, 2 * s + core]
        return sf.at[2 * s + core] if kind == "s" else feed_weights.slot(kind, s)

    def own(unit):
        kind, i = unit
        if kind == "a":
            return aw.at[i, rep]
        return small if kind == "s" else feed_weights.own(kind)

    chain = Chain(at, UNITS, slot, own, zsend, zrecv)

    def plane_copy(layer, s, i):
        ref = wv.at[layer, at.peers[0] if i == 2 else rep, 2 * s + core]
        there = at.peer(1) if i == 2 else at.peer(i)
        return copy_to(ref, ref, psend.at[layer, s, i], precv.at[layer, s, i], there)

    def plane_arrival(layer, s, i):
        ref = wv.at[layer, at.peers[i], 2 * s + core]
        return copy_to(ref, ref, psend.at[layer, s, i], precv.at[layer, s, i], at.peer(i))

    def small_copy(s, source):
        return copy_to(source, sf.at[2 * s + core], ssend.at[s], srecv.at[s], at.sibling)

    def pass_on(unit, s, source):
        kind, i = unit
        if kind == "a":
            for p in range(2):
                plane_copy(i, s, p).start()
        elif kind == "s":
            small_copy(s, source).start()
        else:
            feed_weights.pass_on(kind, s, source)

    def shard_here(layer):
        return pltpu.make_async_copy(aw.at[layer], wv.at[layer, :, 2 * z + core], alocal.at[layer])

    def small_here():
        return pltpu.make_async_copy(small, sf.at[2 * z + core], slocal)

    def own_start(unit):
        kind, i = unit
        if kind == "a":
            shard_here(i).start()
            copy_to(
                aw.at[i], wv.at[i, :, 2 * z + core], asend.at[i, z], arecv.at[i, z], at.sibling
            ).start()
        elif kind == "s":
            small_here().start()
            pass_on(unit, z, small)
        else:
            feed_weights.own_start(kind)

    def line_send_step(index, k):
        chain.send_step(index, k)
        if k == 0:
            own_start(UNITS[index])

    def pass_step(index, k):
        unit = UNITS[index]
        for s, there in chain.come(k):

            @pl.when(there)
            def _():
                pass_on(unit, s, slot(unit, s))

    def core_copy(layer, s):
        ref = wv.at[layer, :, 2 * s + core]
        return copy_to(ref, ref, asend.at[layer, s], arecv.at[layer, s], at.sibling)

    def core_arrival(layer, s):
        ref = wv.at[layer, :, 2 * s + at.other]
        return copy_to(ref, ref, asend.at[layer, s], arecv.at[layer, s], at.sibling)

    def relay_step(layer, k):
        for s, there in chain.come(k):

            @pl.when(there)
            def _():
                plane_arrival(layer, s, 0).wait_recv()
                plane_copy(layer, s, 2).start()

    def plane_step(layer, k):
        for s, there in chain.come(k):

            @pl.when(there)
            def _():
                plane_arrival(layer, s, 1).wait_recv()
                plane_arrival(layer, s, 2).wait_recv()
                core_copy(layer, s).start()

    count = len(UNITS)

    def exchange():
        line_send_step(0, 0)
        for time in range(count + 6):
            if time + 1 < count:
                line_send_step(time + 1, 0)
            for index, unit in enumerate(UNITS):
                k = time - index
                if 1 <= k <= 3:
                    chain.wait_step(index, k - 1)
                    if k <= 2:
                        line_send_step(index, k)
                    pass_step(index, k - 1)
                    yield time
                if unit[0] == "a" and 0 <= k - 2 <= 2:
                    relay_step(unit[1], k - 2)
                    yield time
                if unit[0] == "a" and 0 <= k - 3 <= 2:
                    plane_step(unit[1], k - 3)
                    yield time
            yield time + 1

    steps = exchange()
    clock = [0]

    def pump(times=1):
        for _ in range(times):
            clock[0] = next(steps, 99)

    def until(time):
        while clock[0] < time:
            pump()

    def ready(layer):
        until(UNITS.index(("a", layer)) + 6)
        shard_here(layer).wait()
        for s in range(Z):
            core_arrival(layer, s).wait_recv()
        pltpu.make_async_copy(wv.at[layer], wf.at[layer], wlocal.at[layer]).start()

    for copy in rows_in:
        copy.wait()
    xlow[...] = x[...].astype(LOW)

    def operand_copy(source, p):
        return copy_to(source, ax.at[rep], osend.at[p], orecv.at[p], at.peer(p))

    def operands(source, wanted):
        for p in (2, 0, 1):

            @pl.when(wanted(at.peers[p]))
            def _():
                operand_copy(source, p).start()

        @pl.when(wanted(rep))
        def _():
            pltpu.make_async_copy(source, ax.at[rep], olocal).start()

    until(UNITS.index(("s", 0)) + 4)
    small_here().wait()
    for s in range(Z):
        copy_to(
            small, sf.at[2 * s + at.other], ssend.at[s], srecv.at[s], at.sibling
        ).wait_recv()
    line = lax.broadcasted_iota(jnp.int32, (128, D), 0)
    lane = lax.broadcasted_iota(jnp.int32, (128, D), 1)
    vectors = jnp.zeros((32, D), FULL)
    for d in range(8):
        pick = ((lane == line + SHARD * d) & (line < SHARD)).astype(FULL).astype(LOW)
        vectors = vectors + dot(sf[d, :, :128], pick)
    vec[...] = vectors
    ub[...] = jnp.zeros_like(ub)
    ub[0:2, :] = sf[2 * rep + core].astype(FULL)[21:23, :]

    word_bias = length_bias(lengths, (1, WORDS_HERE), 1)
    ready(0)
    attend(
        x, xlow, wv, vec, 0, EVERY,
        [
            (LANG, VISN, pair_bias(WORDS_EACH, REGIONS_EACH, None)),
            (VISN, LANG, pair_bias(REGIONS_EACH, WORDS_EACH, word_bias)),
        ],
        q0, k0, v0, m0, z0, one, pump,
    )
    onelow[...] = one[...].astype(LOW)
    ready(1)
    attend(
        one, onelow, wv, vec, 1, LANG,
        [(LANG, LANG, pair_bias(WORDS_EACH, WORDS_EACH, word_bias))],
        q1, k1, v1, m1, z1, two, pump,
    )
    ready(2)
    operands(xlow, lambda there: there != 3)
    operands(m0, lambda there: there == 3)
    attend(
        one, onelow, wv, vec, 2, VISN,
        [(VISN, VISN, pair_bias(REGIONS_EACH, REGIONS_EACH, None))],
        q1, k1, v1, m1, z1, two, pump,
    )
    until(99)

    pltpu.make_async_copy(xlow, ax.at[rep], olocal).wait()
    for p in range(3):
        operand_copy(xlow, p).wait_send()
        copy_to(
            xlow, ax.at[at.peers[p]], osend.at[p], orecv.at[p], at.peer(p)
        ).wait_recv()
    for layer in range(3):
        pltpu.make_async_copy(wv.at[layer], wf.at[layer], wlocal.at[layer]).wait()
        for s in range(Z):
            core_copy(layer, s).wait_send()

            @pl.when(s != z)
            def _():
                for i in range(3):
                    plane_copy(layer, s, i).wait_send()

    for s in range(Z):
        small_copy(s, small).wait_send()
    chain.finish()
    feed_weights.finish()


def gather(aw, up, down, small, language, vision, lengths):
    dma = pltpu.SemaphoreType.DMA
    count = len(UNITS)
    full = jax.ShapeDtypeStruct((ROWS, D), FULL)
    low = jax.ShapeDtypeStruct((ROWS, D), LOW)
    return pl.pallas_call(
        gather_kernel,
        out_shape=(
            jax.ShapeDtypeStruct((3, 4, 8, SHARD, D), LOW),
            jax.ShapeDtypeStruct((8, SHARD, PART), LOW),
            jax.ShapeDtypeStruct((PART, D), LOW),
            jax.ShapeDtypeStruct((4, ROWS, D), LOW),
            jax.ShapeDtypeStruct((32, D), FULL),
            jax.ShapeDtypeStruct((8, PART), FULL),
            low, full,
            low, low, low, full,
            low, low, low, low, full,
        ),
        in_specs=[HBM] * 6 + [pl.BlockSpec(memory_space=pltpu.SMEM)],
        out_specs=(HBM,) * 4 + (ONCHIP,) * 13,
        scratch_shapes=[
            pltpu.VMEM((3, 4, 8, SHARD, D), LOW),
            pltpu.VMEM((Z, SHARD, D), LOW),
            pltpu.VMEM((Z, SHARD, D), LOW),
            pltpu.VMEM((8, 32, PART), LOW),
            pltpu.VMEM((ROWS, D), FULL),
            pltpu.VMEM((ROWS, D), FULL),
            pltpu.VMEM((ROWS, D), LOW),
            pltpu.VMEM((ROWS, D), LOW),
            dma((count, Z, 2)), dma((count, Z)),
            dma((3, Z, 3)), dma((3, Z, 3)),
            dma((3, Z)), dma((3, Z)),
            dma((Z,)), dma((Z,)),
            dma((3,)), dma, dma((3,)), dma((2,)), dma((3,)), dma((3,)), dma,
            *feed_sems(),
        ],
        compiler_params=pltpu.CompilerParams(
            collective_id=0, has_side_effects=True, vmem_limit_bytes=VMEM_BYTES
        ),
        cost_estimate=pl.CostEstimate(
            flops=2_200_000_000, bytes_accessed=40_000_000, transcendentals=500_000
        ),
        name="gather_attention",
    )(aw, up, down, small, language, vision, lengths)


def dot(a, b):
    return jnp.dot(a, b, preferred_element_type=FULL)


def dot_t(a, b):
    return lax.dot_general(a, b, (((1,), (1,)), ((), ())), preferred_element_type=FULL)


def t_dot(a, b):
    return lax.dot_general(a, b, (((0,), (0,)), ((), ())), preferred_element_type=FULL)


def column_sum(a):
    return jnp.sum(a.astype(FULL), axis=0, keepdims=True)


def norm_stats(pre):
    mean = jnp.mean(pre, axis=-1, keepdims=True)
    centred = pre - mean
    spread = jnp.mean(centred * centred, axis=-1, keepdims=True)
    scale = lax.rsqrt(spread + 1e-06)
    return centred * scale, scale


def norm_back(grad, unit, scale, gain):
    flow = grad * (1.0 + gain)
    return (
        flow
        - jnp.mean(flow, axis=-1, keepdims=True)
        - unit * jnp.mean(flow * unit, axis=-1, keepdims=True)
    ) * scale


def item_of(index, size):
    return sum((index >= size * k).astype(jnp.int32) for k in range(1, ITEMS_HERE))


def pair_bias(query_size, key_size, key_bias):
    shape = (query_size * ITEMS_HERE, key_size * ITEMS_HERE)
    query_item = item_of(lax.broadcasted_iota(jnp.int32, shape, 0), query_size)
    key_item = item_of(lax.broadcasted_iota(jnp.int32, shape, 1), key_size)
    bias = jnp.where(query_item == key_item, 0.0, -1e30)
    return bias if key_bias is None else bias + key_bias


GROUP = 4


def head_masks(dtype):
    lane = lax.broadcasted_iota(jnp.int32, (1, 64 * GROUP), 1)
    return [
        ((lane >= 64 * i) & (lane < 64 * i + 64)).astype(FULL).astype(dtype) for i in range(GROUP)
    ]


def stacked(value):
    return jnp.concatenate([value * mask for mask in head_masks(LOW)], axis=0)


def unstacked(value, rows):
    value = value.reshape(GROUP, rows, 64 * GROUP)
    return sum(value[i] * mask for i, mask in enumerate(head_masks(FULL)))


def mix_heads(q_ref, k_ref, v_ref, m_ref, qrows, krows, bias, pump):
    nq, nk = qrows.stop - qrows.start, krows.stop - krows.start
    for group in range(HEADS // GROUP):
        lanes = slice(256 * group, 256 * group + 256)
        query, keys, values = q_ref[qrows, lanes], k_ref[krows, lanes], v_ref[krows, lanes]
        scores = dot_t(stacked(query), keys).reshape(GROUP, nq, nk) * 0.125 + bias[None]
        exponent = jnp.exp(scores - jnp.max(scores, axis=-1, keepdims=True))
        probs = exponent / jnp.sum(exponent, axis=-1, keepdims=True)
        mixed = dot(probs.astype(LOW).reshape(GROUP * nq, nk), values)
        m_ref[qrows, lanes] = unstacked(mixed, nq).astype(LOW)
        pump()


def head_back(q_ref, k_ref, v_ref, dm_ref, dq_ref, dk_ref, dv_ref, qrows, krows, bias, group, base):
    nq, nk = qrows.stop - qrows.start, krows.stop - krows.start
    lanes = slice(256 * group, 256 * group + 256)
    query, keys, values = q_ref[qrows, lanes], k_ref[krows, lanes], v_ref[krows, lanes]
    grad = dm_ref[qrows, lanes]
    keys = stacked(keys)
    scores = dot_t(keys, query).reshape(GROUP, nk, nq) * 0.125 + bias[None]
    exponent = jnp.exp(scores - jnp.max(scores, axis=1, keepdims=True))
    probs = exponent / jnp.sum(exponent, axis=1, keepdims=True)
    dp = dot_t(stacked(values), grad).reshape(GROUP, nk, nq)
    ds = probs * (dp - jnp.sum(probs * dp, axis=1, keepdims=True))
    ds = ds.astype(LOW).reshape(GROUP * nk, nq)
    dv = unstacked(dot(probs.astype(LOW).reshape(GROUP * nk, nq), grad), nk)
    dk = unstacked(dot(ds, query), nk) * 0.125
    dq = t_dot(ds, keys) * 0.125
    qhere = slice(qrows.start - base, qrows.stop - base)
    khere = slice(krows.start - base, krows.stop - base)
    dq_ref[qhere, lanes] = dq.astype(LOW)
    dk_ref[khere, lanes] = dk.astype(LOW)
    dv_ref[khere, lanes] = dv.astype(LOW)


def row_of(ref, i):
    return ref[i : i + 1, :]


def attend(
    x_ref, low_ref, w_ref, vec_ref, layer, rows, parts, q_ref, k_ref, v_ref, m_ref, z_ref, out_ref, pump
):
    low = low_ref[rows, :]
    vec = [row_of(vec_ref, 5 * layer + i) for i in range(5)]

    def matrix(m):
        return w_ref[layer, m].reshape(D, D)

    q_ref[rows, :] = (dot(low, matrix(0)) + vec[0]).astype(LOW)
    k_ref[rows, :] = dot(low, matrix(1)).astype(LOW)
    pump()
    v_ref[rows, :] = (dot(low, matrix(2)) + vec[1]).astype(LOW)
    for qrows, krows, bias in parts:
        mix_heads(q_ref, k_ref, v_ref, m_ref, qrows, krows, bias, pump)
    pre = x_ref[rows, :] + (dot(m_ref[rows, :], matrix(3)) + vec[2])
    z_ref[rows, :] = pre
    unit, _ = norm_stats(pre)
    out_ref[rows, :] = unit * (1.0 + vec[3]) + vec[4]
    pump()


WORDS_EACH = WORDS_HERE // ITEMS_HERE
REGIONS_EACH = REGIONS_HERE // ITEMS_HERE


def length_bias(lengths, shape, axis):
    index = lax.broadcasted_iota(jnp.int32, shape, axis)
    item = item_of(index, WORDS_EACH)
    real = sum(jnp.where(item == i, lengths[i], 0) for i in range(ITEMS_HERE))
    return jnp.where(index - WORDS_EACH * item < real, 0.0, -1000000000.0)


STREAMS = (1, 0)
CHUNKS = ((1, WORDS_HERE, 80), (1, WORDS_HERE + 80, 64), (0, 0, WORDS_HERE))
SELF_ROWS = (pl.ds(0, WORDS_HERE), pl.ds(WORDS_HERE, REGIONS_HERE))


def ffn_kernel(
    x2, lang_cot, visn_cot, uw1, dw1, vec, ub, ax0, onelow, m1, up, down,
    lang_out, visn_out, d2, gu, gd, gv, gb, bx0, ax1, ax2, bx1, bx2,
    *scratch,
):
    at = Place()
    rep, core = at.rep, at.core
    scratch = list(scratch)

    def take(count):
        some, scratch[:] = scratch[:count], scratch[count:]
        return some

    many = len(CHUNKS)
    xg, bg, ht, gt, hd, mine, dz = [take(many) for _ in range(7)]
    give, got, stage, land = [[take(many) for _ in range(2)] for _ in range(4)]
    uw0, dw0, ust, dst = take(4)
    psend, precv, csend, crecv, fsend, frecv, osend, orecv, olocal, bsend, brecv = take(11)
    zsend, zrecv = take(2)
    at.enter(1)
    feed_weights = FeedWeights(at, up.at[0], down.at[0], ust, dst, uw0, dw0, scratch)
    chain = Chain(at, "ud", feed_weights.slot, feed_weights.own, zsend, zrecv)

    def weights_step(k):
        for index, kind in enumerate("ud"):
            if k > 0:
                chain.wait_step(index, k - 1)
            if k < 3:
                chain.send_step(index, k)
            if k == 0:
                feed_weights.own_start(kind)
            else:
                for s, there in chain.come(k - 1):

                    @pl.when(there)
                    def _():
                        feed_weights.pass_on(kind, s, feed_weights.slot(kind, s))

    def up_weight(t):
        return uw1[...] if t else uw0[...].reshape(D, PART)

    def down_weight(t):
        return (dw1 if t else dw0)[...]

    def plane_copy(which, i, hop, buffer):
        ref = buffer.at[0, at.peers[0] if hop == 2 else rep]
        there = at.peer(1) if hop == 2 else at.peer(hop)
        return copy_to(ref, ref, psend.at[which, i, hop], precv.at[which, i, hop], there)

    def plane_arrival(which, i, hop, buffer):
        ref = buffer.at[0, at.peers[hop]]
        return copy_to(ref, ref, psend.at[which, i, hop], precv.at[which, i, hop], at.peer(hop))

    def core_copy(which, i, hop, buffer):
        there = rep if hop == 3 else at.peers[hop]
        return copy_to(
            buffer.at[0, there], buffer.at[1, there],
            csend.at[which, i, hop], crecv.at[which, i, hop], at.sibling,
        )

    def gather_start(which, i, buffer):
        for hop in range(2):
            plane_copy(which, i, hop, buffer).start()
        core_copy(which, i, 3, buffer).start()

    def gather_relay(which, i, buffer):
        plane_arrival(which, i, 0, buffer).wait_recv()
        plane_copy(which, i, 2, buffer).start()
        core_copy(which, i, 0, buffer).start()

    def gather_rest(which, i, buffer):
        for hop in (1, 2):
            plane_arrival(which, i, hop, buffer).wait_recv()
            core_copy(which, i, hop, buffer).start()

    def gather_sibling(which, i, buffer):
        for hop in (3, 0, 1, 2):
            core_copy(which, i, hop, buffer).wait_recv()

    def gather_sent(which, i, buffer):
        for hop in range(3):
            plane_copy(which, i, hop, buffer).wait_send()
        for hop in range(4):
            core_copy(which, i, hop, buffer).wait_send()

    def swap_copy(turn, i):
        return copy_to(
            give[turn][i], got[turn][i], fsend.at[turn, i], frecv.at[turn, i], at.sibling
        )

    def first_copy(turn, i):
        return copy_to(
            stage[turn][i].at[pl.ds(0, 2)], land[turn][i].at[pl.ds(0, 2)],
            psend.at[2 * turn + 1, i, 0], precv.at[2 * turn + 1, i, 0], at.peer(0),
        )

    def second_copy(turn, i):
        return copy_to(
            stage[turn][i].at[2], land[turn][i].at[2],
            psend.at[2 * turn + 1, i, 1], precv.at[2 * turn + 1, i, 1], at.peer(1),
        )

    def both_cores(turn, i, there):
        return mine[i][there] + got[turn][i][there].astype(FULL)

    def return_first(turn, i):
        swap_copy(turn, i).wait_recv()
        for hop, p in enumerate((0, 2)):
            stage[turn][i][hop] = both_cores(turn, i, at.peers[p]).astype(LOW)
        first_copy(turn, i).start()

    def return_second(turn, i):
        first_copy(turn, i).wait_recv()
        passed = land[turn][i][1].astype(FULL)
        stage[turn][i][2] = (both_cores(turn, i, at.peers[1]) + passed).astype(LOW)
        second_copy(turn, i).start()

    def summed(turn, i):
        second_copy(turn, i).wait_recv()
        passed = land[turn][i][0].astype(FULL) + land[turn][i][2].astype(FULL)
        return both_cores(turn, i, rep) + passed

    def flat(value):
        return value.reshape(value.shape[0] * value.shape[1], value.shape[2])

    def keep_part(turn, i, side, part):
        part = part.reshape(Z, CHUNKS[i][2], D)
        if side == 0:
            mine[i][...] = part
        else:
            give[turn][i][...] = part.astype(LOW)
            swap_copy(turn, i).start()

    def up_and_down(i, side):
        t = CHUNKS[i][0]
        hidden = dot(flat(xg[i][side]), up_weight(t)) + ub[t : t + 1, :]
        below = 0.5 * (1.0 + lax.erf(hidden * (1.0 / math.sqrt(2.0))))
        active = (hidden * below).astype(LOW)
        gt[i][side] = active
        ht[i][side] = below + hidden * (
            jnp.exp(-0.5 * hidden * hidden) * (1.0 / math.sqrt(2.0 * math.pi))
        )
        keep_part(0, i, side, dot(active, down_weight(t)))

    def rows_back(i, side):
        t = CHUNKS[i][0]
        low = (dot_t(flat(bg[i][side]), down_weight(t)) * ht[i][side]).astype(LOW)
        hd[i][side] = low
        keep_part(1, i, side, dot_t(low, up_weight(t)))

    def weights_back(t):
        pieces = [(i, side) for i in range(many) if CHUNKS[i][0] == t for side in range(2)]
        gd[t] = sum(t_dot(gt[i][side], flat(bg[i][side])) for i, side in pieces).astype(LOW)
        gu[t] = sum(t_dot(flat(xg[i][side]), hd[i][side]) for i, side in pieces).astype(LOW)
        total = sum(column_sum(hd[i][side]) for i, side in pieces)
        twice = jnp.concatenate([total, total], axis=1)
        row = lax.broadcasted_iota(jnp.int32, (Z, D), 0)
        lane = lax.broadcasted_iota(jnp.int32, (Z, D), 1)
        kept = (row == rep) & ((lane >= PART).astype(jnp.int32) == core)
        gb[Z * t : Z * t + Z, :] = jnp.where(kept, jnp.broadcast_to(twice, (Z, D)), 0.0)

    def chunk_rows(i):
        t, start, count = CHUNKS[i]
        here = start - WORDS_HERE * t
        return slice(start, start + count), slice(here, here + count)

    def norm_turn(i):
        t = CHUNKS[i][0]
        rows, here = chunk_rows(i)
        bias, gain, shift = [row_of(vec, 15 + 3 * t + k) for k in range(3)]
        pre = x2[rows, :] + (summed(0, i) + bias)
        unit, scale = norm_stats(pre)
        (lang_out, visn_out)[t][here, :] = unit * (1.0 + gain) + shift
        grad = (lang_cot, visn_cot)[t][here, :]
        dz[i][...] = norm_back(grad, unit, scale, gain)
        branch = dz[i][...].astype(LOW)
        bg[i][0, rep] = branch
        gather_start(2, i, bg[i])
        for k, value in enumerate((column_sum(branch), column_sum(grad * unit), column_sum(grad))):
            gv[3 * t + k : 3 * t + k + 1, :] += value

    landed, across = (ax1, ax2), (bx1, bx2)

    def operand_copy(source, k, p):
        return copy_to(
            source.at[SELF_ROWS[k]], landed[k].at[rep], osend.at[k, p], orecv.at[k, p], at.peer(p)
        )

    def operand_here(source, k):
        return pltpu.make_async_copy(source.at[SELF_ROWS[k]], landed[k].at[rep], olocal.at[k])

    def across_copy(k):
        source, target = (ax0, bx0) if k == 2 else (landed[k], across[k])
        return copy_to(source, target, bsend.at[k], brecv.at[k], at.sibling)

    def operand_send(k, p):
        @pl.when(at.peers[p] != 3)
        def _():
            operand_copy(onelow, k, p).start()

        @pl.when(at.peers[p] == 3)
        def _():
            operand_copy(m1, k, p).start()

    def operands_start():
        across_copy(2).start()
        for k in range(2):

            @pl.when(rep != 3)
            def _():
                operand_here(onelow, k).start()

            @pl.when(rep == 3)
            def _():
                operand_here(m1, k).start()

    def operands_across(k):
        operand_here(m1, k).wait()
        for p in range(3):
            copy_to(
                m1.at[SELF_ROWS[k]], landed[k].at[at.peers[p]],
                osend.at[k, p], orecv.at[k, p], at.peer(p),
            ).wait_recv()
        across_copy(k).start()

    gv[...] = jnp.zeros_like(gv)
    for i in range(many):
        xg[i][0, rep] = x2[chunk_rows(i)[0], :].astype(LOW)
        gather_start(0, i, xg[i])
    weights_step(0)
    operands_start()
    gather_relay(0, 0, xg[0])
    gather_rest(0, 0, xg[0])
    gather_relay(0, 1, xg[1])
    weights_step(1)
    up_and_down(0, 0)
    gather_relay(0, 2, xg[2])
    gather_sibling(0, 0, xg[0])
    up_and_down(0, 1)
    gather_rest(0, 1, xg[1])
    weights_step(2)
    up_and_down(1, 0)
    return_first(0, 0)
    gather_sibling(0, 1, xg[1])
    up_and_down(1, 1)
    gather_rest(0, 2, xg[2])
    weights_step(3)
    operand_send(0, 2)
    return_second(0, 0)
    return_first(0, 1)
    gather_sibling(0, 2, xg[2])
    feed_weights.finish()
    up_and_down(2, 0)
    up_and_down(2, 1)
    norm_turn(0)
    return_second(0, 1)
    return_first(0, 2)
    operand_send(0, 0)
    operand_send(0, 1)
    norm_turn(1)
    gather_relay(2, 0, bg[0])
    return_second(0, 2)
    gather_rest(2, 0, bg[0])
    norm_turn(2)
    operand_send(1, 2)
    rows_back(0, 0)
    gather_relay(2, 1, bg[1])
    gather_sibling(2, 0, bg[0])
    rows_back(0, 1)
    gather_rest(2, 1, bg[1])
    gather_relay(2, 2, bg[2])
    return_first(1, 0)
    operand_send(1, 0)
    rows_back(1, 0)
    gather_sibling(2, 1, bg[1])
    rows_back(1, 1)
    gather_rest(2, 2, bg[2])
    return_second(1, 0)
    return_first(1, 1)
    operand_send(1, 1)
    rows_back(2, 0)
    gather_sibling(2, 2, bg[2])
    rows_back(2, 1)
    return_second(1, 1)
    return_first(1, 2)
    operands_across(0)
    operands_across(1)
    weights_back(0)
    return_second(1, 2)
    weights_back(1)
    for i in range(many):
        d2[chunk_rows(i)[0], :] = dz[i][...] + summed(1, i)
    chain.finish()
    for k in range(3):
        across_copy(k).wait()
    for k in range(2):
        for p in range(3):
            operand_copy(m1, k, p).wait_send()
    for i in range(many):
        gather_sent(0, i, xg[i])
        gather_sent(2, i, bg[i])
        for turn in range(2):
            swap_copy(turn, i).wait_send()
            first_copy(turn, i).wait_send()
            second_copy(turn, i).wait_send()


def feed(x2, lang_cot, visn_cot, uw1, dw1, vec, ub, ax0, onelow, m1, up, down):
    dma = pltpu.SemaphoreType.DMA
    many = len(CHUNKS)

    def each(lead, width, dtype):
        return [pltpu.VMEM((*lead, chunk[2], width), dtype) for chunk in CHUNKS]

    def each_flat(width, dtype):
        return [pltpu.VMEM((2, Z * chunk[2], width), dtype) for chunk in CHUNKS]

    def rows_of_plane(count):
        return jax.ShapeDtypeStruct((4, count, D), LOW)

    return pl.pallas_call(
        ffn_kernel,
        out_shape=(
            jax.ShapeDtypeStruct((WORDS_HERE, D), FULL),
            jax.ShapeDtypeStruct((REGIONS_HERE, D), FULL),
            jax.ShapeDtypeStruct((ROWS, D), FULL),
            jax.ShapeDtypeStruct((2, D, PART), LOW),
            jax.ShapeDtypeStruct((2, PART, D), LOW),
            jax.ShapeDtypeStruct((8, D), FULL),
            jax.ShapeDtypeStruct((8, D), FULL),
            rows_of_plane(ROWS),
            rows_of_plane(WORDS_HERE), rows_of_plane(REGIONS_HERE),
            rows_of_plane(WORDS_HERE), rows_of_plane(REGIONS_HERE),
        ),
        in_specs=[ONCHIP] * 7 + [HBM] * 5,
        out_specs=(ONCHIP,) * 7 + (HBM,) * 5,
        scratch_shapes=each((2, Z), D, LOW)
        + each((2, Z), D, LOW)
        + each_flat(PART, FULL)
        + each_flat(PART, LOW)
        + each_flat(PART, LOW)
        + each((Z,), D, FULL)
        + each((), D, FULL)
        + each((Z,), D, LOW) * 2
        + each((Z,), D, LOW) * 2
        + each((3,), D, LOW) * 2
        + each((3,), D, LOW) * 2
        + [
            pltpu.VMEM((8, SHARD, PART), LOW),
            pltpu.VMEM((PART, D), LOW),
            pltpu.VMEM((Z, SHARD, D), LOW),
            pltpu.VMEM((Z, SHARD, D), LOW),
            dma((4, many, 3)), dma((4, many, 3)),
            dma((4, many, 4)), dma((4, many, 4)),
            dma((2, many)), dma((2, many)),
            dma((2, 3)), dma((2, 3)), dma((2,)), dma((3,)), dma((3,)),
            dma((2, Z, 2)), dma((2, Z)), *feed_sems(),
        ],
        compiler_params=pltpu.CompilerParams(
            collective_id=1, has_side_effects=True, vmem_limit_bytes=VMEM_BYTES
        ),
        cost_estimate=pl.CostEstimate(
            flops=6_400_000_000, bytes_accessed=12_000_000, transcendentals=1_400_000
        ),
        name="feed_forward",
    )(x2, lang_cot, visn_cot, uw1, dw1, vec, ub, ax0, onelow, m1, up, down)


def turned_bias(query_size, key_size, key_bias):
    shape = (key_size * ITEMS_HERE, query_size * ITEMS_HERE)
    key_item = item_of(lax.broadcasted_iota(jnp.int32, shape, 0), key_size)
    query_item = item_of(lax.broadcasted_iota(jnp.int32, shape, 1), query_size)
    bias = jnp.where(query_item == key_item, 0.0, -1e30)
    return bias if key_bias is None else bias + key_bias


LAYER_ROWS = (EVERY, LANG, VISN)
WIDE_UNITS = 5


def backward_kernel(
    d2, lengths, vec, w, q0, k0, v0, z0, q1, k1, v1, z1, gu, gd, gv, gb,
    ax0, ax1, ax2, bx0, bx1, bx2,
    dx, oa, ou, od, os,
    wbuf, xa0, xa1, xa2, ys0, ys1, ys2, ya0, ya1, ya2, yb0, yb1, yb2,
    share, dland, zwide, zlow, rwide, rlow, edge, wide, final, d1, dm, gs, s0, s1, s2, s3, s4, scol,
    wsem, asem, ysend, yrecv, yfsend, yfrecv,
    dsend, drecv, dlocal, wsend, wrecv, lsend, lrecv, rsend, rrecv, esend, erecv,
    gsend, grecv, glocal, ssend, srecv,
):
    at = Place()
    rep, z, core, other = at.rep, at.z, at.core, at.other
    own_half = pl.ds(pl.multiple_of(PART * core, PART), PART)
    other_half = pl.ds(pl.multiple_of(PART * other, PART), PART)
    xa, xin = (xa0, xa1, xa2), ((ax0, bx0), (ax1, bx1), (ax2, bx2))
    ys, ya, yb = (ys0, ys1, ys2), (ya0, ya1, ya2), (yb0, yb1, yb2)

    def load(layer):
        return pltpu.make_async_copy(w.at[layer], wbuf.at[layer], wsem.at[layer])

    def load_rows(layer, side):
        return pltpu.make_async_copy(
            xin[layer][side], xa[layer].at[side], asem.at[layer, side]
        )

    for layer in (1, 2, 0):
        load(layer).start()
    for layer in (1, 2, 0):
        for side in range(2):
            load_rows(layer, side).start()
    at.enter(2)

    def y_copy(layer, p):
        return copy_to(
            ys[layer].at[at.peers[p]], ya[layer].at[rep],
            ysend.at[layer, p], yrecv.at[layer, p], at.peer(p),
        )

    def y_forward(layer, i):
        there = rep if i == 3 else at.peers[i]
        return copy_to(
            ya[layer].at[there, :, other_half], yb[layer].at[there],
            yfsend.at[layer, i], yfrecv.at[layer, i], at.sibling,
        )

    def y_arrival(layer, p):
        return copy_to(
            ys[layer].at[0], ya[layer].at[at.peers[p]],
            ysend.at[layer, p], yrecv.at[layer, p], at.peer(p),
        )

    def share_of(unit, s):
        if unit < 3:
            return share.at[unit, s]
        return gu.at[unit - 3, s] if unit < 5 else dland.at[unit - 5, s]

    def slot_of(unit, s):
        return zwide.at[unit, s] if unit < 5 else zlow.at[unit - 5, s]

    def stop_of(unit):
        return rwide.at[unit] if unit < 5 else rlow.at[unit - 5]

    def column_copy(unit, s, source):
        return copy_to(source, slot_of(unit, z), wsend.at[unit, s], wrecv.at[unit, z], at.column(s))

    def column_arrival(unit, s):
        ref = slot_of(unit, s)
        return copy_to(ref, ref, wsend.at[unit, s], wrecv.at[unit, s], at.column(s))

    def stop_copy(unit):
        far = lax.div(z, 3)
        return copy_to(
            share_of(unit, 2 - far), stop_of(unit),
            rsend.at[unit], rrecv.at[unit], at.column(1 + far),
        )

    def stop_arrival(unit):
        ref = stop_of(unit)
        return copy_to(ref, ref, rsend.at[unit], rrecv.at[unit], at.column(3 * (z - 1)))

    is_end = (z == 0) | (z == Z - 1)
    is_middle = (z > 0) & (z < Z - 1)
    straight = (z > 0, z == 0, z == Z - 1, z < Z - 1)

    def from_layer(s):
        return ((z != s) & is_end) | (is_middle & ((z == s + 1) | (z == s - 1)))

    def column_start(unit):
        @pl.when(is_end)
        def _():
            stop_copy(unit).start()

        for s in (3, 0, 1, 2):

            @pl.when(straight[s])
            def _():
                column_copy(unit, s, share_of(unit, s)).start()

        slot_of(unit, z)[...] = share_of(unit, z)[...]

    def column_stop(unit):
        @pl.when(is_middle)
        def _():
            stop_arrival(unit).wait_recv()
            ref = stop_of(unit)
            ref[...] = (ref[...].astype(FULL) + share_of(unit, 3 - z)[...].astype(FULL)).astype(LOW)
            column_copy(unit, 3 - z, ref).start()

    def column_sum_of(unit):
        for s in range(Z):

            @pl.when(from_layer(s))
            def _():
                column_arrival(unit, s).wait_recv()

        total = slot_of(unit, 0)[...].astype(FULL)
        for s in range(1, Z):
            total = total + slot_of(unit, s)[...].astype(FULL)
        return total.astype(LOW)

    for edge_z, s in ((1, 3), (2, 0)):

        @pl.when(z == edge_z)
        def _():
            for unit in range(7):
                ref = slot_of(unit, s)
                ref[...] = jnp.zeros_like(ref)

    def landing(unit, there):
        if unit < 3:
            return oa.at[unit, there]
        if unit < 5:
            return ou.at[unit - 3, :, pl.ds(pl.multiple_of(D * there, D), D)]
        return od.at[unit - 5, pl.ds(pl.multiple_of(SHARD * there, SHARD), SHARD)]

    def source_of(unit):
        return wide.at[unit] if unit < 5 else final.at[unit - 5]

    def share_copy(unit, i):
        there = at.peers[0] if i == 2 else rep
        return copy_to(
            landing(unit, there) if i == 2 else source_of(unit), landing(unit, there),
            gsend.at[unit, i], grecv.at[unit, i], at.peer(1) if i == 2 else at.peer(i),
        )

    def share_arrival(unit, i):
        ref = landing(unit, at.peers[i])
        return copy_to(ref, ref, gsend.at[unit, i], grecv.at[unit, i], at.peer(i))

    def share_out(unit):
        for i in range(2):
            share_copy(unit, i).start()
        pltpu.make_async_copy(source_of(unit), landing(unit, rep), glocal.at[unit]).start()
        yield
        share_arrival(unit, 0).wait_recv()
        share_copy(unit, 2).start()

    def edge_copy(unit):
        return copy_to(
            edge.at[unit, pl.ds(pl.multiple_of(SHARD * other, SHARD), SHARD)],
            wide.at[unit, :, own_half], esend.at[unit], erecv.at[unit], at.sibling,
        )

    def wide_end(unit):
        column_stop(unit)
        yield
        edge[unit] = column_sum_of(unit)
        edge_copy(unit).start()
        wide[unit, :, own_half] = edge[unit, pl.ds(pl.multiple_of(SHARD * core, SHARD), SHARD), :]
        yield
        edge_copy(unit).wait_recv()
        yield from share_out(unit)

    def up_flow(t):
        column_start(3 + t)
        yield
        yield from wide_end(3 + t)

    def down_copy(t, p):
        return copy_to(
            gd.at[t, at.peers[p]], dland.at[t, rep], dsend.at[t, p], drecv.at[t, p], at.peer(p)
        )

    def down_arrival(t, p):
        return copy_to(
            gd.at[t, rep], dland.at[t, at.peers[p]], dsend.at[t, p], drecv.at[t, p], at.peer(p)
        )

    def down_here(t):
        return pltpu.make_async_copy(gd.at[t, rep], dland.at[t, rep], dlocal.at[t])

    def down_flow(t):
        for p in range(3):
            down_copy(t, p).start()
        down_here(t).start()
        yield
        for p in range(3):
            down_arrival(t, p).wait_recv()
        down_here(t).wait()
        column_start(5 + t)
        yield
        column_stop(5 + t)
        yield
        final[t] = column_sum_of(5 + t)
        yield from share_out(5 + t)

    def flat(value):
        return value.reshape(value.shape[0] * value.shape[1], value.shape[2])

    words, regions = pl.ds(0, WORDS_HERE), pl.ds(WORDS_HERE, REGIONS_HERE)
    pieces = (
        ((0, words), (1, regions), (2, regions), (3, pl.ds(0, ROWS))),
        ((0, regions), (1, words), (2, words)),
    )

    def piece_each(turn, act):
        for p in (2, 0, 1):
            for m, rows in pieces[turn]:

                @pl.when(at.peers[p] == m)
                def _():
                    act(
                        copy_to(
                            ys0.at[m, rows], ya0.at[rep, rows],
                            ysend.at[3 * turn, p], yrecv.at[3 * turn, p], at.peer(p),
                        )
                    )

    def piece_arrivals(p):
        for turn in range(2):
            for m, rows in pieces[turn]:

                @pl.when(rep == m)
                def _():
                    ref = ya0.at[at.peers[p], rows]
                    copy_to(
                        ref, ref, ysend.at[3 * turn, p], yrecv.at[3 * turn, p], at.peer(p)
                    ).wait_recv()

    def y_flow(layer):
        if layer == 0:
            piece_each(0, lambda copy: copy.start())
            yield
            piece_each(1, lambda copy: copy.start())
        else:
            for p in (2, 0, 1):
                y_copy(layer, p).start()
        ya[layer][rep] = ys[layer][rep]
        y_forward(layer, 3).start()
        yield
        for p in range(3):
            if layer == 0:
                piece_arrivals(p)
            else:
                y_arrival(layer, p).wait_recv()
            y_forward(layer, p).start()
        yield
        for side in range(2):
            load_rows(layer, side).wait()
        grad = t_dot(flat(xa[layer][0]), flat(ya[layer][:, :, own_half]))
        for i in range(4):
            y_forward(layer, i).wait_recv()
        grad = grad + t_dot(flat(xa[layer][1]), flat(yb[layer][...]))
        share[layer] = grad.astype(LOW).reshape(Z, 2 * SHARD, PART)
        column_start(layer)
        yield
        yield from wide_end(layer)

    small_ways = (at.sibling, at.peer(0), at.peer(1))
    small_from = (gs, s1, s2)
    small_land = (s0, s3, s4)

    def small_copy(i):
        return copy_to(small_from[i], small_land[i], ssend.at[i], srecv.at[i], small_ways[i])

    def small_line(s):
        return copy_to(scol.at[z], scol.at[z], ssend.at[3 + s], srecv.at[3 + z], at.column(s))

    def small_arrival(s):
        return copy_to(scol.at[s], scol.at[s], ssend.at[3 + s], srecv.at[3 + s], at.column(s))

    def small_flow():
        small_copy(0).start()
        yield
        small_copy(0).wait_recv()
        s1[...] = gs[...] + s0[...]
        small_copy(1).start()
        yield
        small_copy(1).wait_recv()
        s2[...] = s1[...] + s3[...]
        small_copy(2).start()
        yield
        small_copy(2).wait_recv()
        scol[z] = s2[...] + s4[...]
        for s in range(Z):

            @pl.when(s != z)
            def _():
                small_line(s).start()

        yield
        for s in range(Z):

            @pl.when(s != z)
            def _():
                small_arrival(s).wait_recv()

        os[...] = (scol[0] + scol[1]) + (scol[2] + scol[3])

    u0, u1, w0, w1, y0, y1, y2, sm = range(8)
    flows = [
        up_flow(0), up_flow(1), down_flow(0), down_flow(1),
        y_flow(0), y_flow(1), y_flow(2), small_flow(),
    ]

    def go(*names):
        for name in names:
            next(flows[name], None)

    gs[...] = jnp.zeros_like(gs)
    gs[15:21, :] = gv[0:6, :]
    gs[21:29, :] = gb[...]

    def attend_back(grad, layer, parts, q, k, v, zs, dx_ref, marks):
        rows = LAYER_ROWS[layer]
        vecs = [row_of(vec, 5 * layer + i) for i in range(5)]
        unit, scale = norm_stats(zs[rows, :])
        dz = norm_back(grad, unit, scale, vecs[3])
        branch = dz.astype(LOW)
        out = ys[layer]
        out[3] = branch
        for i, value in enumerate(
            (column_sum(branch), column_sum(grad * unit), column_sum(grad))
        ):
            gs[5 * layer + 2 + i : 5 * layer + 3 + i, :] = value
        dx_ref[rows, :] = dz
        load(layer).wait()
        dm[rows, :] = dot_t(branch, wbuf[layer, 3]).astype(LOW)
        go(*marks[0])
        for (qrows, krows, pair_mask), mark in zip(parts, marks[1]):
            for group in range(HEADS // GROUP):
                head_back(
                    q, k, v, dm, out.at[0], out.at[1], out.at[2],
                    qrows, krows, pair_mask, group, rows.start,
                )
            go(*mark)
        gs[5 * layer : 5 * layer + 1, :] = column_sum(out[0])
        gs[5 * layer + 1 : 5 * layer + 2, :] = column_sum(out[2])
        go(*marks[2])
        dx_ref[rows, :] += (
            dot_t(out[0], wbuf[layer, 0])
            + (dot_t(out[1], wbuf[layer, 1]) + dot_t(out[2], wbuf[layer, 2]))
        )
        go(*marks[3])

    word_bias = length_bias(lengths, (WORDS_HERE, 1), 0)
    go(w1, u1, w0, u0)
    attend_back(
        d2[LANG, :], 1,
        [(LANG, LANG, turned_bias(WORDS_EACH, WORDS_EACH, word_bias))], q1, k1, v1, z1, d1,
        ([], [[y1]], [], [u1]),
    )
    attend_back(
        d2[VISN, :], 2,
        [(VISN, VISN, turned_bias(REGIONS_EACH, REGIONS_EACH, None))], q1, k1, v1, z1, d1,
        ([u0], [[y2]], [w1, w0], [u1, y1]),
    )
    attend_back(
        d1[...], 0,
        [
            (LANG, VISN, turned_bias(WORDS_EACH, REGIONS_EACH, None)),
            (VISN, LANG, turned_bias(REGIONS_EACH, WORDS_EACH, word_bias)),
        ],
        q0, k0, v0, z0, dx,
        ([u1, u0, y1], [[y0, u0, w1, w0, y1, y2], [y0]], [sm], [u1, y2, u0]),
    )
    go(sm, y0, y2, y0, sm, w1, w0, y1, y0, y1, sm, y2, w1, w0, y2, y1, sm, y0, y2, y0, y0)
    for flow in range(8):
        for _ in range(9):
            go(flow)

    for unit in range(7):
        pltpu.make_async_copy(source_of(unit), landing(unit, rep), glocal.at[unit]).wait()
        for i in (1, 2):
            share_arrival(unit, i).wait_recv()
        for i in range(3):
            share_copy(unit, i).wait_send()
        for s in range(Z):

            @pl.when(straight[s])
            def _():
                column_copy(unit, s, share_of(unit, s)).wait_send()

        @pl.when(is_end)
        def _():
            stop_copy(unit).wait_send()

        @pl.when(is_middle)
        def _():
            column_copy(unit, 3 - z, stop_of(unit)).wait_send()

    for turn in range(2):
        piece_each(turn, lambda copy: copy.wait_send())
    for layer in range(3):
        if layer > 0:
            for p in range(3):
                y_copy(layer, p).wait_send()
        for i in range(4):
            y_forward(layer, i).wait_send()
    for t in range(2):
        for p in range(3):
            down_copy(t, p).wait_send()
    for unit in range(WIDE_UNITS):
        edge_copy(unit).wait_send()
    for i in range(3):
        small_copy(i).wait_send()
    for s in range(Z):

        @pl.when(s != z)
        def _():
            small_line(s).wait_send()


def backward(d2, lengths, vec, w, kept, gu, gd, gv, gb, rows):
    dma = pltpu.SemaphoreType.DMA
    sizes = [layer_rows.stop - layer_rows.start for layer_rows in LAYER_ROWS]

    def each(lead, width):
        return [pltpu.VMEM((*lead, n, width), LOW) for n in sizes]

    return pl.pallas_call(
        backward_kernel,
        out_shape=(
            jax.ShapeDtypeStruct((ROWS, D), FULL),
            jax.ShapeDtypeStruct((3, 4, SHARD, D), LOW),
            jax.ShapeDtypeStruct((2, SHARD, FF), LOW),
            jax.ShapeDtypeStruct((2, PART, D), LOW),
            jax.ShapeDtypeStruct((32, D), FULL),
        ),
        in_specs=[ONCHIP, pl.BlockSpec(memory_space=pltpu.SMEM), ONCHIP, HBM]
        + [ONCHIP] * 8
        + [ONCHIP, HBM, ONCHIP, ONCHIP]
        + [HBM] * 6,
        out_specs=(ONCHIP, HBM, HBM, HBM, ONCHIP),
        scratch_shapes=[
            pltpu.VMEM((3, 4, D, D), LOW),
            *each((2, 4), D), *each((4,), D), *each((4,), D), *each((4,), PART),
            pltpu.VMEM((3, Z, 2 * SHARD, PART), LOW),
            pltpu.VMEM((2, Z, SHARD, D), LOW),
            pltpu.VMEM((WIDE_UNITS, Z, 2 * SHARD, PART), LOW),
            pltpu.VMEM((2, Z, SHARD, D), LOW),
            pltpu.VMEM((WIDE_UNITS, 2 * SHARD, PART), LOW),
            pltpu.VMEM((2, SHARD, D), LOW),
            pltpu.VMEM((WIDE_UNITS, 2 * SHARD, PART), LOW),
            pltpu.VMEM((WIDE_UNITS, SHARD, D), LOW),
            pltpu.VMEM((2, SHARD, D), LOW),
            pltpu.VMEM((ROWS, D), FULL),
            pltpu.VMEM((ROWS, D), LOW),
            *[pltpu.VMEM((32, D), FULL)] * 6,
            pltpu.VMEM((Z, 32, D), FULL),
            dma((3,)), dma((3, 2)),
            dma((4, 3)), dma((4, 3)), dma((3, 4)), dma((3, 4)),
            dma((2, 3)), dma((2, 3)), dma((2,)),
            dma((7, Z)), dma((7, Z)), dma((2, Z)), dma((2, Z)),
            dma((7,)), dma((7,)),
            dma((WIDE_UNITS,)), dma((WIDE_UNITS,)),
            dma((7, 3)), dma((7, 3)), dma((7,)),
            dma((3 + Z,)), dma((3 + Z,)),
        ],
        compiler_params=pltpu.CompilerParams(
            collective_id=2, has_side_effects=True, vmem_limit_bytes=VMEM_BYTES
        ),
        cost_estimate=pl.CostEstimate(
            flops=4_400_000_000, bytes_accessed=30_000_000, transcendentals=500_000
        ),
        name="attention_backward",
    )(d2, lengths, vec, w, *kept, gu, gd, gv, gb, *rows)


def finish_kernel(
    oa, ou, od, os, dx, lo, vo,
    wa, wu, wd, va, vf, vu, lang_grad, visn_grad, lang_out, visn_out,
):
    wa[...] = oa[...].astype(FULL)
    wu[...] = ou[...].astype(FULL)
    wd[...] = od[...].astype(FULL)

    @pl.when(pl.program_id(0) == 0)
    def _():
        lang_grad[...] = dx[LANG, :]
        visn_grad[...] = dx[VISN, :]
        lang_out[...] = lo[...]
        visn_out[...] = vo[...]
        spot = lax.axis_index("fsdp")
        for d in range(8):

            @pl.when(spot == d)
            def _():
                own = os[:, SHARD * d : SHARD * d + SHARD]
                for layer in range(3):
                    va[layer] = own[5 * layer : 5 * layer + 5, :]
                half = slice(PART * (d % 2), PART * (d % 2) + PART)
                for t in range(2):
                    vf[t] = own[15 + 3 * t : 18 + 3 * t, :]
                    row = 21 + 4 * t + d // 2
                    vu[t : t + 1, :] = os[row : row + 1, half]


def finish(oa, ou, od, os, dx, lo, vo):
    def whole(shape):
        return pl.BlockSpec(shape, lambda i: (0,) * len(shape))

    half = SHARD // 2
    parts = [
        pl.BlockSpec((3, 1, half, D), lambda i: (0, lax.div(i, 2), lax.rem(i, 2), 0)),
        pl.BlockSpec((2, SHARD, PART), lambda i: (0, 0, i)),
        pl.BlockSpec((2, half, D), lambda i: (0, i, 0)),
    ]
    words, regions = (WORDS_HERE, D), (REGIONS_HERE, D)
    smalls = [(3, 5, SHARD), (2, 3, SHARD), (2, PART)]
    singles = [*smalls, words, regions, words, regions]
    return pl.pallas_call(
        finish_kernel,
        grid=(8,),
        out_shape=tuple(jax.ShapeDtypeStruct(ref.shape, FULL) for ref in (oa, ou, od))
        + tuple(jax.ShapeDtypeStruct(shape, FULL) for shape in singles),
        in_specs=[*parts, whole((32, D)), whole((ROWS, D)), whole(words), whole(regions)],
        out_specs=(*parts, *[whole(shape) for shape in singles]),
        compiler_params=pltpu.CompilerParams(vmem_limit_bytes=VMEM_BYTES),
        cost_estimate=pl.CostEstimate(flops=0, bytes_accessed=15_000_000, transcendentals=0),
        name="widen_outputs",
    )(oa, ou, od, os, dx, lo, vo)


def fast_body(
    language, vision, lengths, attn_weights, attn_vectors, ffn_up, ffn_up_bias, ffn_down, ffn_vectors,
    language_cot, vision_cot,
):
    wide = ((0, 0), (0, PART - SHARD))
    vectors = [attn_vectors[i] for i in range(3)] + [ffn_vectors[i] for i in range(2)]
    small = jnp.concatenate([jnp.pad(piece, wide) for piece in vectors] + [ffn_up_bias])
    small = jnp.pad(small, ((0, 9), (0, 0)))
    wf, uf, df, ax0, vec, ub, onelow, two, *kept = gather(
        attn_weights, ffn_up, ffn_down, small, language, vision, lengths
    )
    q0, k0, v0, z0, q1, k1, v1, m1, z1 = kept
    lo, vo, d2, gu, gd, gv, gb, bx0, ax1, ax2, bx1, bx2 = feed(
        two, language_cot, vision_cot, uf.reshape(D, PART), df, vec, ub, ax0, onelow, m1,
        ffn_up, ffn_down,
    )
    dx, oa, ou, od, os = backward(
        d2, lengths, vec, wf.reshape(3, 4, D, D), (q0, k0, v0, z0, q1, k1, v1, z1),
        gu.reshape(2, Z, 2 * SHARD, PART), gd.reshape(2, Z, SHARD, D), gv, gb,
        (ax0, ax1, ax2, bx0, bx1, bx2),
    )
    wa, wu, wd, va, vf, vu, lang_grad, visn_grad, lang_out, visn_out = finish(
        oa, ou, od, os, dx, lo, vo
    )
    return (lang_out, visn_out, lang_grad, visn_grad, wa, va, wu, vu, wd, vf)


def layer_norm(values, gain, shift):
    mean = jnp.mean(values, axis=-1, keepdims=True)
    centred = values - mean
    spread = jnp.mean(centred * centred, axis=-1, keepdims=True)
    return centred * jax.lax.rsqrt(spread + 1e-06) * (1.0 + gain) + shift


def gelu_exact(values):
    return jax.nn.gelu(values, approximate=False)


def project(inputs, matrix):
    return jnp.einsum("isd,de->ise", inputs, matrix, preferred_element_type=jnp.float32)


def project_back(grads, matrix):
    return jnp.einsum("ise,de->isd", grads, matrix, preferred_element_type=jnp.float32)


def outer_sum(inputs, grads):
    return jnp.einsum("isd,ise->de", inputs, grads, preferred_element_type=jnp.float32)


def row_total(grads):
    return jnp.sum(grads.astype(jnp.float32), axis=(0, 1))


def gather_attn(attn_weights, attn_vectors, layer_index):
    return (
        lax.all_gather(attn_weights[layer_index], "fsdp", axis=1, tiled=True),
        lax.all_gather(attn_vectors[layer_index], "fsdp", axis=1, tiled=True),
    )


def regather_attn(attn_weights, attn_vectors, layer_index):
    return (
        lax.all_gather(attn_weights[layer_index], "fsdp", axis=1, tiled=True),
        lax.all_gather(attn_vectors[layer_index], "fsdp", axis=1, tiled=True),
    )


def gather_ffn(ffn_up, ffn_up_bias, ffn_down, ffn_vectors, layer_index):
    return (
        lax.all_gather(ffn_up[layer_index], "fsdp", axis=0, tiled=True),
        lax.all_gather(ffn_up_bias[layer_index], "fsdp", axis=0, tiled=True),
        lax.all_gather(ffn_down[layer_index], "fsdp", axis=0, tiled=True),
        lax.all_gather(ffn_vectors[layer_index], "fsdp", axis=1, tiled=True),
    )


def regather_ffn(ffn_up, ffn_up_bias, ffn_down, ffn_vectors, layer_index):
    return (
        lax.all_gather(ffn_up[layer_index], "fsdp", axis=0, tiled=True),
        lax.all_gather(ffn_up_bias[layer_index], "fsdp", axis=0, tiled=True),
        lax.all_gather(ffn_down[layer_index], "fsdp", axis=0, tiled=True),
        lax.all_gather(ffn_vectors[layer_index], "fsdp", axis=1, tiled=True),
    )


def settle_attn(grad_weights, grad_vector):
    shards = (
        lax.psum_scatter(grad_weights, "fsdp", scatter_dimension=1, tiled=True),
        lax.psum_scatter(grad_vector, "fsdp", scatter_dimension=1, tiled=True),
    )
    quarter = lax.psum_scatter(
        shards[0].astype(jnp.bfloat16), "rep", scatter_dimension=2, tiled=True
    ).astype(jnp.float32)
    vector_sum = lax.psum(shards[1], "rep")
    whole = lax.all_gather(quarter.astype(jnp.bfloat16), "rep", axis=2, tiled=True).astype(
        quarter.dtype
    )
    return (whole, vector_sum)


def settle_ffn(grad_up, grad_up_bias, grad_down, grad_vector):
    shards = (
        lax.psum_scatter(grad_up, "fsdp", scatter_dimension=0, tiled=True),
        lax.psum_scatter(grad_up_bias, "fsdp", scatter_dimension=0, tiled=True),
        lax.psum_scatter(grad_down, "fsdp", scatter_dimension=0, tiled=True),
        lax.psum_scatter(grad_vector, "fsdp", scatter_dimension=1, tiled=True),
    )
    quarters = (
        lax.psum_scatter(
            shards[0].astype(jnp.bfloat16), "rep", scatter_dimension=1, tiled=True
        ).astype(jnp.float32),
        lax.psum_scatter(
            shards[2].astype(jnp.bfloat16), "rep", scatter_dimension=1, tiled=True
        ).astype(jnp.float32),
    )
    smalls = lax.psum((shards[1], shards[3]), "rep")
    wholes = (
        lax.all_gather(quarters[0].astype(jnp.bfloat16), "rep", axis=1, tiled=True).astype(
            jnp.float32
        ),
        lax.all_gather(quarters[1].astype(jnp.bfloat16), "rep", axis=1, tiled=True).astype(
            jnp.float32
        ),
    )
    return (wholes[0], smalls[0], wholes[1], smalls[1])


def attend_forward(residual, query_low, key_low, weights, vector, key_bias):
    item_count, query_len, model_width = residual.shape
    key_len = key_low.shape[1]
    head_size = model_width // HEADS
    vector = vector.astype(jnp.float32)
    queries = (project(query_low, weights[0]) + vector[0]).astype(jnp.bfloat16)
    key_heads = project(key_low, weights[1]).astype(jnp.bfloat16)
    values = (project(key_low, weights[2]) + vector[1]).astype(jnp.bfloat16)
    queries = queries.reshape(item_count, query_len, HEADS, head_size)
    key_heads = key_heads.reshape(item_count, key_len, HEADS, head_size)
    values = values.reshape(item_count, key_len, HEADS, head_size)
    scores = jnp.einsum(
        "iqhd,ikhd->ihqk", queries, key_heads, preferred_element_type=jnp.float32
    ) / math.sqrt(head_size)
    scores = scores + key_bias[:, None, None, :]
    highest = jnp.max(scores, axis=-1, keepdims=True)
    exponent = jnp.exp(scores - highest)
    attn_probs = exponent / jnp.sum(exponent, axis=-1, keepdims=True)
    mixed_heads = jnp.einsum(
        "ihqk,ikhd->iqhd",
        attn_probs.astype(jnp.bfloat16),
        values,
        preferred_element_type=jnp.float32,
    )
    mixed_heads = mixed_heads.astype(jnp.bfloat16).reshape(item_count, query_len, model_width)
    pre_norm = residual + (project(mixed_heads, weights[3]) + vector[2])
    normed = layer_norm(pre_norm, vector[3], vector[4])
    return (normed, (queries, key_heads, values, attn_probs, mixed_heads, pre_norm))


def attend_backward(grad_out, query_low, key_low, weights, vector, kept):
    queries, key_heads, values, attn_probs, mixed_heads, pre_norm = kept
    item_count, query_len, head_count, head_size = queries.shape
    key_len = key_heads.shape[1]
    model_width = head_count * head_size
    vector = vector.astype(jnp.float32)
    _, pull_norm = jax.vjp(layer_norm, pre_norm, vector[3], vector[4])
    grad_pre, grad_gain, grad_shift = pull_norm(grad_out)
    grad_branch = grad_pre.astype(jnp.bfloat16)
    grad_out_weight = outer_sum(mixed_heads, grad_branch)
    grad_mixed = project_back(grad_branch, weights[3]).astype(jnp.bfloat16)
    grad_mixed = grad_mixed.reshape(item_count, query_len, head_count, head_size)
    grad_probs = jnp.einsum(
        "iqhd,ikhd->ihqk", grad_mixed, values, preferred_element_type=jnp.float32
    )
    grad_values = jnp.einsum(
        "ihqk,iqhd->ikhd",
        attn_probs.astype(jnp.bfloat16),
        grad_mixed,
        preferred_element_type=jnp.float32,
    ).astype(jnp.bfloat16)
    grad_scores = attn_probs * (
        grad_probs - jnp.sum(attn_probs * grad_probs, axis=-1, keepdims=True)
    )
    grad_scores = grad_scores.astype(jnp.bfloat16)
    inverse = 1.0 / math.sqrt(head_size)
    grad_queries = (
        jnp.einsum("ihqk,ikhd->iqhd", grad_scores, key_heads, preferred_element_type=jnp.float32)
        * inverse
    )
    grad_queries = grad_queries.astype(jnp.bfloat16).reshape(item_count, query_len, model_width)
    grad_keys = (
        jnp.einsum("ihqk,iqhd->ikhd", grad_scores, queries, preferred_element_type=jnp.float32)
        * inverse
    )
    grad_keys = grad_keys.astype(jnp.bfloat16).reshape(item_count, key_len, model_width)
    grad_values = grad_values.reshape(item_count, key_len, model_width)
    grad_weights = jnp.stack(
        [
            outer_sum(query_low, grad_queries),
            outer_sum(key_low, grad_keys),
            outer_sum(key_low, grad_values),
            grad_out_weight,
        ]
    )
    grad_vector = jnp.stack(
        [
            row_total(grad_queries),
            row_total(grad_values),
            row_total(grad_branch),
            grad_gain,
            grad_shift,
        ]
    )
    grad_query_low = project_back(grad_queries, weights[0])
    grad_key_low = project_back(grad_keys, weights[1]) + project_back(grad_values, weights[2])
    return (grad_pre, grad_query_low, grad_key_low, grad_weights, grad_vector)


def feed_forward(residual, up_weight, up_bias, down_weight, vector):
    vector = vector.astype(jnp.float32)
    residual_low = residual.astype(jnp.bfloat16)
    hidden = project(residual_low, up_weight) + up_bias.astype(jnp.float32)
    active = gelu_exact(hidden).astype(jnp.bfloat16)
    pre_norm = residual + (project(active, down_weight) + vector[0])
    normed = layer_norm(pre_norm, vector[1], vector[2])
    return (normed, (residual_low, hidden, active, pre_norm))


def feed_backward(grad_out, up_weight, down_weight, vector, kept):
    residual_low, hidden, active, pre_norm = kept
    vector = vector.astype(jnp.float32)
    _, pull_norm = jax.vjp(layer_norm, pre_norm, vector[1], vector[2])
    grad_pre, grad_gain, grad_shift = pull_norm(grad_out)
    grad_branch = grad_pre.astype(jnp.bfloat16)
    grad_down = outer_sum(active, grad_branch)
    grad_active = project_back(grad_branch, down_weight)
    _, pull_gate = jax.vjp(gelu_exact, hidden)
    grad_hidden = pull_gate(grad_active)[0].astype(jnp.bfloat16)
    grad_up = outer_sum(residual_low, grad_hidden)
    grad_up_bias = row_total(grad_hidden)
    grad_residual = grad_pre + project_back(grad_hidden, up_weight)
    grad_vector = jnp.stack([row_total(grad_branch), grad_gain, grad_shift])
    return (grad_residual, grad_up, grad_up_bias, grad_down, grad_vector)


def body(
    language,
    vision,
    lengths,
    attn_weights,
    attn_vectors,
    ffn_up,
    ffn_up_bias,
    ffn_down,
    ffn_vectors,
    language_cot,
    vision_cot,
):
    item_count = lengths.shape[0]
    model_width = language.shape[1]
    word_slots = language.shape[0] // item_count
    region_slots = vision.shape[0] // item_count
    lang_rows = language.reshape(item_count, word_slots, model_width)
    visn_rows = vision.reshape(item_count, region_slots, model_width)
    word_bias = jnp.where(
        jnp.arange(word_slots)[None, :] < lengths[:, None], 0.0, -1000000000.0
    ).astype(jnp.float32)
    region_bias = jnp.zeros((item_count, region_slots), jnp.float32)
    cross_weights, cross_vector = gather_attn(attn_weights, attn_vectors, 0)
    lang_low = lang_rows.astype(jnp.bfloat16)
    visn_low = visn_rows.astype(jnp.bfloat16)
    lang_one = attend_forward(
        lang_rows, lang_low, visn_low, cross_weights, cross_vector, region_bias
    )[0]
    visn_one = attend_forward(
        visn_rows, visn_low, lang_low, cross_weights, cross_vector, word_bias
    )[0]
    lang_self = gather_attn(attn_weights, attn_vectors, 1)
    lang_one_low = lang_one.astype(jnp.bfloat16)
    lang_two, lang_self_kept = attend_forward(
        lang_one, lang_one_low, lang_one_low, lang_self[0], lang_self[1], word_bias
    )
    visn_self = gather_attn(attn_weights, attn_vectors, 2)
    visn_one_low = visn_one.astype(jnp.bfloat16)
    visn_two, visn_self_kept = attend_forward(
        visn_one, visn_one_low, visn_one_low, visn_self[0], visn_self[1], region_bias
    )
    lang_ffn = gather_ffn(ffn_up, ffn_up_bias, ffn_down, ffn_vectors, 0)
    lang_three, lang_ffn_kept = feed_forward(
        lang_two, lang_ffn[0], lang_ffn[1], lang_ffn[2], lang_ffn[3]
    )
    visn_ffn = gather_ffn(ffn_up, ffn_up_bias, ffn_down, ffn_vectors, 1)
    visn_three, visn_ffn_kept = feed_forward(
        visn_two, visn_ffn[0], visn_ffn[1], visn_ffn[2], visn_ffn[3]
    )
    visn_ffn_back = regather_ffn(ffn_up, ffn_up_bias, ffn_down, ffn_vectors, 1)
    visn_back = feed_backward(
        vision_cot.reshape(item_count, region_slots, model_width),
        visn_ffn_back[0],
        visn_ffn_back[2],
        visn_ffn_back[3],
        visn_ffn_kept,
    )
    visn_ffn_grads = settle_ffn(visn_back[1], visn_back[2], visn_back[3], visn_back[4])
    lang_ffn_back = regather_ffn(ffn_up, ffn_up_bias, ffn_down, ffn_vectors, 0)
    lang_back = feed_backward(
        language_cot.reshape(item_count, word_slots, model_width),
        lang_ffn_back[0],
        lang_ffn_back[2],
        lang_ffn_back[3],
        lang_ffn_kept,
    )
    lang_ffn_grads = settle_ffn(lang_back[1], lang_back[2], lang_back[3], lang_back[4])
    visn_self_back = regather_attn(attn_weights, attn_vectors, 2)
    visn_attn = attend_backward(
        visn_back[0],
        visn_one_low,
        visn_one_low,
        visn_self_back[0],
        visn_self_back[1],
        visn_self_kept,
    )
    visn_self_grads = settle_attn(visn_attn[3], visn_attn[4])
    grad_visn_one = visn_attn[0] + visn_attn[1] + visn_attn[2]
    lang_self_back = regather_attn(attn_weights, attn_vectors, 1)
    lang_attn = attend_backward(
        lang_back[0],
        lang_one_low,
        lang_one_low,
        lang_self_back[0],
        lang_self_back[1],
        lang_self_kept,
    )
    lang_self_grads = settle_attn(lang_attn[3], lang_attn[4])
    grad_lang_one = lang_attn[0] + lang_attn[1] + lang_attn[2]
    cross_back = regather_attn(attn_weights, attn_vectors, 0)
    lang_cross_kept = attend_forward(
        lang_rows, lang_low, visn_low, cross_back[0], cross_back[1], region_bias
    )[1]
    visn_cross_kept = attend_forward(
        visn_rows, visn_low, lang_low, cross_back[0], cross_back[1], word_bias
    )[1]
    lang_cross = attend_backward(
        grad_lang_one, lang_low, visn_low, cross_back[0], cross_back[1], lang_cross_kept
    )
    visn_cross = attend_backward(
        grad_visn_one, visn_low, lang_low, cross_back[0], cross_back[1], visn_cross_kept
    )
    cross_grads = settle_attn(lang_cross[3] + visn_cross[3], lang_cross[4] + visn_cross[4])
    grad_language = lang_cross[0] + lang_cross[1] + visn_cross[2]
    grad_vision = visn_cross[0] + visn_cross[1] + lang_cross[2]
    return (
        lang_three.reshape(item_count * word_slots, model_width),
        visn_three.reshape(item_count * region_slots, model_width),
        grad_language.reshape(item_count * word_slots, model_width),
        grad_vision.reshape(item_count * region_slots, model_width),
        jnp.stack([cross_grads[0], lang_self_grads[0], visn_self_grads[0]]),
        jnp.stack([cross_grads[1], lang_self_grads[1], visn_self_grads[1]]),
        jnp.stack([lang_ffn_grads[0], visn_ffn_grads[0]]),
        jnp.stack([lang_ffn_grads[1], visn_ffn_grads[1]]),
        jnp.stack([lang_ffn_grads[2], visn_ffn_grads[2]]),
        jnp.stack([lang_ffn_grads[3], visn_ffn_grads[3]]),
    )


def solution(mesh):
    shape = dict(mesh.shape)
    fast = shape["rep"] == 4 and shape["fsdp"] == 8
    return jax.shard_map(
        fast_body if fast else body,
        mesh=mesh,
        in_specs=(
            P(("rep", "fsdp"), None),
            P(("rep", "fsdp"), None),
            P(("rep", "fsdp")),
            P(None, None, "fsdp", None),
            P(None, None, "fsdp"),
            P(None, "fsdp", None),
            P(None, "fsdp"),
            P(None, "fsdp", None),
            P(None, None, "fsdp"),
            P(("rep", "fsdp"), None),
            P(("rep", "fsdp"), None),
        ),
        out_specs=(
            P(("rep", "fsdp"), None),
            P(("rep", "fsdp"), None),
            P(("rep", "fsdp"), None),
            P(("rep", "fsdp"), None),
            P(None, None, "fsdp", None),
            P(None, None, "fsdp"),
            P(None, "fsdp", None),
            P(None, "fsdp"),
            P(None, "fsdp", None),
            P(None, None, "fsdp"),
        ),
        check_vma=False,
    )
```

```python
import functools
import math

import jax
import jax.numpy as jnp
from jax import lax
from jax.experimental import pallas as pl
from jax.experimental.pallas import tpu as pltpu
from jax.sharding import PartitionSpec as P

HEADS = 12
LOW = jnp.bfloat16
FULL = jnp.float32
VMEM_BYTES = 58 * 1024 * 1024
HBM = pl.BlockSpec(memory_space=pl.ANY)
ONCHIP = pl.BlockSpec(memory_space=pltpu.VMEM)


D = 768
WORDS_HERE = 80
REGIONS_HERE = 144
ROWS = WORDS_HERE + REGIONS_HERE
LANG = slice(0, WORDS_HERE)
VISN = slice(WORDS_HERE, ROWS)
EVERY = slice(0, ROWS)
ITEMS_HERE = 4
FF = 3072
PART = 384
SHARD = 96
Z = 4


def copy_to(src, dst, send, recv, device):
    return pltpu.make_async_remote_copy(
        src_ref=src,
        dst_ref=dst,
        send_sem=send,
        recv_sem=recv,
        device_id=device,
        device_id_type=pl.DeviceIdType.MESH,
    )


class Place:
    def __init__(self):
        rep, spot = lax.axis_index("rep"), lax.axis_index("fsdp")
        z = lax.div(spot, 2)
        core = spot - 2 * z
        y = lax.div(rep, 2)
        x = rep - 2 * y
        self.rep, self.spot, self.z, self.core, self.other = rep, spot, z, core, 1 - core
        along_x, along_y = (1 - x) + 2 * y, x + 2 * (1 - y)
        turn = core * (along_y - along_x)
        self.peers = [along_x + turn, along_y - turn, (1 - x) + 2 * (1 - y)]
        self.sibling = (rep, 2 * z + (1 - core))

    def peer(self, p):
        return (self.peers[p], self.spot)

    def above(self):
        return (self.rep, self.spot + 2)

    def below(self):
        return (self.rep, self.spot - 2)

    def column(self, s):
        return (self.rep, 2 * s + self.core)

    def enter(self, line):
        barrier = pltpu.get_barrier_semaphore()

        def greet(device):
            pl.semaphore_signal(
                barrier, inc=1, device_id=device, device_id_type=pl.DeviceIdType.MESH
            )

        for p in range(3):
            greet(self.peer(p))
        greet(self.sibling)
        number = 4
        if line == 1:

            @pl.when(self.z > 0)
            def _():
                greet(self.below())

            @pl.when(self.z < Z - 1)
            def _():
                greet(self.above())

            number = 4 + jnp.minimum(self.z, 1) + jnp.minimum(Z - 1 - self.z, 1)
        if line == 2:
            self.others(lambda s: greet(self.column(s)))
            number = 4 + Z - 1
        pl.semaphore_wait(barrier, number)

    def others(self, act):
        for s in (0, 3, 1, 2):

            @pl.when(s != self.z)
            def _():
                act(s)


class Chain:
    def __init__(self, at, units, slot, own, send, recv):
        self.at, self.units, self.slot, self.own = at, units, slot, own
        self.send, self.recv = send, recv

    def copy(self, index, s, source, upward):
        return copy_to(
            source, self.slot(self.units[index], s),
            self.send.at[index, s, 0 if upward else 1], self.recv.at[index, s],
            self.at.above() if upward else self.at.below(),
        )

    def send_step(self, index, k):
        z, unit = self.at.z, self.units[index]

        @pl.when((z - k >= 0) & (z < Z - 1))
        def _():
            source = self.own(unit) if k == 0 else self.slot(unit, z - k)
            self.copy(index, z - k, source, True).start()

        @pl.when((z + k <= Z - 1) & (z > 0))
        def _():
            source = self.own(unit) if k == 0 else self.slot(unit, z + k)
            self.copy(index, z + k, source, False).start()

    def come(self, k):
        z = self.at.z
        return ((z - 1 - k, z - 1 - k >= 0), (z + 1 + k, z + 1 + k <= Z - 1))

    def wait_step(self, index, k):
        for upward, (s, there) in zip((True, False), self.come(k)):

            @pl.when(there)
            def _():
                ref = self.slot(self.units[index], s)
                self.copy(index, s, ref, not upward).wait_recv()

    def finish(self):
        z = self.at.z
        for index, unit in enumerate(self.units):
            for s in range(Z):

                @pl.when((s <= z) & (z < Z - 1))
                def _():
                    self.copy(index, s, self.slot(unit, s), True).wait_send()

                @pl.when((s >= z) & (z > 0))
                def _():
                    self.copy(index, s, self.slot(unit, s), False).wait_send()


class FeedWeights:
    def __init__(self, at, up, down, dst, uf, df, sems):
        self.at, self.up, self.down = at, up, down
        self.dst, self.uf, self.df = dst, uf, df
        (
            self.usend, self.urecv, self.dsend, self.drecv, self.ulocal, self.dlocal,
            self.xsend, self.xrecv,
        ) = sems
        self.columns = pl.ds(pl.multiple_of(D * at.rep, D), D)

    def rows(self, rep):
        return pl.ds(pl.multiple_of(PART * self.at.core + SHARD * rep, SHARD), SHARD)

    def slot(self, kind, s):
        return self.uf.at[2 * s + self.at.core] if kind == "u" else self.dst.at[s]

    def own(self, kind):
        if kind == "u":
            return self.up.at[:, self.columns]
        return self.down.at[pl.ds(pl.multiple_of(SHARD * self.at.rep, SHARD), SHARD)]

    def up_across(self, s, source):
        target = self.uf.at[2 * s + self.at.core]
        return copy_to(source, target, self.usend.at[s], self.urecv.at[s], self.at.sibling)

    def up_here(self):
        target = self.uf.at[2 * self.at.z + self.at.core]
        return pltpu.make_async_copy(self.up.at[:, self.columns], target, self.ulocal)

    def down_there(self, s, source):
        return copy_to(
            source, self.df.at[self.rows(self.at.rep)],
            self.dsend.at[s], self.drecv.at[self.at.rep], (s, self.at.spot),
        )

    def down_here(self, source):
        return pltpu.make_async_copy(source, self.df.at[self.rows(self.at.rep)], self.dlocal)

    def down_across(self):
        ref = self.df.at[pl.ds(pl.multiple_of(PART * self.at.core, PART), PART)]
        return copy_to(ref, ref, self.xsend, self.xrecv, self.at.sibling)

    def pass_on(self, kind, s, source):
        if kind == "u":
            self.up_across(s, source).start()
        else:

            @pl.when(s != self.at.rep)
            def _():
                self.down_there(s, source).start()

            @pl.when(s == self.at.rep)
            def _():
                self.down_here(source).start()

    def own_start(self, kind):
        if kind == "u":
            self.up_here().start()
        self.pass_on(kind, self.at.z, self.own(kind))

    def collect(self):
        for p in range(3):
            there = self.at.peers[p]
            copy_to(
                self.dst.at[0], self.df.at[self.rows(there)],
                self.dsend.at[0], self.drecv.at[there], self.at.peer(p),
            ).wait_recv()
        self.down_here(self.dst.at[0]).wait()
        self.down_across().start()

    def finish(self):
        self.up_here().wait()
        for s in range(Z):
            self.up_across(s, self.uf.at[2 * s + self.at.core]).wait()

            @pl.when(s != self.at.rep)
            def _():
                self.down_there(s, self.dst.at[s]).wait_send()

        self.down_across().wait()


def feed_sems():
    dma = pltpu.SemaphoreType.DMA
    return [dma((Z,)), dma((Z,)), dma((Z,)), dma((Z,)), dma, dma, dma, dma]


UNITS = [("a", 0), ("s", 0), ("a", 1), ("a", 2), ("u", 1), ("d", 1)]


def gather_kernel(
    aw, up, down, small, language, vision, lengths,
    wf, uf, df, vec, ub, xlow, onelow, two, q0, k0, v0, m0, z0, q1, k1, v1, m1, z1,
    wv, dst, sf, x, one,
    zsend, zrecv, psend, precv, asend, arecv, ssend, srecv,
    alocal, slocal, wlocal, xlocal, *fsems,
):
    at = Place()
    rep, z, core = at.rep, at.z, at.core
    rows_in = [
        pltpu.make_async_copy(ref, x.at[rows], xlocal.at[i])
        for i, (ref, rows) in enumerate(
            ((language, pl.ds(0, WORDS_HERE)), (vision, pl.ds(WORDS_HERE, REGIONS_HERE)))
        )
    ]
    for copy in rows_in:
        copy.start()
    at.enter(1)
    feed_weights = FeedWeights(at, up.at[1], down.at[1], dst, uf, df, fsems)

    def slot(unit, s):
        kind, i = unit
        if kind == "a":
            return wv.at[i, rep, 2 * s + core]
        return sf.at[2 * s + core] if kind == "s" else feed_weights.slot(kind, s)

    def own(unit):
        kind, i = unit
        if kind == "a":
            return aw.at[i, rep]
        return small if kind == "s" else feed_weights.own(kind)

    chain = Chain(at, UNITS, slot, own, zsend, zrecv)

    def plane_copy(layer, s, i):
        ref = wv.at[layer, at.peers[0] if i == 2 else rep, 2 * s + core]
        there = at.peer(1) if i == 2 else at.peer(i)
        return copy_to(ref, ref, psend.at[layer, s, i], precv.at[layer, s, i], there)

    def plane_arrival(layer, s, i):
        ref = wv.at[layer, at.peers[i], 2 * s + core]
        return copy_to(ref, ref, psend.at[layer, s, i], precv.at[layer, s, i], at.peer(i))

    def small_copy(s, source):
        return copy_to(source, sf.at[2 * s + core], ssend.at[s], srecv.at[s], at.sibling)

    def pass_on(unit, s, source):
        kind, i = unit
        if kind == "a":
            for p in range(2):
                plane_copy(i, s, p).start()
        elif kind == "s":
            small_copy(s, source).start()
        else:
            feed_weights.pass_on(kind, s, source)

    def shard_here(layer):
        return pltpu.make_async_copy(aw.at[layer], wv.at[layer, :, 2 * z + core], alocal.at[layer])

    def small_here():
        return pltpu.make_async_copy(small, sf.at[2 * z + core], slocal)

    def own_start(unit):
        kind, i = unit
        if kind == "a":
            shard_here(i).start()
            copy_to(
                aw.at[i], wv.at[i, :, 2 * z + core], asend.at[i, z], arecv.at[i, z], at.sibling
            ).start()
        elif kind == "s":
            small_here().start()
            pass_on(unit, z, small)
        else:
            feed_weights.own_start(kind)

    def line_send_step(index, k):
        chain.send_step(index, k)
        if k == 0:
            own_start(UNITS[index])

    def pass_step(index, k):
        unit = UNITS[index]
        for s, there in chain.come(k):

            @pl.when(there)
            def _():
                pass_on(unit, s, slot(unit, s))

    def core_copy(layer, s):
        ref = wv.at[layer, :, 2 * s + core]
        return copy_to(ref, ref, asend.at[layer, s], arecv.at[layer, s], at.sibling)

    def core_arrival(layer, s):
        ref = wv.at[layer, :, 2 * s + at.other]
        return copy_to(ref, ref, asend.at[layer, s], arecv.at[layer, s], at.sibling)

    def relay_step(layer, k):
        for s, there in chain.come(k):

            @pl.when(there)
            def _():
                plane_arrival(layer, s, 0).wait_recv()
                plane_copy(layer, s, 2).start()

    def plane_step(layer, k):
        for s, there in chain.come(k):

            @pl.when(there)
            def _():
                plane_arrival(layer, s, 1).wait_recv()
                plane_arrival(layer, s, 2).wait_recv()
                core_copy(layer, s).start()

    count = len(UNITS)

    def exchange():
        line_send_step(0, 0)
        for time in range(count + 6):
            if time + 1 < count:
                line_send_step(time + 1, 0)
            for index, unit in enumerate(UNITS):
                k = time - index
                if 1 <= k <= 3:
                    chain.wait_step(index, k - 1)
                    if k <= 2:
                        line_send_step(index, k)
                    pass_step(index, k - 1)
                    yield time
                if unit[0] == "a" and 0 <= k - 2 <= 2:
                    relay_step(unit[1], k - 2)
                    yield time
                if unit[0] == "a" and 0 <= k - 3 <= 2:
                    plane_step(unit[1], k - 3)
                    yield time
            yield time + 1

    steps = exchange()
    clock = [0]

    def pump(times=1):
        for _ in range(times):
            clock[0] = next(steps, 99)

    def until(time):
        while clock[0] < time:
            pump()

    def ready(layer):
        until(UNITS.index(("a", layer)) + 6)
        shard_here(layer).wait()
        for s in range(Z):
            core_arrival(layer, s).wait_recv()
        pltpu.make_async_copy(wv.at[layer], wf.at[layer], wlocal.at[layer]).start()

    for copy in rows_in:
        copy.wait()
    xlow[...] = x[...].astype(LOW)
    until(UNITS.index(("s", 0)) + 4)
    small_here().wait()
    for s in range(Z):
        copy_to(
            small, sf.at[2 * s + at.other], ssend.at[s], srecv.at[s], at.sibling
        ).wait_recv()
    line = lax.broadcasted_iota(jnp.int32, (128, D), 0)
    lane = lax.broadcasted_iota(jnp.int32, (128, D), 1)
    vectors = jnp.zeros((32, D), FULL)
    for d in range(8):
        pick = ((lane == line + SHARD * d) & (line < SHARD)).astype(FULL).astype(LOW)
        vectors = vectors + dot(sf[d, :, :128], pick)
    vec[...] = vectors
    ub[...] = jnp.zeros_like(ub)
    for c in range(2):
        ub[0:2, PART * c : PART * c + PART] = sf[2 * rep + c].astype(FULL)[21:23, :]

    word_bias = length_bias(lengths, (1, WORDS_HERE), 1)
    ready(0)
    attend(
        x, xlow, wv, vec, 0, EVERY,
        [
            (LANG, VISN, pair_bias(WORDS_EACH, REGIONS_EACH, None)),
            (VISN, LANG, pair_bias(REGIONS_EACH, WORDS_EACH, word_bias)),
        ],
        q0, k0, v0, m0, z0, one, pump,
    )
    onelow[...] = one[...].astype(LOW)
    ready(1)
    attend(
        one, onelow, wv, vec, 1, LANG,
        [(LANG, LANG, pair_bias(WORDS_EACH, WORDS_EACH, word_bias))],
        q1, k1, v1, m1, z1, two, pump,
    )
    ready(2)
    attend(
        one, onelow, wv, vec, 2, VISN,
        [(VISN, VISN, pair_bias(REGIONS_EACH, REGIONS_EACH, None))],
        q1, k1, v1, m1, z1, two, pump,
    )
    until(99)
    feed_weights.collect()

    for layer in range(3):
        pltpu.make_async_copy(wv.at[layer], wf.at[layer], wlocal.at[layer]).wait()
        for s in range(Z):
            core_copy(layer, s).wait_send()

            @pl.when(s != z)
            def _():
                for i in range(3):
                    plane_copy(layer, s, i).wait_send()

    for s in range(Z):
        small_copy(s, small).wait_send()
    chain.finish()
    feed_weights.finish()


def gather(aw, up, down, small, language, vision, lengths):
    dma = pltpu.SemaphoreType.DMA
    count = len(UNITS)
    full = jax.ShapeDtypeStruct((ROWS, D), FULL)
    low = jax.ShapeDtypeStruct((ROWS, D), LOW)
    return pl.pallas_call(
        gather_kernel,
        out_shape=(
            jax.ShapeDtypeStruct((3, 4, 8, SHARD, D), LOW),
            jax.ShapeDtypeStruct((8, SHARD, D), LOW),
            jax.ShapeDtypeStruct((D, D), LOW),
            jax.ShapeDtypeStruct((32, D), FULL),
            jax.ShapeDtypeStruct((8, D), FULL),
            low, low, full,
            low, low, low, low, full,
            low, low, low, low, full,
        ),
        in_specs=[HBM] * 6 + [pl.BlockSpec(memory_space=pltpu.SMEM)],
        out_specs=(HBM,) * 3 + (ONCHIP,) * 15,
        scratch_shapes=[
            pltpu.VMEM((3, 4, 8, SHARD, D), LOW),
            pltpu.VMEM((Z, SHARD, D), LOW),
            pltpu.VMEM((8, 32, PART), LOW),
            pltpu.VMEM((ROWS, D), FULL),
            pltpu.VMEM((ROWS, D), FULL),
            dma((count, Z, 2)), dma((count, Z)),
            dma((3, Z, 3)), dma((3, Z, 3)),
            dma((3, Z)), dma((3, Z)),
            dma((Z,)), dma((Z,)),
            dma((3,)), dma, dma((3,)), dma((2,)),
            *feed_sems(),
        ],
        compiler_params=pltpu.CompilerParams(
            collective_id=0, has_side_effects=True, vmem_limit_bytes=VMEM_BYTES
        ),
        cost_estimate=pl.CostEstimate(
            flops=2_200_000_000, bytes_accessed=40_000_000, transcendentals=500_000
        ),
        name="gather_attention",
    )(aw, up, down, small, language, vision, lengths)


def dot(a, b):
    return jnp.dot(a, b, preferred_element_type=FULL)


def dot_t(a, b):
    return lax.dot_general(a, b, (((1,), (1,)), ((), ())), preferred_element_type=FULL)


def t_dot(a, b):
    return lax.dot_general(a, b, (((0,), (0,)), ((), ())), preferred_element_type=FULL)


def column_sum(a):
    return jnp.sum(a.astype(FULL), axis=0, keepdims=True)


def norm_stats(pre):
    mean = jnp.mean(pre, axis=-1, keepdims=True)
    centred = pre - mean
    spread = jnp.mean(centred * centred, axis=-1, keepdims=True)
    scale = lax.rsqrt(spread + 1e-06)
    return centred * scale, scale


def norm_back(grad, unit, scale, gain):
    flow = grad * (1.0 + gain)
    return (
        flow
        - jnp.mean(flow, axis=-1, keepdims=True)
        - unit * jnp.mean(flow * unit, axis=-1, keepdims=True)
    ) * scale


def item_of(index, size):
    return sum((index >= size * k).astype(jnp.int32) for k in range(1, ITEMS_HERE))


def pair_bias(query_size, key_size, key_bias):
    shape = (query_size * ITEMS_HERE, key_size * ITEMS_HERE)
    query_item = item_of(lax.broadcasted_iota(jnp.int32, shape, 0), query_size)
    key_item = item_of(lax.broadcasted_iota(jnp.int32, shape, 1), key_size)
    bias = jnp.where(query_item == key_item, 0.0, -1e30)
    return bias if key_bias is None else bias + key_bias


GROUP = 4


def head_masks(dtype):
    lane = lax.broadcasted_iota(jnp.int32, (1, 64 * GROUP), 1)
    return [
        ((lane >= 64 * i) & (lane < 64 * i + 64)).astype(FULL).astype(dtype) for i in range(GROUP)
    ]


def stacked(value):
    return jnp.concatenate([value * mask for mask in head_masks(LOW)], axis=0)


def unstacked(value, rows):
    value = value.reshape(GROUP, rows, 64 * GROUP)
    return sum(value[i] * mask for i, mask in enumerate(head_masks(FULL)))


def mix_heads(q_ref, k_ref, v_ref, m_ref, qrows, krows, bias, pump):
    nq, nk = qrows.stop - qrows.start, krows.stop - krows.start
    for group in range(HEADS // GROUP):
        lanes = slice(256 * group, 256 * group + 256)
        query, keys, values = q_ref[qrows, lanes], k_ref[krows, lanes], v_ref[krows, lanes]
        scores = dot_t(stacked(query), keys).reshape(GROUP, nq, nk) * 0.125 + bias[None]
        exponent = jnp.exp(scores - jnp.max(scores, axis=-1, keepdims=True))
        probs = exponent / jnp.sum(exponent, axis=-1, keepdims=True)
        mixed = dot(probs.astype(LOW).reshape(GROUP * nq, nk), values)
        m_ref[qrows, lanes] = unstacked(mixed, nq).astype(LOW)
        pump()


def head_back(q_ref, k_ref, v_ref, dm_ref, dq_ref, dk_ref, dv_ref, qrows, krows, bias, group, base):
    nq, nk = qrows.stop - qrows.start, krows.stop - krows.start
    lanes = slice(256 * group, 256 * group + 256)
    query, keys, values = q_ref[qrows, lanes], k_ref[krows, lanes], v_ref[krows, lanes]
    grad = dm_ref[qrows, lanes]
    keys = stacked(keys)
    scores = dot_t(keys, query).reshape(GROUP, nk, nq) * 0.125 + bias[None]
    exponent = jnp.exp(scores - jnp.max(scores, axis=1, keepdims=True))
    probs = exponent / jnp.sum(exponent, axis=1, keepdims=True)
    dp = dot_t(stacked(values), grad).reshape(GROUP, nk, nq)
    ds = probs * (dp - jnp.sum(probs * dp, axis=1, keepdims=True))
    ds = ds.astype(LOW).reshape(GROUP * nk, nq)
    dv = unstacked(dot(probs.astype(LOW).reshape(GROUP * nk, nq), grad), nk)
    dk = unstacked(dot(ds, query), nk) * 0.125
    dq = t_dot(ds, keys) * 0.125
    qhere = slice(qrows.start - base, qrows.stop - base)
    khere = slice(krows.start - base, krows.stop - base)
    dq_ref[qhere, lanes] = dq.astype(LOW)
    dk_ref[khere, lanes] = dk.astype(LOW)
    dv_ref[khere, lanes] = dv.astype(LOW)


def row_of(ref, i):
    return ref[i : i + 1, :]


def attend(
    x_ref, low_ref, w_ref, vec_ref, layer, rows, parts, q_ref, k_ref, v_ref, m_ref, z_ref, out_ref, pump
):
    low = low_ref[rows, :]
    vec = [row_of(vec_ref, 5 * layer + i) for i in range(5)]

    def matrix(m):
        return w_ref[layer, m].reshape(D, D)

    q_ref[rows, :] = (dot(low, matrix(0)) + vec[0]).astype(LOW)
    k_ref[rows, :] = dot(low, matrix(1)).astype(LOW)
    pump()
    v_ref[rows, :] = (dot(low, matrix(2)) + vec[1]).astype(LOW)
    for qrows, krows, bias in parts:
        mix_heads(q_ref, k_ref, v_ref, m_ref, qrows, krows, bias, pump)
    pre = x_ref[rows, :] + (dot(m_ref[rows, :], matrix(3)) + vec[2])
    z_ref[rows, :] = pre
    unit, _ = norm_stats(pre)
    out_ref[rows, :] = unit * (1.0 + vec[3]) + vec[4]
    pump()


WORDS_EACH = WORDS_HERE // ITEMS_HERE
REGIONS_EACH = REGIONS_HERE // ITEMS_HERE


def length_bias(lengths, shape, axis):
    index = lax.broadcasted_iota(jnp.int32, shape, axis)
    item = item_of(index, WORDS_EACH)
    real = sum(jnp.where(item == i, lengths[i], 0) for i in range(ITEMS_HERE))
    return jnp.where(index - WORDS_EACH * item < real, 0.0, -1000000000.0)


STREAMS = (1, 0)
CHUNKS = ((1, WORDS_HERE, 80), (1, WORDS_HERE + 80, 64), (0, 0, WORDS_HERE))
SELF_ROWS = (pl.ds(0, WORDS_HERE), pl.ds(WORDS_HERE, REGIONS_HERE))


def ffn_kernel(
    x2, lang_cot, visn_cot, uw1, dw1, vec, ub, onelow, m1, up, down,
    lang_out, visn_out, d2, gu, gd, gv, gb, ax1, ax2, bx1, bx2,
    *scratch,
):
    at = Place()
    rep, z, core = at.rep, at.z, at.core
    scratch = list(scratch)

    def take(count):
        some, scratch[:] = scratch[:count], scratch[count:]
        return some

    many = len(CHUNKS)
    xg, bg, ht, gt, hd, mine, dz = [take(many) for _ in range(7)]
    stage, land = [[take(many) for _ in range(2)] for _ in range(2)]
    uw0, dw0, dst = take(3)
    psend, precv, osend, orecv, olocal, bsend, brecv = take(7)
    zsend, zrecv = take(2)
    at.enter(2)
    feed_weights = FeedWeights(at, up.at[0], down.at[0], dst, uw0, dw0, scratch)

    def weights_copy(index, s):
        kind = "ud"[index]
        return copy_to(
            feed_weights.own(kind), feed_weights.slot(kind, z),
            zsend.at[index, s], zrecv.at[index, z], at.column(s),
        )

    def weights_start():
        for index, kind in enumerate("ud"):
            at.others(lambda s: weights_copy(index, s).start())
            feed_weights.own_start(kind)

    def weights_arrive(index):
        kind = "ud"[index]

        def one(s):
            ref = feed_weights.slot(kind, s)
            copy_to(
                ref, ref, zsend.at[index, s], zrecv.at[index, s], at.column(s)
            ).wait_recv()
            feed_weights.pass_on(kind, s, ref)

        at.others(one)

    def up_weight(t):
        return uw1[...] if t else uw0[...].reshape(D, D)

    def down_weight(t):
        return (dw1 if t else dw0)[...]

    def plane_copy(which, i, hop, buffer):
        ref = buffer.at[at.peers[0] if hop == 2 else rep]
        there = at.peer(1) if hop == 2 else at.peer(hop)
        return copy_to(ref, ref, psend.at[which, i, hop], precv.at[which, i, hop], there)

    def plane_arrival(which, i, hop, buffer):
        ref = buffer.at[at.peers[hop]]
        return copy_to(ref, ref, psend.at[which, i, hop], precv.at[which, i, hop], at.peer(hop))

    def gather_start(which, i, buffer):
        for hop in range(2):
            plane_copy(which, i, hop, buffer).start()

    def gather_relay(which, i, buffer):
        plane_arrival(which, i, 0, buffer).wait_recv()
        plane_copy(which, i, 2, buffer).start()

    def gather_rest(which, i, buffer):
        for hop in (1, 2):
            plane_arrival(which, i, hop, buffer).wait_recv()

    def gather_sent(which, i, buffer):
        for hop in range(3):
            plane_copy(which, i, hop, buffer).wait_send()

    def first_copy(turn, i):
        return copy_to(
            stage[turn][i].at[pl.ds(0, 2)], land[turn][i].at[pl.ds(0, 2)],
            psend.at[2 * turn + 1, i, 0], precv.at[2 * turn + 1, i, 0], at.peer(0),
        )

    def second_copy(turn, i):
        return copy_to(
            stage[turn][i].at[2], land[turn][i].at[2],
            psend.at[2 * turn + 1, i, 1], precv.at[2 * turn + 1, i, 1], at.peer(1),
        )

    def return_first(turn, i):
        for hop, p in enumerate((0, 2)):
            stage[turn][i][hop] = mine[i][at.peers[p]].astype(LOW)
        first_copy(turn, i).start()

    def return_second(turn, i):
        first_copy(turn, i).wait_recv()
        passed = land[turn][i][1].astype(FULL)
        stage[turn][i][2] = (mine[i][at.peers[1]] + passed).astype(LOW)
        second_copy(turn, i).start()

    def summed(turn, i):
        second_copy(turn, i).wait_recv()
        passed = land[turn][i][0].astype(FULL) + land[turn][i][2].astype(FULL)
        return mine[i][rep] + passed

    def flat(ref):
        value = ref[...]
        return value.reshape(value.shape[0] * value.shape[1], value.shape[2])

    def up_and_down(i):
        t, _, count = CHUNKS[i]
        hidden = dot(flat(xg[i]), up_weight(t)) + ub[t : t + 1, :]
        below = 0.5 * (1.0 + lax.erf(hidden * (1.0 / math.sqrt(2.0))))
        active = (hidden * below).astype(LOW)
        gt[i][...] = active
        ht[i][...] = below + hidden * (
            jnp.exp(-0.5 * hidden * hidden) * (1.0 / math.sqrt(2.0 * math.pi))
        )
        mine[i][...] = dot(active, down_weight(t)).reshape(4, count, D)

    def rows_back(i):
        t, _, count = CHUNKS[i]
        low = (dot_t(flat(bg[i]), down_weight(t)) * ht[i][...]).astype(LOW)
        hd[i][...] = low
        mine[i][...] = dot_t(low, up_weight(t)).reshape(4, count, D)

    def weights_back(t):
        pieces = [i for i in range(many) if CHUNKS[i][0] == t]
        for k in range(3):
            lanes = slice(256 * k, 256 * k + 256)
            gd[t, :, lanes] = sum(t_dot(gt[i][...], flat(bg[i])[:, lanes]) for i in pieces).astype(LOW)
            gu[t, :, lanes] = sum(t_dot(flat(xg[i]), hd[i][:, lanes]) for i in pieces).astype(LOW)
        total = sum(column_sum(hd[i][...]) for i in pieces)
        row = lax.broadcasted_iota(jnp.int32, (Z, D), 0)
        gb[Z * t : Z * t + Z, :] = jnp.where(row == rep, jnp.broadcast_to(total, (Z, D)), 0.0)

    def chunk_rows(i):
        t, start, count = CHUNKS[i]
        here = start - WORDS_HERE * t
        return slice(start, start + count), slice(here, here + count)

    def norm_turn(i):
        t = CHUNKS[i][0]
        rows, here = chunk_rows(i)
        bias, gain, shift = [row_of(vec, 15 + 3 * t + k) for k in range(3)]
        pre = x2[rows, :] + (summed(0, i) + bias)
        unit, scale = norm_stats(pre)
        (lang_out, visn_out)[t][here, :] = unit * (1.0 + gain) + shift
        grad = (lang_cot, visn_cot)[t][here, :]
        dz[i][...] = norm_back(grad, unit, scale, gain)
        branch = dz[i][...].astype(LOW)
        bg[i][rep] = branch
        gather_start(2, i, bg[i])
        for k, value in enumerate((column_sum(branch), column_sum(grad * unit), column_sum(grad))):
            gv[3 * t + k : 3 * t + k + 1, :] += value

    landed, across = (ax1, ax2), (bx1, bx2)

    def operand_copy(source, k, p):
        return copy_to(
            source.at[SELF_ROWS[k]], landed[k].at[rep], osend.at[k, p], orecv.at[k, p], at.peer(p)
        )

    def operand_here(source, k):
        return pltpu.make_async_copy(source.at[SELF_ROWS[k]], landed[k].at[rep], olocal.at[k])

    def across_copy(k):
        return copy_to(landed[k], across[k], bsend.at[k], brecv.at[k], at.sibling)

    def operand_send(k, p):
        @pl.when(at.peers[p] != 3)
        def _():
            operand_copy(onelow, k, p).start()

        @pl.when(at.peers[p] == 3)
        def _():
            operand_copy(m1, k, p).start()

    def operands_start():
        for k in range(2):

            @pl.when(rep != 3)
            def _():
                operand_here(onelow, k).start()

            @pl.when(rep == 3)
            def _():
                operand_here(m1, k).start()

    def operands_across(k):
        operand_here(m1, k).wait()
        for p in range(3):
            copy_to(
                m1.at[SELF_ROWS[k]], landed[k].at[at.peers[p]],
                osend.at[k, p], orecv.at[k, p], at.peer(p),
            ).wait_recv()
        across_copy(k).start()

    gv[...] = jnp.zeros_like(gv)
    for i in range(many):
        xg[i][rep] = x2[chunk_rows(i)[0], :].astype(LOW)
        gather_start(0, i, xg[i])
    weights_start()
    operands_start()
    gather_relay(0, 0, xg[0])
    gather_rest(0, 0, xg[0])
    gather_relay(0, 1, xg[1])
    up_and_down(0)
    return_first(0, 0)
    gather_relay(0, 2, xg[2])
    gather_rest(0, 1, xg[1])
    weights_arrive(1)
    up_and_down(1)
    return_second(0, 0)
    return_first(0, 1)
    gather_rest(0, 2, xg[2])
    weights_arrive(0)
    feed_weights.collect()
    operand_send(0, 2)
    norm_turn(0)
    return_second(0, 1)
    feed_weights.finish()
    up_and_down(2)
    return_first(0, 2)
    gather_relay(2, 0, bg[0])
    operand_send(0, 0)
    operand_send(0, 1)
    norm_turn(1)
    return_second(0, 2)
    gather_rest(2, 0, bg[0])
    rows_back(0)
    return_first(1, 0)
    gather_relay(2, 1, bg[1])
    norm_turn(2)
    operand_send(1, 2)
    gather_rest(2, 1, bg[1])
    rows_back(1)
    return_second(1, 0)
    return_first(1, 1)
    operand_send(1, 0)
    gather_relay(2, 2, bg[2])
    gather_rest(2, 2, bg[2])
    rows_back(2)
    return_second(1, 1)
    return_first(1, 2)
    operand_send(1, 1)
    weights_back(1)
    return_second(1, 2)
    operands_across(0)
    operands_across(1)
    weights_back(0)
    for i in range(many):
        d2[chunk_rows(i)[0], :] = dz[i][...] + summed(1, i)
    for index in range(2):
        at.others(lambda s: weights_copy(index, s).wait_send())
    for k in range(2):
        across_copy(k).wait()
    for k in range(2):
        for p in range(3):
            operand_copy(m1, k, p).wait_send()
    for i in range(many):
        gather_sent(0, i, xg[i])
        gather_sent(2, i, bg[i])
        for turn in range(2):
            first_copy(turn, i).wait_send()
            second_copy(turn, i).wait_send()


def feed(x2, lang_cot, visn_cot, uw1, dw1, vec, ub, onelow, m1, up, down):
    dma = pltpu.SemaphoreType.DMA
    many = len(CHUNKS)

    def each(lead, width, dtype):
        return [pltpu.VMEM((*lead, chunk[2], width), dtype) for chunk in CHUNKS]

    def each_flat(width, dtype):
        return [pltpu.VMEM((4 * chunk[2], width), dtype) for chunk in CHUNKS]

    def rows_of_plane(count):
        return jax.ShapeDtypeStruct((4, count, D), LOW)

    return pl.pallas_call(
        ffn_kernel,
        out_shape=(
            jax.ShapeDtypeStruct((WORDS_HERE, D), FULL),
            jax.ShapeDtypeStruct((REGIONS_HERE, D), FULL),
            jax.ShapeDtypeStruct((ROWS, D), FULL),
            jax.ShapeDtypeStruct((2, D, D), LOW),
            jax.ShapeDtypeStruct((2, D, D), LOW),
            jax.ShapeDtypeStruct((8, D), FULL),
            jax.ShapeDtypeStruct((8, D), FULL),
            rows_of_plane(WORDS_HERE), rows_of_plane(REGIONS_HERE),
            rows_of_plane(WORDS_HERE), rows_of_plane(REGIONS_HERE),
        ),
        in_specs=[ONCHIP] * 7 + [HBM] * 4,
        out_specs=(ONCHIP,) * 7 + (HBM,) * 4,
        scratch_shapes=each((4,), D, LOW)
        + each((4,), D, LOW)
        + each_flat(D, FULL)
        + each_flat(D, LOW)
        + each_flat(D, LOW)
        + each((4,), D, FULL)
        + each((), D, FULL)
        + each((3,), D, LOW) * 2
        + each((3,), D, LOW) * 2
        + [
            pltpu.VMEM((8, SHARD, D), LOW),
            pltpu.VMEM((D, D), LOW),
            pltpu.VMEM((Z, SHARD, D), LOW),
            dma((4, many, 3)), dma((4, many, 3)),
            dma((2, 3)), dma((2, 3)), dma((2,)), dma((2,)), dma((2,)),
            dma((2, Z)), dma((2, Z)), *feed_sems(),
        ],
        compiler_params=pltpu.CompilerParams(
            collective_id=1, has_side_effects=True, vmem_limit_bytes=VMEM_BYTES
        ),
        cost_estimate=pl.CostEstimate(
            flops=6_400_000_000, bytes_accessed=12_000_000, transcendentals=1_400_000
        ),
        name="feed_forward",
    )(x2, lang_cot, visn_cot, uw1, dw1, vec, ub, onelow, m1, up, down)


def turned_bias(query_size, key_size, key_bias):
    shape = (key_size * ITEMS_HERE, query_size * ITEMS_HERE)
    key_item = item_of(lax.broadcasted_iota(jnp.int32, shape, 0), key_size)
    query_item = item_of(lax.broadcasted_iota(jnp.int32, shape, 1), query_size)
    bias = jnp.where(query_item == key_item, 0.0, -1e30)
    return bias if key_bias is None else bias + key_bias


LAYER_ROWS = (EVERY, LANG, VISN)
WIDE_UNITS = 5


def backward_kernel(
    d2, lengths, vec, w, q0, k0, v0, z0, q1, k1, v1, z1, gu, gd, gv, gb,
    xlow, m0, ax1, ax2, bx1, bx2,
    dx, oa, ou, od, os,
    wbuf, xa0, xa1, xa2, ys0, ys1, ys2, ya0, ya1, ya2, yb0, yb1, yb2,
    share, gou, gsu, god, gsd, dland, zwide, zlow, rwide, rlow, edge, wide, final, d1, dm, gs, s0, s1, s2, s3, s4, scol,
    wsem, asem, ysend, yrecv, yfsend, yfrecv,
    dsend, drecv, dlocal, wsend, wrecv, lsend, lrecv, rsend, rrecv, esend, erecv,
    gsend, grecv, glocal, ssend, srecv, osend, orecv, olocal, bsend, brecv, hsend, hrecv, hlocal,
):
    at = Place()
    rep, z, core, other = at.rep, at.z, at.core, at.other
    own_half = pl.ds(pl.multiple_of(PART * core, PART), PART)
    other_half = pl.ds(pl.multiple_of(PART * other, PART), PART)
    xa, xin = (xa0, xa1, xa2), (None, (ax1, bx1), (ax2, bx2))
    ys, ya, yb = (ys0, ys1, ys2), (ya0, ya1, ya2), (yb0, yb1, yb2)

    def load(layer):
        return pltpu.make_async_copy(w.at[layer], wbuf.at[layer], wsem.at[layer])

    def load_rows(layer, side):
        return pltpu.make_async_copy(
            xin[layer][side], xa[layer].at[side], asem.at[layer, side]
        )

    for layer in (1, 2, 0):
        load(layer).start()
    for layer in (1, 2):
        for side in range(2):
            load_rows(layer, side).start()
    at.enter(2)

    def operand_copy(source, p):
        return copy_to(source, xa0.at[0, rep], osend.at[p], orecv.at[p], at.peer(p))

    def operand_across():
        return copy_to(xa0.at[0], xa0.at[1], bsend, brecv, at.sibling)

    def operand_flow():
        for p in (2, 0, 1):

            @pl.when(at.peers[p] != 3)
            def _():
                operand_copy(xlow, p).start()

            @pl.when(at.peers[p] == 3)
            def _():
                operand_copy(m0, p).start()

        @pl.when(rep != 3)
        def _():
            pltpu.make_async_copy(xlow, xa0.at[0, rep], olocal).start()

        @pl.when(rep == 3)
        def _():
            pltpu.make_async_copy(m0, xa0.at[0, rep], olocal).start()

        yield
        pltpu.make_async_copy(m0, xa0.at[0, rep], olocal).wait()
        for p in range(3):
            copy_to(
                m0, xa0.at[0, at.peers[p]], osend.at[p], orecv.at[p], at.peer(p)
            ).wait_recv()
        operand_across().start()

    def y_copy(layer, p):
        return copy_to(
            ys[layer].at[at.peers[p]], ya[layer].at[rep],
            ysend.at[layer, p], yrecv.at[layer, p], at.peer(p),
        )

    def y_forward(layer, i):
        there = rep if i == 3 else at.peers[i]
        return copy_to(
            ya[layer].at[there, :, other_half], yb[layer].at[there],
            yfsend.at[layer, i], yfrecv.at[layer, i], at.sibling,
        )

    def y_arrival(layer, p):
        return copy_to(
            ys[layer].at[0], ya[layer].at[at.peers[p]],
            ysend.at[layer, p], yrecv.at[layer, p], at.peer(p),
        )

    def share_of(unit, s):
        if unit < 3:
            return share.at[unit, s]
        return gou.at[unit - 3, s] if unit < 5 else dland.at[unit - 5, s]

    def slot_of(unit, s):
        return zwide.at[unit, s] if unit < 5 else zlow.at[unit - 5, s]

    def stop_of(unit):
        return rwide.at[unit] if unit < 5 else rlow.at[unit - 5]

    def column_copy(unit, s, source):
        return copy_to(source, slot_of(unit, z), wsend.at[unit, s], wrecv.at[unit, z], at.column(s))

    def column_arrival(unit, s):
        ref = slot_of(unit, s)
        return copy_to(ref, ref, wsend.at[unit, s], wrecv.at[unit, s], at.column(s))

    def stop_copy(unit):
        far = lax.div(z, 3)
        return copy_to(
            share_of(unit, 2 - far), stop_of(unit),
            rsend.at[unit], rrecv.at[unit], at.column(1 + far),
        )

    def stop_arrival(unit):
        ref = stop_of(unit)
        return copy_to(ref, ref, rsend.at[unit], rrecv.at[unit], at.column(3 * (z - 1)))

    is_end = (z == 0) | (z == Z - 1)
    is_middle = (z > 0) & (z < Z - 1)
    straight = (z > 0, z == 0, z == Z - 1, z < Z - 1)

    def from_layer(s):
        return ((z != s) & is_end) | (is_middle & ((z == s + 1) | (z == s - 1)))

    def column_start(unit):
        @pl.when(is_end)
        def _():
            stop_copy(unit).start()

        for s in (3, 0, 1, 2):

            @pl.when(straight[s])
            def _():
                column_copy(unit, s, share_of(unit, s)).start()

        slot_of(unit, z)[...] = share_of(unit, z)[...]

    def column_stop(unit):
        @pl.when(is_middle)
        def _():
            stop_arrival(unit).wait_recv()
            ref = stop_of(unit)
            ref[...] = (ref[...].astype(FULL) + share_of(unit, 3 - z)[...].astype(FULL)).astype(LOW)
            column_copy(unit, 3 - z, ref).start()

    def column_sum_of(unit):
        for s in range(Z):

            @pl.when(from_layer(s))
            def _():
                column_arrival(unit, s).wait_recv()

        total = slot_of(unit, 0)[...].astype(FULL)
        for s in range(1, Z):
            total = total + slot_of(unit, s)[...].astype(FULL)
        return total.astype(LOW)

    for edge_z, s in ((1, 3), (2, 0)):

        @pl.when(z == edge_z)
        def _():
            for unit in range(7):
                ref = slot_of(unit, s)
                ref[...] = jnp.zeros_like(ref)

    def landing(unit, there):
        if unit < 3:
            return oa.at[unit, there]
        if unit < 5:
            return ou.at[unit - 3, :, pl.ds(pl.multiple_of(D * there, D), D)]
        return od.at[unit - 5, pl.ds(pl.multiple_of(SHARD * there, SHARD), SHARD)]

    def source_of(unit):
        return wide.at[unit] if unit < 5 else final.at[unit - 5]

    def share_copy(unit, i):
        there = at.peers[0] if i == 2 else rep
        return copy_to(
            landing(unit, there) if i == 2 else source_of(unit), landing(unit, there),
            gsend.at[unit, i], grecv.at[unit, i], at.peer(1) if i == 2 else at.peer(i),
        )

    def share_arrival(unit, i):
        ref = landing(unit, at.peers[i])
        return copy_to(ref, ref, gsend.at[unit, i], grecv.at[unit, i], at.peer(i))

    def share_out(unit):
        for i in range(2):
            share_copy(unit, i).start()
        pltpu.make_async_copy(source_of(unit), landing(unit, rep), glocal.at[unit]).start()
        yield
        share_arrival(unit, 0).wait_recv()
        share_copy(unit, 2).start()

    def edge_copy(unit):
        return copy_to(
            edge.at[unit, pl.ds(pl.multiple_of(SHARD * other, SHARD), SHARD)],
            wide.at[unit, :, own_half], esend.at[unit], erecv.at[unit], at.sibling,
        )

    def wide_end(unit):
        column_stop(unit)
        yield
        edge[unit] = column_sum_of(unit)
        edge_copy(unit).start()
        wide[unit, :, own_half] = edge[unit, pl.ds(pl.multiple_of(SHARD * core, SHARD), SHARD), :]
        yield
        edge_copy(unit).wait_recv()
        yield from share_out(unit)

    def half_of(kind, t, side):
        if kind:
            return gd.at[t, side]
        return gu.at[t, :, :, pl.ds(pl.multiple_of(PART * side, PART), PART)]

    def half_across(kind, t):
        return copy_to(
            half_of(kind, t, other), (gsu, gsd)[kind].at[t],
            hsend.at[kind, t], hrecv.at[kind, t], at.sibling,
        )

    def half_here(kind, t):
        return pltpu.make_async_copy(
            half_of(kind, t, core), (gou, god)[kind].at[t], hlocal.at[kind, t]
        )

    def half_start(kind, t):
        half_across(kind, t).start()
        half_here(kind, t).start()

    def half_sum(kind, t):
        half_across(kind, t).wait_recv()
        half_here(kind, t).wait()
        ours, theirs = ((gou, gsu), (god, gsd))[kind]
        ours[t] = (ours[t].astype(FULL) + theirs[t].astype(FULL)).astype(LOW)

    def up_flow(t):
        half_start(0, t)
        yield
        half_sum(0, t)
        column_start(3 + t)
        yield
        yield from wide_end(3 + t)

    def down_copy(t, p):
        return copy_to(
            god.at[t, at.peers[p]], dland.at[t, rep], dsend.at[t, p], drecv.at[t, p], at.peer(p)
        )

    def down_arrival(t, p):
        return copy_to(
            god.at[t, rep], dland.at[t, at.peers[p]], dsend.at[t, p], drecv.at[t, p], at.peer(p)
        )

    def down_here(t):
        return pltpu.make_async_copy(god.at[t, rep], dland.at[t, rep], dlocal.at[t])

    def down_flow(t):
        half_start(1, t)
        yield
        half_sum(1, t)
        for p in range(3):
            down_copy(t, p).start()
        down_here(t).start()
        yield
        for p in range(3):
            down_arrival(t, p).wait_recv()
        down_here(t).wait()
        column_start(5 + t)
        yield
        column_stop(5 + t)
        yield
        final[t] = column_sum_of(5 + t)
        yield from share_out(5 + t)

    def flat(value):
        return value.reshape(value.shape[0] * value.shape[1], value.shape[2])

    words, regions = pl.ds(0, WORDS_HERE), pl.ds(WORDS_HERE, REGIONS_HERE)
    pieces = (
        ((0, words), (1, regions), (2, regions), (3, pl.ds(0, ROWS))),
        ((0, regions), (1, words), (2, words)),
    )

    def piece_each(turn, act):
        for p in (2, 0, 1):
            for m, rows in pieces[turn]:

                @pl.when(at.peers[p] == m)
                def _():
                    act(
                        copy_to(
                            ys0.at[m, rows], ya0.at[rep, rows],
                            ysend.at[3 * turn, p], yrecv.at[3 * turn, p], at.peer(p),
                        )
                    )

    def piece_arrivals(p):
        for turn in range(2):
            for m, rows in pieces[turn]:

                @pl.when(rep == m)
                def _():
                    ref = ya0.at[at.peers[p], rows]
                    copy_to(
                        ref, ref, ysend.at[3 * turn, p], yrecv.at[3 * turn, p], at.peer(p)
                    ).wait_recv()

    def y_flow(layer):
        if layer == 0:
            piece_each(0, lambda copy: copy.start())
            yield
            piece_each(1, lambda copy: copy.start())
        else:
            for p in (2, 0, 1):
                y_copy(layer, p).start()
        ya[layer][rep] = ys[layer][rep]
        y_forward(layer, 3).start()
        yield
        for p in range(3):
            if layer == 0:
                piece_arrivals(p)
            else:
                y_arrival(layer, p).wait_recv()
            y_forward(layer, p).start()
        yield
        if layer > 0:
            for side in range(2):
                load_rows(layer, side).wait()
        else:
            operand_across().wait_recv()
        grad = t_dot(flat(xa[layer][0]), flat(ya[layer][:, :, own_half]))
        for i in range(4):
            y_forward(layer, i).wait_recv()
        grad = grad + t_dot(flat(xa[layer][1]), flat(yb[layer][...]))
        share[layer] = grad.astype(LOW).reshape(Z, 2 * SHARD, PART)
        column_start(layer)
        yield
        yield from wide_end(layer)

    small_ways = (at.sibling, at.peer(0), at.peer(1))
    small_from = (gs, s1, s2)
    small_land = (s0, s3, s4)

    def small_copy(i):
        return copy_to(small_from[i], small_land[i], ssend.at[i], srecv.at[i], small_ways[i])

    def small_line(s):
        return copy_to(scol.at[z], scol.at[z], ssend.at[3 + s], srecv.at[3 + z], at.column(s))

    def small_arrival(s):
        return copy_to(scol.at[s], scol.at[s], ssend.at[3 + s], srecv.at[3 + s], at.column(s))

    def small_flow():
        small_copy(0).start()
        yield
        small_copy(0).wait_recv()
        s1[...] = gs[...] + s0[...]
        small_copy(1).start()
        yield
        small_copy(1).wait_recv()
        s2[...] = s1[...] + s3[...]
        small_copy(2).start()
        yield
        small_copy(2).wait_recv()
        scol[z] = s2[...] + s4[...]
        for s in range(Z):

            @pl.when(s != z)
            def _():
                small_line(s).start()

        yield
        for s in range(Z):

            @pl.when(s != z)
            def _():
                small_arrival(s).wait_recv()

        os[...] = (scol[0] + scol[1]) + (scol[2] + scol[3])

    u0, u1, w0, w1, y0, y1, y2, sm, xm = range(9)
    flows = [
        up_flow(0), up_flow(1), down_flow(0), down_flow(1),
        y_flow(0), y_flow(1), y_flow(2), small_flow(), operand_flow(),
    ]

    def go(*names):
        for name in names:
            next(flows[name], None)

    gs[...] = jnp.zeros_like(gs)
    gs[15:21, :] = gv[0:6, :]
    gs[21:29, :] = gb[...]

    def attend_back(grad, layer, parts, q, k, v, zs, dx_ref, marks):
        rows = LAYER_ROWS[layer]
        vecs = [row_of(vec, 5 * layer + i) for i in range(5)]
        unit, scale = norm_stats(zs[rows, :])
        dz = norm_back(grad, unit, scale, vecs[3])
        branch = dz.astype(LOW)
        out = ys[layer]
        out[3] = branch
        for i, value in enumerate(
            (column_sum(branch), column_sum(grad * unit), column_sum(grad))
        ):
            gs[5 * layer + 2 + i : 5 * layer + 3 + i, :] = value
        dx_ref[rows, :] = dz
        load(layer).wait()
        dm[rows, :] = dot_t(branch, wbuf[layer, 3]).astype(LOW)
        go(*marks[0])
        for (qrows, krows, pair_mask), mark in zip(parts, marks[1]):
            for group in range(HEADS // GROUP):
                head_back(
                    q, k, v, dm, out.at[0], out.at[1], out.at[2],
                    qrows, krows, pair_mask, group, rows.start,
                )
            go(*mark)
        gs[5 * layer : 5 * layer + 1, :] = column_sum(out[0])
        gs[5 * layer + 1 : 5 * layer + 2, :] = column_sum(out[2])
        go(*marks[2])
        dx_ref[rows, :] += (
            dot_t(out[0], wbuf[layer, 0])
            + (dot_t(out[1], wbuf[layer, 1]) + dot_t(out[2], wbuf[layer, 2]))
        )
        go(*marks[3])

    word_bias = length_bias(lengths, (WORDS_HERE, 1), 0)
    go(w1, u1, w0, u0, xm)
    attend_back(
        d2[LANG, :], 1,
        [(LANG, LANG, turned_bias(WORDS_EACH, WORDS_EACH, word_bias))], q1, k1, v1, z1, d1,
        ([w1, u1, w0, u0], [[y1]], [], [u1]),
    )
    attend_back(
        d2[VISN, :], 2,
        [(VISN, VISN, turned_bias(REGIONS_EACH, REGIONS_EACH, None))], q1, k1, v1, z1, d1,
        ([u0], [[y2]], [w1, w0], [u1, y1]),
    )
    attend_back(
        d1[...], 0,
        [
            (LANG, VISN, turned_bias(WORDS_EACH, REGIONS_EACH, None)),
            (VISN, LANG, turned_bias(REGIONS_EACH, WORDS_EACH, word_bias)),
        ],
        q0, k0, v0, z0, dx,
        ([u1, u0, y1], [[y0, u0, w1, w0, y1, y2, xm], [y0]], [sm], [u1, y2, u0]),
    )
    go(sm, y0, y2, y0, sm, w1, w0, y1, y0, y1, sm, y2, w1, w0, y2, y1, sm, y0, y2, y0, y0)
    for flow in range(9):
        for _ in range(9):
            go(flow)

    for unit in range(7):
        pltpu.make_async_copy(source_of(unit), landing(unit, rep), glocal.at[unit]).wait()
        for i in (1, 2):
            share_arrival(unit, i).wait_recv()
        for i in range(3):
            share_copy(unit, i).wait_send()
        for s in range(Z):

            @pl.when(straight[s])
            def _():
                column_copy(unit, s, share_of(unit, s)).wait_send()

        @pl.when(is_end)
        def _():
            stop_copy(unit).wait_send()

        @pl.when(is_middle)
        def _():
            column_copy(unit, 3 - z, stop_of(unit)).wait_send()

    for p in range(3):
        operand_copy(m0, p).wait_send()
    operand_across().wait_send()
    for t in range(2):
        for kind in range(2):
            half_across(kind, t).wait_send()
    for turn in range(2):
        piece_each(turn, lambda copy: copy.wait_send())
    for layer in range(3):
        if layer > 0:
            for p in range(3):
                y_copy(layer, p).wait_send()
        for i in range(4):
            y_forward(layer, i).wait_send()
    for t in range(2):
        for p in range(3):
            down_copy(t, p).wait_send()
    for unit in range(WIDE_UNITS):
        edge_copy(unit).wait_send()
    for i in range(3):
        small_copy(i).wait_send()
    for s in range(Z):

        @pl.when(s != z)
        def _():
            small_line(s).wait_send()


def backward(d2, lengths, vec, w, kept, gu, gd, gv, gb, rows):
    dma = pltpu.SemaphoreType.DMA
    sizes = [layer_rows.stop - layer_rows.start for layer_rows in LAYER_ROWS]

    def each(lead, width):
        return [pltpu.VMEM((*lead, n, width), LOW) for n in sizes]

    return pl.pallas_call(
        backward_kernel,
        out_shape=(
            jax.ShapeDtypeStruct((ROWS, D), FULL),
            jax.ShapeDtypeStruct((3, 4, SHARD, D), LOW),
            jax.ShapeDtypeStruct((2, SHARD, FF), LOW),
            jax.ShapeDtypeStruct((2, PART, D), LOW),
            jax.ShapeDtypeStruct((32, D), FULL),
        ),
        in_specs=[ONCHIP, pl.BlockSpec(memory_space=pltpu.SMEM), ONCHIP, HBM]
        + [ONCHIP] * 8
        + [HBM, HBM, ONCHIP, ONCHIP]
        + [HBM] * 6,
        out_specs=(ONCHIP, HBM, HBM, HBM, ONCHIP),
        scratch_shapes=[
            pltpu.VMEM((3, 4, D, D), LOW),
            *each((2, 4), D), *each((4,), D), *each((4,), D), *each((4,), PART),
            pltpu.VMEM((3, Z, 2 * SHARD, PART), LOW),
            pltpu.VMEM((2, Z, 2 * SHARD, PART), LOW),
            pltpu.VMEM((2, Z, 2 * SHARD, PART), LOW),
            pltpu.VMEM((2, 4, SHARD, D), LOW),
            pltpu.VMEM((2, 4, SHARD, D), LOW),
            pltpu.VMEM((2, Z, SHARD, D), LOW),
            pltpu.VMEM((WIDE_UNITS, Z, 2 * SHARD, PART), LOW),
            pltpu.VMEM((2, Z, SHARD, D), LOW),
            pltpu.VMEM((WIDE_UNITS, 2 * SHARD, PART), LOW),
            pltpu.VMEM((2, SHARD, D), LOW),
            pltpu.VMEM((WIDE_UNITS, 2 * SHARD, PART), LOW),
            pltpu.VMEM((WIDE_UNITS, SHARD, D), LOW),
            pltpu.VMEM((2, SHARD, D), LOW),
            pltpu.VMEM((ROWS, D), FULL),
            pltpu.VMEM((ROWS, D), LOW),
            *[pltpu.VMEM((32, D), FULL)] * 6,
            pltpu.VMEM((Z, 32, D), FULL),
            dma((3,)), dma((3, 2)),
            dma((4, 3)), dma((4, 3)), dma((3, 4)), dma((3, 4)),
            dma((2, 3)), dma((2, 3)), dma((2,)),
            dma((7, Z)), dma((7, Z)), dma((2, Z)), dma((2, Z)),
            dma((7,)), dma((7,)),
            dma((WIDE_UNITS,)), dma((WIDE_UNITS,)),
            dma((7, 3)), dma((7, 3)), dma((7,)),
            dma((3 + Z,)), dma((3 + Z,)),
            dma((3,)), dma((3,)), dma, dma, dma, dma((2, 2)), dma((2, 2)), dma((2, 2)),
        ],
        compiler_params=pltpu.CompilerParams(
            collective_id=2, has_side_effects=True, vmem_limit_bytes=VMEM_BYTES
        ),
        cost_estimate=pl.CostEstimate(
            flops=4_400_000_000, bytes_accessed=30_000_000, transcendentals=500_000
        ),
        name="attention_backward",
    )(d2, lengths, vec, w, *kept, gu, gd, gv, gb, *rows)


def finish_kernel(
    oa, ou, od, os, dx, lo, vo,
    wa, wu, wd, va, vf, vu, lang_grad, visn_grad, lang_out, visn_out,
):
    wa[...] = oa[...].astype(FULL)
    wu[...] = ou[...].astype(FULL)
    wd[...] = od[...].astype(FULL)

    @pl.when(pl.program_id(0) == 0)
    def _():
        lang_grad[...] = dx[LANG, :]
        visn_grad[...] = dx[VISN, :]
        lang_out[...] = lo[...]
        visn_out[...] = vo[...]
        spot = lax.axis_index("fsdp")
        z = lax.div(spot, 2)
        own = jnp.zeros((32, SHARD), FULL)
        for d in range(8):
            own = jnp.where(spot == d, os[:, SHARD * d : SHARD * d + SHARD], own)
        for i in range(5):
            for layer in range(3):
                va[i, layer : layer + 1, :] = own[5 * layer + i : 5 * layer + i + 1, :]
        for i in range(3):
            for t in range(2):
                vf[i, t : t + 1, :] = own[15 + 3 * t + i : 16 + 3 * t + i, :]
        for t in range(2):
            row = os[pl.ds(21 + 4 * t + z, 1), :]
            vu[t : t + 1, :] = jnp.where(spot == 2 * z, row[:, :PART], row[:, PART:])


def finish(oa, ou, od, os, dx, lo, vo):
    def whole(shape):
        return pl.BlockSpec(shape, lambda i: (0,) * len(shape))

    parts = [
        pl.BlockSpec((3, 1, SHARD, D), lambda i: (0, i, 0, 0)),
        pl.BlockSpec((2, SHARD, D), lambda i: (0, 0, i)),
        pl.BlockSpec((2, SHARD, D), lambda i: (0, i, 0)),
    ]
    words, regions = (WORDS_HERE, D), (REGIONS_HERE, D)
    smalls = [(5, 3, SHARD), (3, 2, SHARD), (2, PART)]
    singles = [*smalls, words, regions, words, regions]
    return pl.pallas_call(
        finish_kernel,
        grid=(4,),
        out_shape=tuple(jax.ShapeDtypeStruct(ref.shape, FULL) for ref in (oa, ou, od))
        + tuple(jax.ShapeDtypeStruct(shape, FULL) for shape in singles),
        in_specs=[*parts, whole((32, D)), whole((ROWS, D)), whole(words), whole(regions)],
        out_specs=(*parts, *[whole(shape) for shape in singles]),
        compiler_params=pltpu.CompilerParams(vmem_limit_bytes=VMEM_BYTES),
        cost_estimate=pl.CostEstimate(flops=0, bytes_accessed=15_000_000, transcendentals=0),
        name="widen_outputs",
    )(oa, ou, od, os, dx, lo, vo)


def fast_body(
    language, vision, lengths, attn_weights, attn_vectors, ffn_up, ffn_up_bias, ffn_down, ffn_vectors,
    language_cot, vision_cot,
):
    wide = ((0, 0), (0, PART - SHARD))
    vectors = [attn_vectors[i] for i in range(3)] + [ffn_vectors[i] for i in range(2)]
    small = jnp.concatenate([jnp.pad(piece, wide) for piece in vectors] + [ffn_up_bias])
    small = jnp.pad(small, ((0, 9), (0, 0)))
    wf, uf, df, vec, ub, xlow, onelow, two, *kept = gather(
        attn_weights, ffn_up, ffn_down, small, language, vision, lengths
    )
    q0, k0, v0, m0, z0, q1, k1, v1, m1, z1 = kept
    lo, vo, d2, gu, gd, gv, gb, ax1, ax2, bx1, bx2 = feed(
        two, language_cot, vision_cot, uf.reshape(D, D), df, vec, ub, onelow, m1,
        ffn_up, ffn_down,
    )
    dx, oa, ou, od, os = backward(
        d2, lengths, vec, wf.reshape(3, 4, D, D), (q0, k0, v0, z0, q1, k1, v1, z1),
        gu.reshape(2, Z, 2 * SHARD, D), gd.reshape(2, 2, 4, SHARD, D), gv, gb,
        (xlow, m0, ax1, ax2, bx1, bx2),
    )
    wa, wu, wd, va, vf, vu, lang_grad, visn_grad, lang_out, visn_out = finish(
        oa, ou, od, os, dx, lo, vo
    )
    va, vf = va.transpose(1, 0, 2), vf.transpose(1, 0, 2)
    return (lang_out, visn_out, lang_grad, visn_grad, wa, va, wu, vu, wd, vf)


def layer_norm(values, gain, shift):
    mean = jnp.mean(values, axis=-1, keepdims=True)
    centred = values - mean
    spread = jnp.mean(centred * centred, axis=-1, keepdims=True)
    return centred * jax.lax.rsqrt(spread + 1e-06) * (1.0 + gain) + shift


def gelu_exact(values):
    return jax.nn.gelu(values, approximate=False)


def project(inputs, matrix):
    return jnp.einsum("isd,de->ise", inputs, matrix, preferred_element_type=jnp.float32)


def project_back(grads, matrix):
    return jnp.einsum("ise,de->isd", grads, matrix, preferred_element_type=jnp.float32)


def outer_sum(inputs, grads):
    return jnp.einsum("isd,ise->de", inputs, grads, preferred_element_type=jnp.float32)


def row_total(grads):
    return jnp.sum(grads.astype(jnp.float32), axis=(0, 1))


def gather_attn(attn_weights, attn_vectors, layer_index):
    return (
        lax.all_gather(attn_weights[layer_index], "fsdp", axis=1, tiled=True),
        lax.all_gather(attn_vectors[layer_index], "fsdp", axis=1, tiled=True),
    )


def regather_attn(attn_weights, attn_vectors, layer_index):
    return (
        lax.all_gather(attn_weights[layer_index], "fsdp", axis=1, tiled=True),
        lax.all_gather(attn_vectors[layer_index], "fsdp", axis=1, tiled=True),
    )


def gather_ffn(ffn_up, ffn_up_bias, ffn_down, ffn_vectors, layer_index):
    return (
        lax.all_gather(ffn_up[layer_index], "fsdp", axis=0, tiled=True),
        lax.all_gather(ffn_up_bias[layer_index], "fsdp", axis=0, tiled=True),
        lax.all_gather(ffn_down[layer_index], "fsdp", axis=0, tiled=True),
        lax.all_gather(ffn_vectors[layer_index], "fsdp", axis=1, tiled=True),
    )


def regather_ffn(ffn_up, ffn_up_bias, ffn_down, ffn_vectors, layer_index):
    return (
        lax.all_gather(ffn_up[layer_index], "fsdp", axis=0, tiled=True),
        lax.all_gather(ffn_up_bias[layer_index], "fsdp", axis=0, tiled=True),
        lax.all_gather(ffn_down[layer_index], "fsdp", axis=0, tiled=True),
        lax.all_gather(ffn_vectors[layer_index], "fsdp", axis=1, tiled=True),
    )


def settle_attn(grad_weights, grad_vector):
    shards = (
        lax.psum_scatter(grad_weights, "fsdp", scatter_dimension=1, tiled=True),
        lax.psum_scatter(grad_vector, "fsdp", scatter_dimension=1, tiled=True),
    )
    quarter = lax.psum_scatter(
        shards[0].astype(jnp.bfloat16), "rep", scatter_dimension=2, tiled=True
    ).astype(jnp.float32)
    vector_sum = lax.psum(shards[1], "rep")
    whole = lax.all_gather(quarter.astype(jnp.bfloat16), "rep", axis=2, tiled=True).astype(
        quarter.dtype
    )
    return (whole, vector_sum)


def settle_ffn(grad_up, grad_up_bias, grad_down, grad_vector):
    shards = (
        lax.psum_scatter(grad_up, "fsdp", scatter_dimension=0, tiled=True),
        lax.psum_scatter(grad_up_bias, "fsdp", scatter_dimension=0, tiled=True),
        lax.psum_scatter(grad_down, "fsdp", scatter_dimension=0, tiled=True),
        lax.psum_scatter(grad_vector, "fsdp", scatter_dimension=1, tiled=True),
    )
    quarters = (
        lax.psum_scatter(
            shards[0].astype(jnp.bfloat16), "rep", scatter_dimension=1, tiled=True
        ).astype(jnp.float32),
        lax.psum_scatter(
            shards[2].astype(jnp.bfloat16), "rep", scatter_dimension=1, tiled=True
        ).astype(jnp.float32),
    )
    smalls = lax.psum((shards[1], shards[3]), "rep")
    wholes = (
        lax.all_gather(quarters[0].astype(jnp.bfloat16), "rep", axis=1, tiled=True).astype(
            jnp.float32
        ),
        lax.all_gather(quarters[1].astype(jnp.bfloat16), "rep", axis=1, tiled=True).astype(
            jnp.float32
        ),
    )
    return (wholes[0], smalls[0], wholes[1], smalls[1])


def attend_forward(residual, query_low, key_low, weights, vector, key_bias):
    item_count, query_len, model_width = residual.shape
    key_len = key_low.shape[1]
    head_size = model_width // HEADS
    vector = vector.astype(jnp.float32)
    queries = (project(query_low, weights[0]) + vector[0]).astype(jnp.bfloat16)
    key_heads = project(key_low, weights[1]).astype(jnp.bfloat16)
    values = (project(key_low, weights[2]) + vector[1]).astype(jnp.bfloat16)
    queries = queries.reshape(item_count, query_len, HEADS, head_size)
    key_heads = key_heads.reshape(item_count, key_len, HEADS, head_size)
    values = values.reshape(item_count, key_len, HEADS, head_size)
    scores = jnp.einsum(
        "iqhd,ikhd->ihqk", queries, key_heads, preferred_element_type=jnp.float32
    ) / math.sqrt(head_size)
    scores = scores + key_bias[:, None, None, :]
    highest = jnp.max(scores, axis=-1, keepdims=True)
    exponent = jnp.exp(scores - highest)
    attn_probs = exponent / jnp.sum(exponent, axis=-1, keepdims=True)
    mixed_heads = jnp.einsum(
        "ihqk,ikhd->iqhd",
        attn_probs.astype(jnp.bfloat16),
        values,
        preferred_element_type=jnp.float32,
    )
    mixed_heads = mixed_heads.astype(jnp.bfloat16).reshape(item_count, query_len, model_width)
    pre_norm = residual + (project(mixed_heads, weights[3]) + vector[2])
    normed = layer_norm(pre_norm, vector[3], vector[4])
    return (normed, (queries, key_heads, values, attn_probs, mixed_heads, pre_norm))


def attend_backward(grad_out, query_low, key_low, weights, vector, kept):
    queries, key_heads, values, attn_probs, mixed_heads, pre_norm = kept
    item_count, query_len, head_count, head_size = queries.shape
    key_len = key_heads.shape[1]
    model_width = head_count * head_size
    vector = vector.astype(jnp.float32)
    _, pull_norm = jax.vjp(layer_norm, pre_norm, vector[3], vector[4])
    grad_pre, grad_gain, grad_shift = pull_norm(grad_out)
    grad_branch = grad_pre.astype(jnp.bfloat16)
    grad_out_weight = outer_sum(mixed_heads, grad_branch)
    grad_mixed = project_back(grad_branch, weights[3]).astype(jnp.bfloat16)
    grad_mixed = grad_mixed.reshape(item_count, query_len, head_count, head_size)
    grad_probs = jnp.einsum(
        "iqhd,ikhd->ihqk", grad_mixed, values, preferred_element_type=jnp.float32
    )
    grad_values = jnp.einsum(
        "ihqk,iqhd->ikhd",
        attn_probs.astype(jnp.bfloat16),
        grad_mixed,
        preferred_element_type=jnp.float32,
    ).astype(jnp.bfloat16)
    grad_scores = attn_probs * (
        grad_probs - jnp.sum(attn_probs * grad_probs, axis=-1, keepdims=True)
    )
    grad_scores = grad_scores.astype(jnp.bfloat16)
    inverse = 1.0 / math.sqrt(head_size)
    grad_queries = (
        jnp.einsum("ihqk,ikhd->iqhd", grad_scores, key_heads, preferred_element_type=jnp.float32)
        * inverse
    )
    grad_queries = grad_queries.astype(jnp.bfloat16).reshape(item_count, query_len, model_width)
    grad_keys = (
        jnp.einsum("ihqk,iqhd->ikhd", grad_scores, queries, preferred_element_type=jnp.float32)
        * inverse
    )
    grad_keys = grad_keys.astype(jnp.bfloat16).reshape(item_count, key_len, model_width)
    grad_values = grad_values.reshape(item_count, key_len, model_width)
    grad_weights = jnp.stack(
        [
            outer_sum(query_low, grad_queries),
            outer_sum(key_low, grad_keys),
            outer_sum(key_low, grad_values),
            grad_out_weight,
        ]
    )
    grad_vector = jnp.stack(
        [
            row_total(grad_queries),
            row_total(grad_values),
            row_total(grad_branch),
            grad_gain,
            grad_shift,
        ]
    )
    grad_query_low = project_back(grad_queries, weights[0])
    grad_key_low = project_back(grad_keys, weights[1]) + project_back(grad_values, weights[2])
    return (grad_pre, grad_query_low, grad_key_low, grad_weights, grad_vector)


def feed_forward(residual, up_weight, up_bias, down_weight, vector):
    vector = vector.astype(jnp.float32)
    residual_low = residual.astype(jnp.bfloat16)
    hidden = project(residual_low, up_weight) + up_bias.astype(jnp.float32)
    active = gelu_exact(hidden).astype(jnp.bfloat16)
    pre_norm = residual + (project(active, down_weight) + vector[0])
    normed = layer_norm(pre_norm, vector[1], vector[2])
    return (normed, (residual_low, hidden, active, pre_norm))


def feed_backward(grad_out, up_weight, down_weight, vector, kept):
    residual_low, hidden, active, pre_norm = kept
    vector = vector.astype(jnp.float32)
    _, pull_norm = jax.vjp(layer_norm, pre_norm, vector[1], vector[2])
    grad_pre, grad_gain, grad_shift = pull_norm(grad_out)
    grad_branch = grad_pre.astype(jnp.bfloat16)
    grad_down = outer_sum(active, grad_branch)
    grad_active = project_back(grad_branch, down_weight)
    _, pull_gate = jax.vjp(gelu_exact, hidden)
    grad_hidden = pull_gate(grad_active)[0].astype(jnp.bfloat16)
    grad_up = outer_sum(residual_low, grad_hidden)
    grad_up_bias = row_total(grad_hidden)
    grad_residual = grad_pre + project_back(grad_hidden, up_weight)
    grad_vector = jnp.stack([row_total(grad_branch), grad_gain, grad_shift])
    return (grad_residual, grad_up, grad_up_bias, grad_down, grad_vector)


def body(
    language,
    vision,
    lengths,
    attn_weights,
    attn_vectors,
    ffn_up,
    ffn_up_bias,
    ffn_down,
    ffn_vectors,
    language_cot,
    vision_cot,
):
    item_count = lengths.shape[0]
    model_width = language.shape[1]
    word_slots = language.shape[0] // item_count
    region_slots = vision.shape[0] // item_count
    lang_rows = language.reshape(item_count, word_slots, model_width)
    visn_rows = vision.reshape(item_count, region_slots, model_width)
    word_bias = jnp.where(
        jnp.arange(word_slots)[None, :] < lengths[:, None], 0.0, -1000000000.0
    ).astype(jnp.float32)
    region_bias = jnp.zeros((item_count, region_slots), jnp.float32)
    cross_weights, cross_vector = gather_attn(attn_weights, attn_vectors, 0)
    lang_low = lang_rows.astype(jnp.bfloat16)
    visn_low = visn_rows.astype(jnp.bfloat16)
    lang_one = attend_forward(
        lang_rows, lang_low, visn_low, cross_weights, cross_vector, region_bias
    )[0]
    visn_one = attend_forward(
        visn_rows, visn_low, lang_low, cross_weights, cross_vector, word_bias
    )[0]
    lang_self = gather_attn(attn_weights, attn_vectors, 1)
    lang_one_low = lang_one.astype(jnp.bfloat16)
    lang_two, lang_self_kept = attend_forward(
        lang_one, lang_one_low, lang_one_low, lang_self[0], lang_self[1], word_bias
    )
    visn_self = gather_attn(attn_weights, attn_vectors, 2)
    visn_one_low = visn_one.astype(jnp.bfloat16)
    visn_two, visn_self_kept = attend_forward(
        visn_one, visn_one_low, visn_one_low, visn_self[0], visn_self[1], region_bias
    )
    lang_ffn = gather_ffn(ffn_up, ffn_up_bias, ffn_down, ffn_vectors, 0)
    lang_three, lang_ffn_kept = feed_forward(
        lang_two, lang_ffn[0], lang_ffn[1], lang_ffn[2], lang_ffn[3]
    )
    visn_ffn = gather_ffn(ffn_up, ffn_up_bias, ffn_down, ffn_vectors, 1)
    visn_three, visn_ffn_kept = feed_forward(
        visn_two, visn_ffn[0], visn_ffn[1], visn_ffn[2], visn_ffn[3]
    )
    visn_ffn_back = regather_ffn(ffn_up, ffn_up_bias, ffn_down, ffn_vectors, 1)
    visn_back = feed_backward(
        vision_cot.reshape(item_count, region_slots, model_width),
        visn_ffn_back[0],
        visn_ffn_back[2],
        visn_ffn_back[3],
        visn_ffn_kept,
    )
    visn_ffn_grads = settle_ffn(visn_back[1], visn_back[2], visn_back[3], visn_back[4])
    lang_ffn_back = regather_ffn(ffn_up, ffn_up_bias, ffn_down, ffn_vectors, 0)
    lang_back = feed_backward(
        language_cot.reshape(item_count, word_slots, model_width),
        lang_ffn_back[0],
        lang_ffn_back[2],
        lang_ffn_back[3],
        lang_ffn_kept,
    )
    lang_ffn_grads = settle_ffn(lang_back[1], lang_back[2], lang_back[3], lang_back[4])
    visn_self_back = regather_attn(attn_weights, attn_vectors, 2)
    visn_attn = attend_backward(
        visn_back[0],
        visn_one_low,
        visn_one_low,
        visn_self_back[0],
        visn_self_back[1],
        visn_self_kept,
    )
    visn_self_grads = settle_attn(visn_attn[3], visn_attn[4])
    grad_visn_one = visn_attn[0] + visn_attn[1] + visn_attn[2]
    lang_self_back = regather_attn(attn_weights, attn_vectors, 1)
    lang_attn = attend_backward(
        lang_back[0],
        lang_one_low,
        lang_one_low,
        lang_self_back[0],
        lang_self_back[1],
        lang_self_kept,
    )
    lang_self_grads = settle_attn(lang_attn[3], lang_attn[4])
    grad_lang_one = lang_attn[0] + lang_attn[1] + lang_attn[2]
    cross_back = regather_attn(attn_weights, attn_vectors, 0)
    lang_cross_kept = attend_forward(
        lang_rows, lang_low, visn_low, cross_back[0], cross_back[1], region_bias
    )[1]
    visn_cross_kept = attend_forward(
        visn_rows, visn_low, lang_low, cross_back[0], cross_back[1], word_bias
    )[1]
    lang_cross = attend_backward(
        grad_lang_one, lang_low, visn_low, cross_back[0], cross_back[1], lang_cross_kept
    )
    visn_cross = attend_backward(
        grad_visn_one, visn_low, lang_low, cross_back[0], cross_back[1], visn_cross_kept
    )
    cross_grads = settle_attn(lang_cross[3] + visn_cross[3], lang_cross[4] + visn_cross[4])
    grad_language = lang_cross[0] + lang_cross[1] + visn_cross[2]
    grad_vision = visn_cross[0] + visn_cross[1] + lang_cross[2]
    return (
        lang_three.reshape(item_count * word_slots, model_width),
        visn_three.reshape(item_count * region_slots, model_width),
        grad_language.reshape(item_count * word_slots, model_width),
        grad_vision.reshape(item_count * region_slots, model_width),
        jnp.stack([cross_grads[0], lang_self_grads[0], visn_self_grads[0]]),
        jnp.stack([cross_grads[1], lang_self_grads[1], visn_self_grads[1]]),
        jnp.stack([lang_ffn_grads[0], visn_ffn_grads[0]]),
        jnp.stack([lang_ffn_grads[1], visn_ffn_grads[1]]),
        jnp.stack([lang_ffn_grads[2], visn_ffn_grads[2]]),
        jnp.stack([lang_ffn_grads[3], visn_ffn_grads[3]]),
    )


def solution(mesh):
    shape = dict(mesh.shape)
    fast = shape["rep"] == 4 and shape["fsdp"] == 8
    return jax.shard_map(
        fast_body if fast else body,
        mesh=mesh,
        in_specs=(
            P(("rep", "fsdp"), None),
            P(("rep", "fsdp"), None),
            P(("rep", "fsdp")),
            P(None, None, "fsdp", None),
            P(None, None, "fsdp"),
            P(None, "fsdp", None),
            P(None, "fsdp"),
            P(None, "fsdp", None),
            P(None, None, "fsdp"),
            P(("rep", "fsdp"), None),
            P(("rep", "fsdp"), None),
        ),
        out_specs=(
            P(("rep", "fsdp"), None),
            P(("rep", "fsdp"), None),
            P(("rep", "fsdp"), None),
            P(("rep", "fsdp"), None),
            P(None, None, "fsdp", None),
            P(None, None, "fsdp"),
            P(None, "fsdp", None),
            P(None, "fsdp"),
            P(None, "fsdp", None),
            P(None, None, "fsdp"),
        ),
        check_vma=False,
    )
```

```python
import functools
import math

import jax
import jax.numpy as jnp
from jax import lax
from jax.experimental import pallas as pl
from jax.experimental.pallas import tpu as pltpu
from jax.sharding import PartitionSpec as P

HEADS = 12
LOW = jnp.bfloat16
FULL = jnp.float32
VMEM_BYTES = 58 * 1024 * 1024
HBM = pl.BlockSpec(memory_space=pl.ANY)
ONCHIP = pl.BlockSpec(memory_space=pltpu.VMEM)


D = 768
WORDS_HERE = 80
REGIONS_HERE = 144
ROWS = WORDS_HERE + REGIONS_HERE
LANG = slice(0, WORDS_HERE)
VISN = slice(WORDS_HERE, ROWS)
EVERY = slice(0, ROWS)
ITEMS_HERE = 4
FF = 3072
PART = 384
SHARD = 96
Z = 4


def copy_to(src, dst, send, recv, device):
    return pltpu.make_async_remote_copy(
        src_ref=src,
        dst_ref=dst,
        send_sem=send,
        recv_sem=recv,
        device_id=device,
        device_id_type=pl.DeviceIdType.MESH,
    )


class Place:
    def __init__(self):
        rep, spot = lax.axis_index("rep"), lax.axis_index("fsdp")
        z = lax.div(spot, 2)
        core = spot - 2 * z
        y = lax.div(rep, 2)
        x = rep - 2 * y
        self.rep, self.spot, self.z, self.core, self.other = rep, spot, z, core, 1 - core
        along_x, along_y = (1 - x) + 2 * y, x + 2 * (1 - y)
        turn = core * (along_y - along_x)
        self.peers = [along_x + turn, along_y - turn, (1 - x) + 2 * (1 - y)]
        self.sibling = (rep, 2 * z + (1 - core))

    def peer(self, p):
        return (self.peers[p], self.spot)

    def above(self):
        return (self.rep, self.spot + 2)

    def below(self):
        return (self.rep, self.spot - 2)

    def column(self, s):
        return (self.rep, 2 * s + self.core)

    def enter(self, line):
        barrier = pltpu.get_barrier_semaphore()

        def greet(device):
            pl.semaphore_signal(
                barrier, inc=1, device_id=device, device_id_type=pl.DeviceIdType.MESH
            )

        for p in range(3):
            greet(self.peer(p))
        greet(self.sibling)
        number = 4
        if line == 1:

            @pl.when(self.z > 0)
            def _():
                greet(self.below())

            @pl.when(self.z < Z - 1)
            def _():
                greet(self.above())

            number = 4 + jnp.minimum(self.z, 1) + jnp.minimum(Z - 1 - self.z, 1)
        if line == 2:
            self.others(lambda s: greet(self.column(s)))
            number = 4 + Z - 1
        pl.semaphore_wait(barrier, number)

    def others(self, act):
        for s in (0, 3, 1, 2):

            @pl.when(s != self.z)
            def _():
                act(s)


class Chain:
    def __init__(self, at, units, slot, own, send, recv):
        self.at, self.units, self.slot, self.own = at, units, slot, own
        self.send, self.recv = send, recv

    def copy(self, index, s, source, upward):
        return copy_to(
            source, self.slot(self.units[index], s),
            self.send.at[index, s, 0 if upward else 1], self.recv.at[index, s],
            self.at.above() if upward else self.at.below(),
        )

    def send_step(self, index, k):
        z, unit = self.at.z, self.units[index]

        @pl.when((z - k >= 0) & (z < Z - 1))
        def _():
            source = self.own(unit) if k == 0 else self.slot(unit, z - k)
            self.copy(index, z - k, source, True).start()

        @pl.when((z + k <= Z - 1) & (z > 0))
        def _():
            source = self.own(unit) if k == 0 else self.slot(unit, z + k)
            self.copy(index, z + k, source, False).start()

    def come(self, k):
        z = self.at.z
        return ((z - 1 - k, z - 1 - k >= 0), (z + 1 + k, z + 1 + k <= Z - 1))

    def wait_step(self, index, k):
        for upward, (s, there) in zip((True, False), self.come(k)):

            @pl.when(there)
            def _():
                ref = self.slot(self.units[index], s)
                self.copy(index, s, ref, not upward).wait_recv()

    def finish(self):
        z = self.at.z
        for index, unit in enumerate(self.units):
            for s in range(Z):

                @pl.when((s <= z) & (z < Z - 1))
                def _():
                    self.copy(index, s, self.slot(unit, s), True).wait_send()

                @pl.when((s >= z) & (z > 0))
                def _():
                    self.copy(index, s, self.slot(unit, s), False).wait_send()


class FeedWeights:
    def __init__(self, at, up, down, dst, uf, df, sems):
        self.at, self.up, self.down = at, up, down
        self.dst, self.uf, self.df = dst, uf, df
        (
            self.usend, self.urecv, self.dsend, self.drecv, self.ulocal, self.dlocal,
            self.xsend, self.xrecv,
        ) = sems
        self.columns = pl.ds(pl.multiple_of(D * at.rep, D), D)

    def rows(self, rep):
        return pl.ds(pl.multiple_of(PART * self.at.core + SHARD * rep, SHARD), SHARD)

    def slot(self, kind, s):
        return self.uf.at[2 * s + self.at.core] if kind == "u" else self.dst.at[s]

    def own(self, kind):
        if kind == "u":
            return self.up.at[:, self.columns]
        return self.down.at[pl.ds(pl.multiple_of(SHARD * self.at.rep, SHARD), SHARD)]

    def up_across(self, s, source):
        target = self.uf.at[2 * s + self.at.core]
        return copy_to(source, target, self.usend.at[s], self.urecv.at[s], self.at.sibling)

    def up_here(self):
        target = self.uf.at[2 * self.at.z + self.at.core]
        return pltpu.make_async_copy(self.up.at[:, self.columns], target, self.ulocal)

    def down_there(self, s, source):
        return copy_to(
            source, self.df.at[self.rows(self.at.rep)],
            self.dsend.at[s], self.drecv.at[self.at.rep], (s, self.at.spot),
        )

    def down_here(self, source):
        return pltpu.make_async_copy(source, self.df.at[self.rows(self.at.rep)], self.dlocal)

    def down_across(self):
        ref = self.df.at[pl.ds(pl.multiple_of(PART * self.at.core, PART), PART)]
        return copy_to(ref, ref, self.xsend, self.xrecv, self.at.sibling)

    def pass_on(self, kind, s, source):
        if kind == "u":
            self.up_across(s, source).start()
        else:

            @pl.when(s != self.at.rep)
            def _():
                self.down_there(s, source).start()

            @pl.when(s == self.at.rep)
            def _():
                self.down_here(source).start()

    def own_start(self, kind):
        if kind == "u":
            self.up_here().start()
        self.pass_on(kind, self.at.z, self.own(kind))

    def collect(self):
        for p in range(3):
            there = self.at.peers[p]
            copy_to(
                self.dst.at[0], self.df.at[self.rows(there)],
                self.dsend.at[0], self.drecv.at[there], self.at.peer(p),
            ).wait_recv()
        self.down_here(self.dst.at[0]).wait()
        self.down_across().start()

    def finish(self):
        self.up_here().wait()
        for s in range(Z):
            self.up_across(s, self.uf.at[2 * s + self.at.core]).wait()

            @pl.when(s != self.at.rep)
            def _():
                self.down_there(s, self.dst.at[s]).wait_send()

        self.down_across().wait()


def feed_sems():
    dma = pltpu.SemaphoreType.DMA
    return [dma((Z,)), dma((Z,)), dma((Z,)), dma((Z,)), dma, dma, dma, dma]


UNITS = [("a", 0), ("s", 0), ("a", 1), ("a", 2), ("u", 1), ("d", 1)]


def gather_kernel(
    aw, up, down, small, language, vision, lengths,
    wf, uf, df, vec, ub, xlow, onelow, two, q0, k0, v0, m0, z0, q1, k1, v1, m1, z1,
    wv, dst, sf, x, one,
    zsend, zrecv, psend, precv, asend, arecv, ssend, srecv,
    alocal, slocal, wlocal, xlocal, *fsems,
):
    at = Place()
    rep, z, core = at.rep, at.z, at.core
    rows_in = [
        pltpu.make_async_copy(ref, x.at[rows], xlocal.at[i])
        for i, (ref, rows) in enumerate(
            ((language, pl.ds(0, WORDS_HERE)), (vision, pl.ds(WORDS_HERE, REGIONS_HERE)))
        )
    ]
    for copy in rows_in:
        copy.start()
    at.enter(1)
    feed_weights = FeedWeights(at, up.at[1], down.at[1], dst, uf, df, fsems)

    def slot(unit, s):
        kind, i = unit
        if kind == "a":
            return wv.at[i, rep, 2 * s + core]
        return sf.at[2 * s + core] if kind == "s" else feed_weights.slot(kind, s)

    def own(unit):
        kind, i = unit
        if kind == "a":
            return aw.at[i, rep]
        return small if kind == "s" else feed_weights.own(kind)

    chain = Chain(at, UNITS, slot, own, zsend, zrecv)

    def plane_copy(layer, s, i):
        ref = wv.at[layer, at.peers[0] if i == 2 else rep, 2 * s + core]
        there = at.peer(1) if i == 2 else at.peer(i)
        return copy_to(ref, ref, psend.at[layer, s, i], precv.at[layer, s, i], there)

    def plane_arrival(layer, s, i):
        ref = wv.at[layer, at.peers[i], 2 * s + core]
        return copy_to(ref, ref, psend.at[layer, s, i], precv.at[layer, s, i], at.peer(i))

    def small_copy(s, source):
        return copy_to(source, sf.at[2 * s + core], ssend.at[s], srecv.at[s], at.sibling)

    def pass_on(unit, s, source):
        kind, i = unit
        if kind == "a":
            for p in range(2):
                plane_copy(i, s, p).start()
        elif kind == "s":
            small_copy(s, source).start()
        else:
            feed_weights.pass_on(kind, s, source)

    def shard_here(layer):
        return pltpu.make_async_copy(aw.at[layer], wv.at[layer, :, 2 * z + core], alocal.at[layer])

    def small_here():
        return pltpu.make_async_copy(small, sf.at[2 * z + core], slocal)

    def own_start(unit):
        kind, i = unit
        if kind == "a":
            shard_here(i).start()
            copy_to(
                aw.at[i], wv.at[i, :, 2 * z + core], asend.at[i, z], arecv.at[i, z], at.sibling
            ).start()
        elif kind == "s":
            small_here().start()
            pass_on(unit, z, small)
        else:
            feed_weights.own_start(kind)

    def line_send_step(index, k):
        chain.send_step(index, k)
        if k == 0:
            own_start(UNITS[index])

    def pass_step(index, k):
        unit = UNITS[index]
        for s, there in chain.come(k):

            @pl.when(there)
            def _():
                pass_on(unit, s, slot(unit, s))

    def core_copy(layer, s):
        ref = wv.at[layer, :, 2 * s + core]
        return copy_to(ref, ref, asend.at[layer, s], arecv.at[layer, s], at.sibling)

    def core_arrival(layer, s):
        ref = wv.at[layer, :, 2 * s + at.other]
        return copy_to(ref, ref, asend.at[layer, s], arecv.at[layer, s], at.sibling)

    def relay_step(layer, k):
        for s, there in chain.come(k):

            @pl.when(there)
            def _():
                plane_arrival(layer, s, 0).wait_recv()
                plane_copy(layer, s, 2).start()

    def plane_step(layer, k):
        for s, there in chain.come(k):

            @pl.when(there)
            def _():
                plane_arrival(layer, s, 1).wait_recv()
                plane_arrival(layer, s, 2).wait_recv()
                core_copy(layer, s).start()

    count = len(UNITS)

    def exchange():
        line_send_step(0, 0)
        for time in range(count + 6):
            if time + 1 < count:
                line_send_step(time + 1, 0)
            for index, unit in enumerate(UNITS):
                k = time - index
                if 1 <= k <= 3:
                    chain.wait_step(index, k - 1)
                    if k <= 2:
                        line_send_step(index, k)
                    pass_step(index, k - 1)
                    yield time
                if unit[0] == "a" and 0 <= k - 2 <= 2:
                    relay_step(unit[1], k - 2)
                    yield time
                if unit[0] == "a" and 0 <= k - 3 <= 2:
                    plane_step(unit[1], k - 3)
                    yield time
            yield time + 1

    steps = exchange()
    clock = [0]

    def pump(times=1):
        for _ in range(times):
            clock[0] = next(steps, 99)

    def until(time):
        while clock[0] < time:
            pump()

    def ready(layer):
        until(UNITS.index(("a", layer)) + 6)
        shard_here(layer).wait()
        for s in range(Z):
            core_arrival(layer, s).wait_recv()
        pltpu.make_async_copy(wv.at[layer], wf.at[layer], wlocal.at[layer]).start()

    for copy in rows_in:
        copy.wait()
    xlow[...] = x[...].astype(LOW)
    until(UNITS.index(("s", 0)) + 4)
    small_here().wait()
    for s in range(Z):
        copy_to(
            small, sf.at[2 * s + at.other], ssend.at[s], srecv.at[s], at.sibling
        ).wait_recv()
    line = lax.broadcasted_iota(jnp.int32, (128, D), 0)
    lane = lax.broadcasted_iota(jnp.int32, (128, D), 1)
    vectors = jnp.zeros((32, D), FULL)
    for d in range(8):
        pick = ((lane == line + SHARD * d) & (line < SHARD)).astype(FULL).astype(LOW)
        vectors = vectors + dot(sf[d, :, :128], pick)
    vec[...] = vectors
    ub[...] = jnp.zeros_like(ub)
    for c in range(2):
        ub[0:2, PART * c : PART * c + PART] = sf[2 * rep + c].astype(FULL)[21:23, :]

    word_bias = length_bias(lengths, (1, WORDS_HERE), 1)
    ready(0)
    attend(
        x, xlow, wv, vec, 0, EVERY,
        [
            (LANG, VISN, pair_bias(WORDS_EACH, REGIONS_EACH, None)),
            (VISN, LANG, pair_bias(REGIONS_EACH, WORDS_EACH, word_bias)),
        ],
        q0, k0, v0, m0, z0, one, pump,
    )
    onelow[...] = one[...].astype(LOW)
    ready(1)
    attend(
        one, onelow, wv, vec, 1, LANG,
        [(LANG, LANG, pair_bias(WORDS_EACH, WORDS_EACH, word_bias))],
        q1, k1, v1, m1, z1, two, pump,
    )
    ready(2)
    attend(
        one, onelow, wv, vec, 2, VISN,
        [(VISN, VISN, pair_bias(REGIONS_EACH, REGIONS_EACH, None))],
        q1, k1, v1, m1, z1, two, pump,
    )
    until(99)
    feed_weights.collect()

    for layer in range(3):
        pltpu.make_async_copy(wv.at[layer], wf.at[layer], wlocal.at[layer]).wait()
        for s in range(Z):
            core_copy(layer, s).wait_send()

            @pl.when(s != z)
            def _():
                for i in range(3):
                    plane_copy(layer, s, i).wait_send()

    for s in range(Z):
        small_copy(s, small).wait_send()
    chain.finish()
    feed_weights.finish()


def gather(aw, up, down, small, language, vision, lengths):
    dma = pltpu.SemaphoreType.DMA
    count = len(UNITS)
    full = jax.ShapeDtypeStruct((ROWS, D), FULL)
    low = jax.ShapeDtypeStruct((ROWS, D), LOW)
    return pl.pallas_call(
        gather_kernel,
        out_shape=(
            jax.ShapeDtypeStruct((3, 4, 8, SHARD, D), LOW),
            jax.ShapeDtypeStruct((8, SHARD, D), LOW),
            jax.ShapeDtypeStruct((D, D), LOW),
            jax.ShapeDtypeStruct((32, D), FULL),
            jax.ShapeDtypeStruct((8, D), FULL),
            low, low, full,
            low, low, low, low, full,
            low, low, low, low, full,
        ),
        in_specs=[HBM] * 6 + [pl.BlockSpec(memory_space=pltpu.SMEM)],
        out_specs=(HBM,) * 3 + (ONCHIP,) * 15,
        scratch_shapes=[
            pltpu.VMEM((3, 4, 8, SHARD, D), LOW),
            pltpu.VMEM((Z, SHARD, D), LOW),
            pltpu.VMEM((8, 32, PART), LOW),
            pltpu.VMEM((ROWS, D), FULL),
            pltpu.VMEM((ROWS, D), FULL),
            dma((count, Z, 2)), dma((count, Z)),
            dma((3, Z, 3)), dma((3, Z, 3)),
            dma((3, Z)), dma((3, Z)),
            dma((Z,)), dma((Z,)),
            dma((3,)), dma, dma((3,)), dma((2,)),
            *feed_sems(),
        ],
        compiler_params=pltpu.CompilerParams(
            collective_id=0, has_side_effects=True, vmem_limit_bytes=VMEM_BYTES
        ),
        cost_estimate=pl.CostEstimate(
            flops=2_200_000_000, bytes_accessed=40_000_000, transcendentals=500_000
        ),
        name="gather_attention",
    )(aw, up, down, small, language, vision, lengths)


def dot(a, b):
    return jnp.dot(a, b, preferred_element_type=FULL)


def dot_t(a, b):
    return lax.dot_general(a, b, (((1,), (1,)), ((), ())), preferred_element_type=FULL)


def t_dot(a, b):
    return lax.dot_general(a, b, (((0,), (0,)), ((), ())), preferred_element_type=FULL)


def column_sum(a):
    return jnp.sum(a.astype(FULL), axis=0, keepdims=True)


def norm_stats(pre):
    mean = jnp.mean(pre, axis=-1, keepdims=True)
    centred = pre - mean
    spread = jnp.mean(centred * centred, axis=-1, keepdims=True)
    scale = lax.rsqrt(spread + 1e-06)
    return centred * scale, scale


def norm_back(grad, unit, scale, gain):
    flow = grad * (1.0 + gain)
    return (
        flow
        - jnp.mean(flow, axis=-1, keepdims=True)
        - unit * jnp.mean(flow * unit, axis=-1, keepdims=True)
    ) * scale


def item_of(index, size):
    return sum((index >= size * k).astype(jnp.int32) for k in range(1, ITEMS_HERE))


def pair_bias(query_size, key_size, key_bias):
    shape = (query_size * ITEMS_HERE, key_size * ITEMS_HERE)
    query_item = item_of(lax.broadcasted_iota(jnp.int32, shape, 0), query_size)
    key_item = item_of(lax.broadcasted_iota(jnp.int32, shape, 1), key_size)
    bias = jnp.where(query_item == key_item, 0.0, -1e30)
    return bias if key_bias is None else bias + key_bias


GROUP = 4


def head_masks(dtype):
    lane = lax.broadcasted_iota(jnp.int32, (1, 64 * GROUP), 1)
    return [
        ((lane >= 64 * i) & (lane < 64 * i + 64)).astype(FULL).astype(dtype) for i in range(GROUP)
    ]


def stacked(value):
    return jnp.concatenate([value * mask for mask in head_masks(LOW)], axis=0)


def unstacked(value, rows):
    value = value.reshape(GROUP, rows, 64 * GROUP)
    return sum(value[i] * mask for i, mask in enumerate(head_masks(FULL)))


def mix_heads(q_ref, k_ref, v_ref, m_ref, qrows, krows, bias, pump):
    nq, nk = qrows.stop - qrows.start, krows.stop - krows.start
    for group in range(HEADS // GROUP):
        lanes = slice(256 * group, 256 * group + 256)
        query, keys, values = q_ref[qrows, lanes], k_ref[krows, lanes], v_ref[krows, lanes]
        scores = dot_t(stacked(query), keys).reshape(GROUP, nq, nk) * 0.125 + bias[None]
        exponent = jnp.exp(scores - jnp.max(scores, axis=-1, keepdims=True))
        probs = exponent / jnp.sum(exponent, axis=-1, keepdims=True)
        mixed = dot(probs.astype(LOW).reshape(GROUP * nq, nk), values)
        m_ref[qrows, lanes] = unstacked(mixed, nq).astype(LOW)
        pump()


def head_back(q_ref, k_ref, v_ref, dm_ref, dq_ref, dk_ref, dv_ref, qrows, krows, bias, group, base):
    nq, nk = qrows.stop - qrows.start, krows.stop - krows.start
    lanes = slice(256 * group, 256 * group + 256)
    query, keys, values = q_ref[qrows, lanes], k_ref[krows, lanes], v_ref[krows, lanes]
    grad = dm_ref[qrows, lanes]
    keys = stacked(keys)
    scores = dot_t(keys, query).reshape(GROUP, nk, nq) * 0.125 + bias[None]
    exponent = jnp.exp(scores - jnp.max(scores, axis=1, keepdims=True))
    probs = exponent / jnp.sum(exponent, axis=1, keepdims=True)
    dp = dot_t(stacked(values), grad).reshape(GROUP, nk, nq)
    ds = probs * (dp - jnp.sum(probs * dp, axis=1, keepdims=True))
    ds = ds.astype(LOW).reshape(GROUP * nk, nq)
    dv = unstacked(dot(probs.astype(LOW).reshape(GROUP * nk, nq), grad), nk)
    dk = unstacked(dot(ds, query), nk) * 0.125
    dq = t_dot(ds, keys) * 0.125
    qhere = slice(qrows.start - base, qrows.stop - base)
    khere = slice(krows.start - base, krows.stop - base)
    dq_ref[qhere, lanes] = dq.astype(LOW)
    dk_ref[khere, lanes] = dk.astype(LOW)
    dv_ref[khere, lanes] = dv.astype(LOW)


def row_of(ref, i):
    return ref[i : i + 1, :]


def attend(
    x_ref, low_ref, w_ref, vec_ref, layer, rows, parts, q_ref, k_ref, v_ref, m_ref, z_ref, out_ref, pump
):
    low = low_ref[rows, :]
    vec = [row_of(vec_ref, 5 * layer + i) for i in range(5)]

    def matrix(m):
        return w_ref[layer, m].reshape(D, D)

    q_ref[rows, :] = (dot(low, matrix(0)) + vec[0]).astype(LOW)
    k_ref[rows, :] = dot(low, matrix(1)).astype(LOW)
    pump()
    v_ref[rows, :] = (dot(low, matrix(2)) + vec[1]).astype(LOW)
    for qrows, krows, bias in parts:
        mix_heads(q_ref, k_ref, v_ref, m_ref, qrows, krows, bias, pump)
    pre = x_ref[rows, :] + (dot(m_ref[rows, :], matrix(3)) + vec[2])
    z_ref[rows, :] = pre
    unit, _ = norm_stats(pre)
    out_ref[rows, :] = unit * (1.0 + vec[3]) + vec[4]
    pump()


WORDS_EACH = WORDS_HERE // ITEMS_HERE
REGIONS_EACH = REGIONS_HERE // ITEMS_HERE


def length_bias(lengths, shape, axis):
    index = lax.broadcasted_iota(jnp.int32, shape, axis)
    item = item_of(index, WORDS_EACH)
    real = sum(jnp.where(item == i, lengths[i], 0) for i in range(ITEMS_HERE))
    return jnp.where(index - WORDS_EACH * item < real, 0.0, -1000000000.0)


STREAMS = (1, 0)
CHUNKS = ((1, WORDS_HERE, 64), (1, WORDS_HERE + 64, 80), (0, 0, WORDS_HERE))
SELF_ROWS = (pl.ds(0, WORDS_HERE), pl.ds(WORDS_HERE, REGIONS_HERE))
PIECES = ((0, 0, 48), (0, 48, 32), (1, 0, 48), (1, 48, 48), (1, 96, 48))


def ffn_kernel(
    x2, lang_cot, visn_cot, uw1, dw1, vec, ub, onelow, m1, up, down,
    lang_out, visn_out, d2, gu, gd, gv, gb, ax1, ax2, bx1, bx2,
    *scratch,
):
    at = Place()
    rep, z, core = at.rep, at.z, at.core
    scratch = list(scratch)

    def take(count):
        some, scratch[:] = scratch[:count], scratch[count:]
        return some

    many = len(CHUNKS)
    xg, bg, ht, gt, hd, mine, dz = [take(many) for _ in range(7)]
    stage, land = [[take(many) for _ in range(2)] for _ in range(2)]
    uw0, dw0, dst = take(3)
    psend, precv, osend, orecv, olocal, bsend, brecv = take(7)
    zsend, zrecv = take(2)
    at.enter(1)
    feed_weights = FeedWeights(at, up.at[0], down.at[0], dst, uw0, dw0, scratch)

    chain = Chain(at, "ud", feed_weights.slot, feed_weights.own, zsend, zrecv)

    def weights_step(k):
        for index, kind in enumerate("ud"):
            if k > 0:
                chain.wait_step(index, k - 1)
            if k < 3:
                chain.send_step(index, k)
            if k == 0:
                feed_weights.own_start(kind)
            else:
                for s, there in chain.come(k - 1):

                    @pl.when(there)
                    def _():
                        feed_weights.pass_on(kind, s, feed_weights.slot(kind, s))

    def up_weight(t, lanes=slice(0, D)):
        return uw1[:, lanes] if t else uw0[:, :, lanes].reshape(D, lanes.stop - lanes.start)

    def down_weight(t, rows=slice(0, D)):
        return (dw1 if t else dw0)[rows, :]

    def plane_copy(which, i, hop, buffer):
        ref = buffer.at[at.peers[0] if hop == 2 else rep]
        there = at.peer(1) if hop == 2 else at.peer(hop)
        return copy_to(ref, ref, psend.at[which, i, hop], precv.at[which, i, hop], there)

    def plane_arrival(which, i, hop, buffer):
        ref = buffer.at[at.peers[hop]]
        return copy_to(ref, ref, psend.at[which, i, hop], precv.at[which, i, hop], at.peer(hop))

    def gather_start(which, i, buffer):
        for hop in range(2):
            plane_copy(which, i, hop, buffer).start()

    def gather_relay(which, i, buffer):
        plane_arrival(which, i, 0, buffer).wait_recv()
        plane_copy(which, i, 2, buffer).start()

    def gather_rest(which, i, buffer):
        for hop in (1, 2):
            plane_arrival(which, i, hop, buffer).wait_recv()

    def gather_sent(which, i, buffer):
        for hop in range(3):
            plane_copy(which, i, hop, buffer).wait_send()

    def first_copy(turn, i):
        return copy_to(
            stage[turn][i].at[pl.ds(0, 2)], land[turn][i].at[pl.ds(0, 2)],
            psend.at[2 * turn + 1, i, 0], precv.at[2 * turn + 1, i, 0], at.peer(0),
        )

    def second_copy(turn, i):
        return copy_to(
            stage[turn][i].at[2], land[turn][i].at[2],
            psend.at[2 * turn + 1, i, 1], precv.at[2 * turn + 1, i, 1], at.peer(1),
        )

    def return_first(turn, i):
        for hop, p in enumerate((0, 2)):
            stage[turn][i][hop] = mine[i][at.peers[p]].astype(LOW)
        first_copy(turn, i).start()

    def return_second(turn, i):
        first_copy(turn, i).wait_recv()
        passed = land[turn][i][1].astype(FULL)
        stage[turn][i][2] = (mine[i][at.peers[1]] + passed).astype(LOW)
        second_copy(turn, i).start()

    def summed(turn, i):
        second_copy(turn, i).wait_recv()
        passed = land[turn][i][0].astype(FULL) + land[turn][i][2].astype(FULL)
        return mine[i][rep] + passed

    def flat(ref):
        value = ref[...]
        return value.reshape(value.shape[0] * value.shape[1], value.shape[2])

    blocks = [slice(256 * k, 256 * k + 256) for k in range(3)]

    def up_and_down(i):
        t, _, count = CHUNKS[i]
        rows = flat(xg[i])
        hidden = dot(rows, up_weight(t, blocks[0]))
        for k, block in enumerate(blocks):
            ahead = dot(rows, up_weight(t, blocks[k + 1])) if k < 2 else None
            hidden = hidden + ub[t : t + 1, block]
            below = 0.5 * (1.0 + lax.erf(hidden * (1.0 / math.sqrt(2.0))))
            gt[i][:, block] = (hidden * below).astype(LOW)
            ht[i][:, block] = below + hidden * (
                jnp.exp(-0.5 * hidden * hidden) * (1.0 / math.sqrt(2.0 * math.pi))
            )
            hidden = ahead
        mine[i][...] = dot(gt[i][...], down_weight(t)).reshape(4, count, D)

    def rows_back(i):
        t, _, count = CHUNKS[i]
        rows = flat(bg[i])
        for block in blocks:
            grad = dot_t(rows, down_weight(t, block)) * ht[i][:, block]
            hd[i][:, block] = grad.astype(LOW)
        mine[i][...] = dot_t(hd[i][...], up_weight(t)).reshape(4, count, D)

    def weights_back(t):
        pieces = [i for i in range(many) if CHUNKS[i][0] == t]
        for block in blocks:
            gd[t, block, :] = sum(t_dot(gt[i][:, block], flat(bg[i])) for i in pieces).astype(LOW)
            gu[t, block, :] = sum(t_dot(flat(xg[i])[:, block], hd[i][...]) for i in pieces).astype(LOW)
        total = sum(column_sum(hd[i][...]) for i in pieces)
        row = lax.broadcasted_iota(jnp.int32, (Z, D), 0)
        gb[Z * t : Z * t + Z, :] = jnp.where(row == rep, jnp.broadcast_to(total, (Z, D)), 0.0)

    def chunk_rows(i):
        t, start, count = CHUNKS[i]
        here = start - WORDS_HERE * t
        return slice(start, start + count), slice(here, here + count)

    def norm_turn(i):
        t = CHUNKS[i][0]
        rows, here = chunk_rows(i)
        bias, gain, shift = [row_of(vec, 15 + 3 * t + k) for k in range(3)]
        pre = x2[rows, :] + (summed(0, i) + bias)
        unit, scale = norm_stats(pre)
        (lang_out, visn_out)[t][here, :] = unit * (1.0 + gain) + shift
        grad = (lang_cot, visn_cot)[t][here, :]
        dz[i][...] = norm_back(grad, unit, scale, gain)
        branch = dz[i][...].astype(LOW)
        bg[i][rep] = branch
        gather_start(2, i, bg[i])
        for k, value in enumerate((column_sum(branch), column_sum(grad * unit), column_sum(grad))):
            gv[3 * t + k : 3 * t + k + 1, :] += value

    landed, across = (ax1, ax2), (bx1, bx2)

    def operand_copy(source, piece, p):
        k, first, count = PIECES[piece]
        return copy_to(
            source.at[pl.ds(WORDS_HERE * k + first, count)],
            landed[k].at[rep, pl.ds(first, count)],
            osend.at[piece, p], orecv.at[piece, p], at.peer(p),
        )

    def operand_here(source, k):
        return pltpu.make_async_copy(source.at[SELF_ROWS[k]], landed[k].at[rep], olocal.at[k])

    def across_copy(k):
        return copy_to(landed[k], across[k], bsend.at[k], brecv.at[k], at.sibling)

    def operand_send(piece, p):
        @pl.when(at.peers[p] != 3)
        def _():
            operand_copy(onelow, piece, p).start()

        @pl.when(at.peers[p] == 3)
        def _():
            operand_copy(m1, piece, p).start()

    def operands_start():
        for k in range(2):

            @pl.when(rep != 3)
            def _():
                operand_here(onelow, k).start()

            @pl.when(rep == 3)
            def _():
                operand_here(m1, k).start()

    def operands_across(k):
        operand_here(m1, k).wait()
        for piece, (which, first, count) in enumerate(PIECES):
            if which == k:
                for p in range(3):
                    ref = landed[k].at[at.peers[p], pl.ds(first, count)]
                    copy_to(
                        ref, ref, osend.at[piece, p], orecv.at[piece, p], at.peer(p)
                    ).wait_recv()
        across_copy(k).start()

    gv[...] = jnp.zeros_like(gv)
    for i in range(many):
        xg[i][rep] = x2[chunk_rows(i)[0], :].astype(LOW)
        gather_start(0, i, xg[i])
    weights_step(0)
    operands_start()
    gather_relay(0, 0, xg[0])
    gather_rest(0, 0, xg[0])
    gather_relay(0, 1, xg[1])
    up_and_down(0)
    return_first(0, 0)
    weights_step(1)
    gather_relay(0, 2, xg[2])
    gather_rest(0, 1, xg[1])
    operand_send(0, 0)
    operand_send(0, 1)
    up_and_down(1)
    return_second(0, 0)
    return_first(0, 1)
    weights_step(2)
    gather_rest(0, 2, xg[2])
    norm_turn(0)
    weights_step(3)
    return_second(0, 1)
    feed_weights.collect()
    feed_weights.finish()
    operand_send(0, 2)
    operand_send(1, 0)
    operand_send(1, 1)
    up_and_down(2)
    return_first(0, 2)
    gather_relay(2, 0, bg[0])
    norm_turn(1)
    return_second(0, 2)
    gather_rest(2, 0, bg[0])
    operand_send(1, 2)
    operand_send(2, 0)
    operand_send(2, 1)
    rows_back(0)
    return_first(1, 0)
    gather_relay(2, 1, bg[1])
    norm_turn(2)
    gather_rest(2, 1, bg[1])
    operand_send(2, 2)
    operand_send(3, 0)
    operand_send(3, 1)
    rows_back(1)
    return_second(1, 0)
    return_first(1, 1)
    gather_relay(2, 2, bg[2])
    gather_rest(2, 2, bg[2])
    operand_send(3, 2)
    operand_send(4, 0)
    operand_send(4, 1)
    rows_back(2)
    return_second(1, 1)
    return_first(1, 2)
    operand_send(4, 2)
    operands_across(0)
    weights_back(1)
    return_second(1, 2)
    operands_across(1)
    weights_back(0)
    for i in range(many):
        d2[chunk_rows(i)[0], :] = dz[i][...] + summed(1, i)
    chain.finish()
    for k in range(2):
        across_copy(k).wait()
    for k in range(2):
        for p in range(3):
            for piece, (which, _, _) in enumerate(PIECES):
                if which == k:
                    operand_copy(m1, piece, p).wait_send()
    for i in range(many):
        gather_sent(0, i, xg[i])
        gather_sent(2, i, bg[i])
        for turn in range(2):
            first_copy(turn, i).wait_send()
            second_copy(turn, i).wait_send()


def feed(x2, lang_cot, visn_cot, uw1, dw1, vec, ub, onelow, m1, up, down):
    dma = pltpu.SemaphoreType.DMA
    many = len(CHUNKS)

    def each(lead, width, dtype):
        return [pltpu.VMEM((*lead, chunk[2], width), dtype) for chunk in CHUNKS]

    def each_flat(width, dtype):
        return [pltpu.VMEM((4 * chunk[2], width), dtype) for chunk in CHUNKS]

    def rows_of_plane(count):
        return jax.ShapeDtypeStruct((4, count, D), LOW)

    return pl.pallas_call(
        ffn_kernel,
        out_shape=(
            jax.ShapeDtypeStruct((WORDS_HERE, D), FULL),
            jax.ShapeDtypeStruct((REGIONS_HERE, D), FULL),
            jax.ShapeDtypeStruct((ROWS, D), FULL),
            jax.ShapeDtypeStruct((2, D, D), LOW),
            jax.ShapeDtypeStruct((2, D, D), LOW),
            jax.ShapeDtypeStruct((8, D), FULL),
            jax.ShapeDtypeStruct((8, D), FULL),
            rows_of_plane(WORDS_HERE), rows_of_plane(REGIONS_HERE),
            rows_of_plane(WORDS_HERE), rows_of_plane(REGIONS_HERE),
        ),
        in_specs=[ONCHIP] * 7 + [HBM] * 4,
        out_specs=(ONCHIP,) * 7 + (HBM,) * 4,
        scratch_shapes=each((4,), D, LOW)
        + each((4,), D, LOW)
        + each_flat(D, FULL)
        + each_flat(D, LOW)
        + each_flat(D, LOW)
        + each((4,), D, FULL)
        + each((), D, FULL)
        + each((3,), D, LOW) * 2
        + each((3,), D, LOW) * 2
        + [
            pltpu.VMEM((8, SHARD, D), LOW),
            pltpu.VMEM((D, D), LOW),
            pltpu.VMEM((Z, SHARD, D), LOW),
            dma((4, many, 3)), dma((4, many, 3)),
            dma((5, 3)), dma((5, 3)), dma((2,)), dma((2,)), dma((2,)),
            dma((2, Z, 2)), dma((2, Z)), *feed_sems(),
        ],
        compiler_params=pltpu.CompilerParams(
            collective_id=1, has_side_effects=True, vmem_limit_bytes=VMEM_BYTES
        ),
        cost_estimate=pl.CostEstimate(
            flops=6_400_000_000, bytes_accessed=12_000_000, transcendentals=1_400_000
        ),
        name="feed_forward",
    )(x2, lang_cot, visn_cot, uw1, dw1, vec, ub, onelow, m1, up, down)


def turned_bias(query_size, key_size, key_bias):
    shape = (key_size * ITEMS_HERE, query_size * ITEMS_HERE)
    key_item = item_of(lax.broadcasted_iota(jnp.int32, shape, 0), key_size)
    query_item = item_of(lax.broadcasted_iota(jnp.int32, shape, 1), query_size)
    bias = jnp.where(query_item == key_item, 0.0, -1e30)
    return bias if key_bias is None else bias + key_bias


LAYER_ROWS = (EVERY, LANG, VISN)
WIDE_UNITS = 5


def backward_kernel(
    d2, lengths, vec, w, q0, k0, v0, z0, q1, k1, v1, z1, gu, gd, gv, gb,
    xlow, m0, ax1, ax2, bx1, bx2,
    dx, oa, ou, od, os,
    wbuf, xa0, xa1, xa2, ys0, ys1, ys2, ya0, ya1, ya2, yb0, yb1, yb2,
    share, gou, gsu, god, gsd, dland, zwide, zlow, rwide, rlow, edge, wide, final, d1, dm, gs, s0, s1, s2, s3, s4, scol,
    wsem, asem, ysend, yrecv, yfsend, yfrecv,
    dsend, drecv, dlocal, wsend, wrecv, lsend, lrecv, rsend, rrecv, esend, erecv,
    gsend, grecv, glocal, ssend, srecv, osend, orecv, olocal, bsend, brecv, hsend, hrecv, hlocal,
):
    at = Place()
    rep, z, core, other = at.rep, at.z, at.core, at.other
    own_half = pl.ds(pl.multiple_of(PART * core, PART), PART)
    other_half = pl.ds(pl.multiple_of(PART * other, PART), PART)
    xa, xin = (xa0, xa1, xa2), (None, (ax1, bx1), (ax2, bx2))
    ys, ya, yb = (ys0, ys1, ys2), (ya0, ya1, ya2), (yb0, yb1, yb2)

    def load(layer):
        return pltpu.make_async_copy(w.at[layer], wbuf.at[layer], wsem.at[layer])

    def load_rows(layer, side):
        return pltpu.make_async_copy(
            xin[layer][side], xa[layer].at[side], asem.at[layer, side]
        )

    for layer in (1, 2, 0):
        load(layer).start()
    for layer in (1, 2):
        for side in range(2):
            load_rows(layer, side).start()
    at.enter(2)

    def operand_copy(source, p):
        return copy_to(source, xa0.at[0, rep], osend.at[p], orecv.at[p], at.peer(p))

    def operand_across():
        return copy_to(xa0.at[0], xa0.at[1], bsend, brecv, at.sibling)

    def operand_flow():
        for p in (2, 0, 1):

            @pl.when(at.peers[p] != 3)
            def _():
                operand_copy(xlow, p).start()

            @pl.when(at.peers[p] == 3)
            def _():
                operand_copy(m0, p).start()

        @pl.when(rep != 3)
        def _():
            pltpu.make_async_copy(xlow, xa0.at[0, rep], olocal).start()

        @pl.when(rep == 3)
        def _():
            pltpu.make_async_copy(m0, xa0.at[0, rep], olocal).start()

        yield
        pltpu.make_async_copy(m0, xa0.at[0, rep], olocal).wait()
        for p in range(3):
            copy_to(
                m0, xa0.at[0, at.peers[p]], osend.at[p], orecv.at[p], at.peer(p)
            ).wait_recv()
        operand_across().start()

    def y_copy(layer, p):
        return copy_to(
            ys[layer].at[at.peers[p]], ya[layer].at[rep],
            ysend.at[layer, p], yrecv.at[layer, p], at.peer(p),
        )

    def y_forward(layer, i):
        there = rep if i == 3 else at.peers[i]
        return copy_to(
            ya[layer].at[there, :, other_half], yb[layer].at[there],
            yfsend.at[layer, i], yfrecv.at[layer, i], at.sibling,
        )

    def y_arrival(layer, p):
        return copy_to(
            ys[layer].at[0], ya[layer].at[at.peers[p]],
            ysend.at[layer, p], yrecv.at[layer, p], at.peer(p),
        )

    def share_of(unit, s):
        if unit < 3:
            return share.at[unit, s]
        return gou.at[unit - 3, s] if unit < 5 else dland.at[unit - 5, s]

    def slot_of(unit, s):
        return zwide.at[unit, s] if unit < 5 else zlow.at[unit - 5, s]

    def stop_of(unit):
        return rwide.at[unit] if unit < 5 else rlow.at[unit - 5]

    def column_copy(unit, s, source):
        return copy_to(source, slot_of(unit, z), wsend.at[unit, s], wrecv.at[unit, z], at.column(s))

    def column_arrival(unit, s):
        ref = slot_of(unit, s)
        return copy_to(ref, ref, wsend.at[unit, s], wrecv.at[unit, s], at.column(s))

    def stop_copy(unit):
        far = lax.div(z, 3)
        return copy_to(
            share_of(unit, 2 - far), stop_of(unit),
            rsend.at[unit], rrecv.at[unit], at.column(1 + far),
        )

    def stop_arrival(unit):
        ref = stop_of(unit)
        return copy_to(ref, ref, rsend.at[unit], rrecv.at[unit], at.column(3 * (z - 1)))

    is_end = (z == 0) | (z == Z - 1)
    is_middle = (z > 0) & (z < Z - 1)
    straight = (z > 0, z == 0, z == Z - 1, z < Z - 1)

    def from_layer(s):
        return ((z != s) & is_end) | (is_middle & ((z == s + 1) | (z == s - 1)))

    def column_start(unit):
        @pl.when(is_end)
        def _():
            stop_copy(unit).start()

        for s in (3, 0, 1, 2):

            @pl.when(straight[s])
            def _():
                column_copy(unit, s, share_of(unit, s)).start()

        slot_of(unit, z)[...] = share_of(unit, z)[...]

    def column_stop(unit):
        @pl.when(is_middle)
        def _():
            stop_arrival(unit).wait_recv()
            ref = stop_of(unit)
            ref[...] = (ref[...].astype(FULL) + share_of(unit, 3 - z)[...].astype(FULL)).astype(LOW)
            column_copy(unit, 3 - z, ref).start()

    def column_sum_of(unit):
        for s in range(Z):

            @pl.when(from_layer(s))
            def _():
                column_arrival(unit, s).wait_recv()

        total = slot_of(unit, 0)[...].astype(FULL)
        for s in range(1, Z):
            total = total + slot_of(unit, s)[...].astype(FULL)
        return total.astype(LOW)

    for edge_z, s in ((1, 3), (2, 0)):

        @pl.when(z == edge_z)
        def _():
            for unit in range(7):
                ref = slot_of(unit, s)
                ref[...] = jnp.zeros_like(ref)

    def landing(unit, there):
        if unit < 3:
            return oa.at[unit, there]
        if unit < 5:
            return ou.at[unit - 3, :, pl.ds(pl.multiple_of(D * there, D), D)]
        return od.at[unit - 5, pl.ds(pl.multiple_of(SHARD * there, SHARD), SHARD)]

    def source_of(unit):
        return wide.at[unit] if unit < 5 else final.at[unit - 5]

    def share_copy(unit, i):
        there = at.peers[0] if i == 2 else rep
        return copy_to(
            landing(unit, there) if i == 2 else source_of(unit), landing(unit, there),
            gsend.at[unit, i], grecv.at[unit, i], at.peer(1) if i == 2 else at.peer(i),
        )

    def share_arrival(unit, i):
        ref = landing(unit, at.peers[i])
        return copy_to(ref, ref, gsend.at[unit, i], grecv.at[unit, i], at.peer(i))

    def share_out(unit):
        for i in range(2):
            share_copy(unit, i).start()
        pltpu.make_async_copy(source_of(unit), landing(unit, rep), glocal.at[unit]).start()
        yield
        share_arrival(unit, 0).wait_recv()
        share_copy(unit, 2).start()

    def edge_copy(unit):
        return copy_to(
            edge.at[unit, pl.ds(pl.multiple_of(SHARD * other, SHARD), SHARD)],
            wide.at[unit, :, own_half], esend.at[unit], erecv.at[unit], at.sibling,
        )

    def wide_end(unit):
        column_stop(unit)
        yield
        edge[unit] = column_sum_of(unit)
        edge_copy(unit).start()
        wide[unit, :, own_half] = edge[unit, pl.ds(pl.multiple_of(SHARD * core, SHARD), SHARD), :]
        yield
        edge_copy(unit).wait_recv()
        yield from share_out(unit)

    def half_of(kind, t, side):
        if kind:
            return gd.at[t, side]
        return gu.at[t, :, :, pl.ds(pl.multiple_of(PART * side, PART), PART)]

    def half_across(kind, t):
        return copy_to(
            half_of(kind, t, other), (gsu, gsd)[kind].at[t],
            hsend.at[kind, t], hrecv.at[kind, t], at.sibling,
        )

    def half_here(kind, t):
        return pltpu.make_async_copy(
            half_of(kind, t, core), (gou, god)[kind].at[t], hlocal.at[kind, t]
        )

    def half_start(kind, t):
        half_across(kind, t).start()
        half_here(kind, t).start()

    def half_sum(kind, t):
        half_across(kind, t).wait_recv()
        half_here(kind, t).wait()
        ours, theirs = ((gou, gsu), (god, gsd))[kind]
        ours[t] = (ours[t].astype(FULL) + theirs[t].astype(FULL)).astype(LOW)

    def up_flow(t):
        half_start(0, t)
        yield
        half_sum(0, t)
        column_start(3 + t)
        yield
        yield from wide_end(3 + t)

    def down_copy(t, p):
        return copy_to(
            god.at[t, at.peers[p]], dland.at[t, rep], dsend.at[t, p], drecv.at[t, p], at.peer(p)
        )

    def down_arrival(t, p):
        return copy_to(
            god.at[t, rep], dland.at[t, at.peers[p]], dsend.at[t, p], drecv.at[t, p], at.peer(p)
        )

    def down_here(t):
        return pltpu.make_async_copy(god.at[t, rep], dland.at[t, rep], dlocal.at[t])

    def down_flow(t):
        half_start(1, t)
        yield
        half_sum(1, t)
        for p in range(3):
            down_copy(t, p).start()
        down_here(t).start()
        yield
        for p in range(3):
            down_arrival(t, p).wait_recv()
        down_here(t).wait()
        column_start(5 + t)
        yield
        column_stop(5 + t)
        yield
        final[t] = column_sum_of(5 + t)
        yield from share_out(5 + t)

    def flat(value):
        return value.reshape(value.shape[0] * value.shape[1], value.shape[2])

    words, regions = pl.ds(0, WORDS_HERE), pl.ds(WORDS_HERE, REGIONS_HERE)
    pieces = (
        ((0, words), (1, regions), (2, regions), (3, pl.ds(0, ROWS))),
        ((0, regions), (1, words), (2, words)),
    )

    def piece_each(turn, act):
        for p in (2, 0, 1):
            for m, rows in pieces[turn]:

                @pl.when(at.peers[p] == m)
                def _():
                    act(
                        copy_to(
                            ys0.at[m, rows], ya0.at[rep, rows],
                            ysend.at[3 * turn, p], yrecv.at[3 * turn, p], at.peer(p),
                        )
                    )

    def piece_arrivals(p):
        for turn in range(2):
            for m, rows in pieces[turn]:

                @pl.when(rep == m)
                def _():
                    ref = ya0.at[at.peers[p], rows]
                    copy_to(
                        ref, ref, ysend.at[3 * turn, p], yrecv.at[3 * turn, p], at.peer(p)
                    ).wait_recv()

    def y_flow(layer):
        if layer == 0:
            piece_each(0, lambda copy: copy.start())
            yield
            piece_each(1, lambda copy: copy.start())
        else:
            for p in (2, 0, 1):
                y_copy(layer, p).start()
        ya[layer][rep] = ys[layer][rep]
        y_forward(layer, 3).start()
        yield
        for p in range(3):
            if layer == 0:
                piece_arrivals(p)
            else:
                y_arrival(layer, p).wait_recv()
            y_forward(layer, p).start()
        yield
        if layer > 0:
            for side in range(2):
                load_rows(layer, side).wait()
        else:
            operand_across().wait_recv()
        grad = t_dot(flat(xa[layer][0]), flat(ya[layer][:, :, own_half]))
        for i in range(4):
            y_forward(layer, i).wait_recv()
        grad = grad + t_dot(flat(xa[layer][1]), flat(yb[layer][...]))
        share[layer] = grad.astype(LOW).reshape(Z, 2 * SHARD, PART)
        column_start(layer)
        yield
        yield from wide_end(layer)

    small_ways = (at.sibling, at.peer(0), at.peer(1))
    small_from = (gs, s1, s2)
    small_land = (s0, s3, s4)

    def small_copy(i):
        return copy_to(small_from[i], small_land[i], ssend.at[i], srecv.at[i], small_ways[i])

    def small_line(s):
        return copy_to(scol.at[z], scol.at[z], ssend.at[3 + s], srecv.at[3 + z], at.column(s))

    def small_arrival(s):
        return copy_to(scol.at[s], scol.at[s], ssend.at[3 + s], srecv.at[3 + s], at.column(s))

    def small_flow():
        small_copy(0).start()
        yield
        small_copy(0).wait_recv()
        s1[...] = gs[...] + s0[...]
        small_copy(1).start()
        yield
        small_copy(1).wait_recv()
        s2[...] = s1[...] + s3[...]
        small_copy(2).start()
        yield
        small_copy(2).wait_recv()
        scol[z] = s2[...] + s4[...]
        for s in range(Z):

            @pl.when(s != z)
            def _():
                small_line(s).start()

        yield
        for s in range(Z):

            @pl.when(s != z)
            def _():
                small_arrival(s).wait_recv()

        os[...] = (scol[0] + scol[1]) + (scol[2] + scol[3])

    u0, u1, w0, w1, y0, y1, y2, sm, xm = range(9)
    flows = [
        up_flow(0), up_flow(1), down_flow(0), down_flow(1),
        y_flow(0), y_flow(1), y_flow(2), small_flow(), operand_flow(),
    ]

    def go(*names):
        for name in names:
            next(flows[name], None)

    gs[...] = jnp.zeros_like(gs)
    gs[15:21, :] = gv[0:6, :]
    gs[21:29, :] = gb[...]

    def attend_back(grad, layer, parts, q, k, v, zs, dx_ref, marks):
        rows = LAYER_ROWS[layer]
        vecs = [row_of(vec, 5 * layer + i) for i in range(5)]
        unit, scale = norm_stats(zs[rows, :])
        dz = norm_back(grad, unit, scale, vecs[3])
        branch = dz.astype(LOW)
        out = ys[layer]
        out[3] = branch
        for i, value in enumerate(
            (column_sum(branch), column_sum(grad * unit), column_sum(grad))
        ):
            gs[5 * layer + 2 + i : 5 * layer + 3 + i, :] = value
        dx_ref[rows, :] = dz
        load(layer).wait()
        dm[rows, :] = dot_t(branch, wbuf[layer, 3]).astype(LOW)
        go(*marks[0])
        for (qrows, krows, pair_mask), mark in zip(parts, marks[1]):
            for group in range(HEADS // GROUP):
                head_back(
                    q, k, v, dm, out.at[0], out.at[1], out.at[2],
                    qrows, krows, pair_mask, group, rows.start,
                )
            go(*mark)
        gs[5 * layer : 5 * layer + 1, :] = column_sum(out[0])
        gs[5 * layer + 1 : 5 * layer + 2, :] = column_sum(out[2])
        go(*marks[2])
        dx_ref[rows, :] += (
            dot_t(out[0], wbuf[layer, 0])
            + (dot_t(out[1], wbuf[layer, 1]) + dot_t(out[2], wbuf[layer, 2]))
        )
        go(*marks[3])

    word_bias = length_bias(lengths, (WORDS_HERE, 1), 0)
    go(w1, u1, w0, u0, xm)
    attend_back(
        d2[LANG, :], 1,
        [(LANG, LANG, turned_bias(WORDS_EACH, WORDS_EACH, word_bias))], q1, k1, v1, z1, d1,
        ([w1, u1, w0, u0], [[y1]], [], [u1]),
    )
    attend_back(
        d2[VISN, :], 2,
        [(VISN, VISN, turned_bias(REGIONS_EACH, REGIONS_EACH, None))], q1, k1, v1, z1, d1,
        ([u0], [[y2]], [w1, w0], [u1, y1]),
    )
    attend_back(
        d1[...], 0,
        [
            (LANG, VISN, turned_bias(WORDS_EACH, REGIONS_EACH, None)),
            (VISN, LANG, turned_bias(REGIONS_EACH, WORDS_EACH, word_bias)),
        ],
        q0, k0, v0, z0, dx,
        ([u1, u0, y1], [[y0, u0, w1, w0, y1, y2, xm], [y0]], [sm], [u1, y2, u0]),
    )
    go(sm, y0, y2, y0, sm, w1, w0, y1, y0, y1, sm, y2, w1, w0, y2, y1, sm, y0, y2, y0, y0)
    for flow in range(9):
        for _ in range(9):
            go(flow)

    for unit in range(7):
        pltpu.make_async_copy(source_of(unit), landing(unit, rep), glocal.at[unit]).wait()
        for i in (1, 2):
            share_arrival(unit, i).wait_recv()
        for i in range(3):
            share_copy(unit, i).wait_send()
        for s in range(Z):

            @pl.when(straight[s])
            def _():
                column_copy(unit, s, share_of(unit, s)).wait_send()

        @pl.when(is_end)
        def _():
            stop_copy(unit).wait_send()

        @pl.when(is_middle)
        def _():
            column_copy(unit, 3 - z, stop_of(unit)).wait_send()

    for p in range(3):
        operand_copy(m0, p).wait_send()
    operand_across().wait_send()
    for t in range(2):
        for kind in range(2):
            half_across(kind, t).wait_send()
    for turn in range(2):
        piece_each(turn, lambda copy: copy.wait_send())
    for layer in range(3):
        if layer > 0:
            for p in range(3):
                y_copy(layer, p).wait_send()
        for i in range(4):
            y_forward(layer, i).wait_send()
    for t in range(2):
        for p in range(3):
            down_copy(t, p).wait_send()
    for unit in range(WIDE_UNITS):
        edge_copy(unit).wait_send()
    for i in range(3):
        small_copy(i).wait_send()
    for s in range(Z):

        @pl.when(s != z)
        def _():
            small_line(s).wait_send()


def backward(d2, lengths, vec, w, kept, gu, gd, gv, gb, rows):
    dma = pltpu.SemaphoreType.DMA
    sizes = [layer_rows.stop - layer_rows.start for layer_rows in LAYER_ROWS]

    def each(lead, width):
        return [pltpu.VMEM((*lead, n, width), LOW) for n in sizes]

    return pl.pallas_call(
        backward_kernel,
        out_shape=(
            jax.ShapeDtypeStruct((ROWS, D), FULL),
            jax.ShapeDtypeStruct((3, 4, SHARD, D), LOW),
            jax.ShapeDtypeStruct((2, SHARD, FF), LOW),
            jax.ShapeDtypeStruct((2, PART, D), LOW),
            jax.ShapeDtypeStruct((32, D), FULL),
        ),
        in_specs=[ONCHIP, pl.BlockSpec(memory_space=pltpu.SMEM), ONCHIP, HBM]
        + [ONCHIP] * 8
        + [HBM, HBM, ONCHIP, ONCHIP]
        + [HBM] * 6,
        out_specs=(ONCHIP, HBM, HBM, HBM, ONCHIP),
        scratch_shapes=[
            pltpu.VMEM((3, 4, D, D), LOW),
            *each((2, 4), D), *each((4,), D), *each((4,), D), *each((4,), PART),
            pltpu.VMEM((3, Z, 2 * SHARD, PART), LOW),
            pltpu.VMEM((2, Z, 2 * SHARD, PART), LOW),
            pltpu.VMEM((2, Z, 2 * SHARD, PART), LOW),
            pltpu.VMEM((2, 4, SHARD, D), LOW),
            pltpu.VMEM((2, 4, SHARD, D), LOW),
            pltpu.VMEM((2, Z, SHARD, D), LOW),
            pltpu.VMEM((WIDE_UNITS, Z, 2 * SHARD, PART), LOW),
            pltpu.VMEM((2, Z, SHARD, D), LOW),
            pltpu.VMEM((WIDE_UNITS, 2 * SHARD, PART), LOW),
            pltpu.VMEM((2, SHARD, D), LOW),
            pltpu.VMEM((WIDE_UNITS, 2 * SHARD, PART), LOW),
            pltpu.VMEM((WIDE_UNITS, SHARD, D), LOW),
            pltpu.VMEM((2, SHARD, D), LOW),
            pltpu.VMEM((ROWS, D), FULL),
            pltpu.VMEM((ROWS, D), LOW),
            *[pltpu.VMEM((32, D), FULL)] * 6,
            pltpu.VMEM((Z, 32, D), FULL),
            dma((3,)), dma((3, 2)),
            dma((4, 3)), dma((4, 3)), dma((3, 4)), dma((3, 4)),
            dma((2, 3)), dma((2, 3)), dma((2,)),
            dma((7, Z)), dma((7, Z)), dma((2, Z)), dma((2, Z)),
            dma((7,)), dma((7,)),
            dma((WIDE_UNITS,)), dma((WIDE_UNITS,)),
            dma((7, 3)), dma((7, 3)), dma((7,)),
            dma((3 + Z,)), dma((3 + Z,)),
            dma((3,)), dma((3,)), dma, dma, dma, dma((2, 2)), dma((2, 2)), dma((2, 2)),
        ],
        compiler_params=pltpu.CompilerParams(
            collective_id=2, has_side_effects=True, vmem_limit_bytes=VMEM_BYTES
        ),
        cost_estimate=pl.CostEstimate(
            flops=4_400_000_000, bytes_accessed=30_000_000, transcendentals=500_000
        ),
        name="attention_backward",
    )(d2, lengths, vec, w, *kept, gu, gd, gv, gb, *rows)


def finish_kernel(
    oa, ou, od, os, dx, lo, vo,
    wa, wu, wd, va, vf, vu, lang_grad, visn_grad, lang_out, visn_out,
):
    wa[...] = oa[...].astype(FULL)
    wu[...] = ou[...].astype(FULL)
    wd[...] = od[...].astype(FULL)

    @pl.when(pl.program_id(0) == 0)
    def _():
        lang_grad[...] = dx[LANG, :]
        visn_grad[...] = dx[VISN, :]
        lang_out[...] = lo[...]
        visn_out[...] = vo[...]
        spot = lax.axis_index("fsdp")
        z = lax.div(spot, 2)
        own = jnp.zeros((32, SHARD), FULL)
        for d in range(8):
            own = jnp.where(spot == d, os[:, SHARD * d : SHARD * d + SHARD], own)
        for i in range(5):
            for layer in range(3):
                va[i, layer : layer + 1, :] = own[5 * layer + i : 5 * layer + i + 1, :]
        for i in range(3):
            for t in range(2):
                vf[i, t : t + 1, :] = own[15 + 3 * t + i : 16 + 3 * t + i, :]
        for t in range(2):
            row = os[pl.ds(21 + 4 * t + z, 1), :]
            vu[t : t + 1, :] = jnp.where(spot == 2 * z, row[:, :PART], row[:, PART:])


def finish(oa, ou, od, os, dx, lo, vo):
    def whole(shape):
        return pl.BlockSpec(shape, lambda i: (0,) * len(shape))

    parts = [
        pl.BlockSpec((3, 1, SHARD, D), lambda i: (0, i, 0, 0)),
        pl.BlockSpec((2, SHARD, D), lambda i: (0, 0, i)),
        pl.BlockSpec((2, SHARD, D), lambda i: (0, i, 0)),
    ]
    words, regions = (WORDS_HERE, D), (REGIONS_HERE, D)
    smalls = [(5, 3, SHARD), (3, 2, SHARD), (2, PART)]
    singles = [*smalls, words, regions, words, regions]
    return pl.pallas_call(
        finish_kernel,
        grid=(4,),
        out_shape=tuple(jax.ShapeDtypeStruct(ref.shape, FULL) for ref in (oa, ou, od))
        + tuple(jax.ShapeDtypeStruct(shape, FULL) for shape in singles),
        in_specs=[*parts, whole((32, D)), whole((ROWS, D)), whole(words), whole(regions)],
        out_specs=(*parts, *[whole(shape) for shape in singles]),
        compiler_params=pltpu.CompilerParams(vmem_limit_bytes=VMEM_BYTES),
        cost_estimate=pl.CostEstimate(flops=0, bytes_accessed=15_000_000, transcendentals=0),
        name="widen_outputs",
    )(oa, ou, od, os, dx, lo, vo)


def fast_body(
    language, vision, lengths, attn_weights, attn_vectors, ffn_up, ffn_up_bias, ffn_down, ffn_vectors,
    language_cot, vision_cot,
):
    wide = ((0, 0), (0, PART - SHARD))
    vectors = [attn_vectors[i] for i in range(3)] + [ffn_vectors[i] for i in range(2)]
    small = jnp.concatenate([jnp.pad(piece, wide) for piece in vectors] + [ffn_up_bias])
    small = jnp.pad(small, ((0, 9), (0, 0)))
    wf, uf, df, vec, ub, xlow, onelow, two, *kept = gather(
        attn_weights, ffn_up, ffn_down, small, language, vision, lengths
    )
    q0, k0, v0, m0, z0, q1, k1, v1, m1, z1 = kept
    lo, vo, d2, gu, gd, gv, gb, ax1, ax2, bx1, bx2 = feed(
        two, language_cot, vision_cot, uf.reshape(D, D), df, vec, ub, onelow, m1,
        ffn_up, ffn_down,
    )
    dx, oa, ou, od, os = backward(
        d2, lengths, vec, wf.reshape(3, 4, D, D), (q0, k0, v0, z0, q1, k1, v1, z1),
        gu.reshape(2, Z, 2 * SHARD, D), gd.reshape(2, 2, 4, SHARD, D), gv, gb,
        (xlow, m0, ax1, ax2, bx1, bx2),
    )
    wa, wu, wd, va, vf, vu, lang_grad, visn_grad, lang_out, visn_out = finish(
        oa, ou, od, os, dx, lo, vo
    )
    va, vf = va.transpose(1, 0, 2), vf.transpose(1, 0, 2)
    return (lang_out, visn_out, lang_grad, visn_grad, wa, va, wu, vu, wd, vf)


def layer_norm(values, gain, shift):
    mean = jnp.mean(values, axis=-1, keepdims=True)
    centred = values - mean
    spread = jnp.mean(centred * centred, axis=-1, keepdims=True)
    return centred * jax.lax.rsqrt(spread + 1e-06) * (1.0 + gain) + shift


def gelu_exact(values):
    return jax.nn.gelu(values, approximate=False)


def project(inputs, matrix):
    return jnp.einsum("isd,de->ise", inputs, matrix, preferred_element_type=jnp.float32)


def project_back(grads, matrix):
    return jnp.einsum("ise,de->isd", grads, matrix, preferred_element_type=jnp.float32)


def outer_sum(inputs, grads):
    return jnp.einsum("isd,ise->de", inputs, grads, preferred_element_type=jnp.float32)


def row_total(grads):
    return jnp.sum(grads.astype(jnp.float32), axis=(0, 1))


def gather_attn(attn_weights, attn_vectors, layer_index):
    return (
        lax.all_gather(attn_weights[layer_index], "fsdp", axis=1, tiled=True),
        lax.all_gather(attn_vectors[layer_index], "fsdp", axis=1, tiled=True),
    )


def regather_attn(attn_weights, attn_vectors, layer_index):
    return (
        lax.all_gather(attn_weights[layer_index], "fsdp", axis=1, tiled=True),
        lax.all_gather(attn_vectors[layer_index], "fsdp", axis=1, tiled=True),
    )


def gather_ffn(ffn_up, ffn_up_bias, ffn_down, ffn_vectors, layer_index):
    return (
        lax.all_gather(ffn_up[layer_index], "fsdp", axis=0, tiled=True),
        lax.all_gather(ffn_up_bias[layer_index], "fsdp", axis=0, tiled=True),
        lax.all_gather(ffn_down[layer_index], "fsdp", axis=0, tiled=True),
        lax.all_gather(ffn_vectors[layer_index], "fsdp", axis=1, tiled=True),
    )


def regather_ffn(ffn_up, ffn_up_bias, ffn_down, ffn_vectors, layer_index):
    return (
        lax.all_gather(ffn_up[layer_index], "fsdp", axis=0, tiled=True),
        lax.all_gather(ffn_up_bias[layer_index], "fsdp", axis=0, tiled=True),
        lax.all_gather(ffn_down[layer_index], "fsdp", axis=0, tiled=True),
        lax.all_gather(ffn_vectors[layer_index], "fsdp", axis=1, tiled=True),
    )


def settle_attn(grad_weights, grad_vector):
    shards = (
        lax.psum_scatter(grad_weights, "fsdp", scatter_dimension=1, tiled=True),
        lax.psum_scatter(grad_vector, "fsdp", scatter_dimension=1, tiled=True),
    )
    quarter = lax.psum_scatter(
        shards[0].astype(jnp.bfloat16), "rep", scatter_dimension=2, tiled=True
    ).astype(jnp.float32)
    vector_sum = lax.psum(shards[1], "rep")
    whole = lax.all_gather(quarter.astype(jnp.bfloat16), "rep", axis=2, tiled=True).astype(
        quarter.dtype
    )
    return (whole, vector_sum)


def settle_ffn(grad_up, grad_up_bias, grad_down, grad_vector):
    shards = (
        lax.psum_scatter(grad_up, "fsdp", scatter_dimension=0, tiled=True),
        lax.psum_scatter(grad_up_bias, "fsdp", scatter_dimension=0, tiled=True),
        lax.psum_scatter(grad_down, "fsdp", scatter_dimension=0, tiled=True),
        lax.psum_scatter(grad_vector, "fsdp", scatter_dimension=1, tiled=True),
    )
    quarters = (
        lax.psum_scatter(
            shards[0].astype(jnp.bfloat16), "rep", scatter_dimension=1, tiled=True
        ).astype(jnp.float32),
        lax.psum_scatter(
            shards[2].astype(jnp.bfloat16), "rep", scatter_dimension=1, tiled=True
        ).astype(jnp.float32),
    )
    smalls = lax.psum((shards[1], shards[3]), "rep")
    wholes = (
        lax.all_gather(quarters[0].astype(jnp.bfloat16), "rep", axis=1, tiled=True).astype(
            jnp.float32
        ),
        lax.all_gather(quarters[1].astype(jnp.bfloat16), "rep", axis=1, tiled=True).astype(
            jnp.float32
        ),
    )
    return (wholes[0], smalls[0], wholes[1], smalls[1])


def attend_forward(residual, query_low, key_low, weights, vector, key_bias):
    item_count, query_len, model_width = residual.shape
    key_len = key_low.shape[1]
    head_size = model_width // HEADS
    vector = vector.astype(jnp.float32)
    queries = (project(query_low, weights[0]) + vector[0]).astype(jnp.bfloat16)
    key_heads = project(key_low, weights[1]).astype(jnp.bfloat16)
    values = (project(key_low, weights[2]) + vector[1]).astype(jnp.bfloat16)
    queries = queries.reshape(item_count, query_len, HEADS, head_size)
    key_heads = key_heads.reshape(item_count, key_len, HEADS, head_size)
    values = values.reshape(item_count, key_len, HEADS, head_size)
    scores = jnp.einsum(
        "iqhd,ikhd->ihqk", queries, key_heads, preferred_element_type=jnp.float32
    ) / math.sqrt(head_size)
    scores = scores + key_bias[:, None, None, :]
    highest = jnp.max(scores, axis=-1, keepdims=True)
    exponent = jnp.exp(scores - highest)
    attn_probs = exponent / jnp.sum(exponent, axis=-1, keepdims=True)
    mixed_heads = jnp.einsum(
        "ihqk,ikhd->iqhd",
        attn_probs.astype(jnp.bfloat16),
        values,
        preferred_element_type=jnp.float32,
    )
    mixed_heads = mixed_heads.astype(jnp.bfloat16).reshape(item_count, query_len, model_width)
    pre_norm = residual + (project(mixed_heads, weights[3]) + vector[2])
    normed = layer_norm(pre_norm, vector[3], vector[4])
    return (normed, (queries, key_heads, values, attn_probs, mixed_heads, pre_norm))


def attend_backward(grad_out, query_low, key_low, weights, vector, kept):
    queries, key_heads, values, attn_probs, mixed_heads, pre_norm = kept
    item_count, query_len, head_count, head_size = queries.shape
    key_len = key_heads.shape[1]
    model_width = head_count * head_size
    vector = vector.astype(jnp.float32)
    _, pull_norm = jax.vjp(layer_norm, pre_norm, vector[3], vector[4])
    grad_pre, grad_gain, grad_shift = pull_norm(grad_out)
    grad_branch = grad_pre.astype(jnp.bfloat16)
    grad_out_weight = outer_sum(mixed_heads, grad_branch)
    grad_mixed = project_back(grad_branch, weights[3]).astype(jnp.bfloat16)
    grad_mixed = grad_mixed.reshape(item_count, query_len, head_count, head_size)
    grad_probs = jnp.einsum(
        "iqhd,ikhd->ihqk", grad_mixed, values, preferred_element_type=jnp.float32
    )
    grad_values = jnp.einsum(
        "ihqk,iqhd->ikhd",
        attn_probs.astype(jnp.bfloat16),
        grad_mixed,
        preferred_element_type=jnp.float32,
    ).astype(jnp.bfloat16)
    grad_scores = attn_probs * (
        grad_probs - jnp.sum(attn_probs * grad_probs, axis=-1, keepdims=True)
    )
    grad_scores = grad_scores.astype(jnp.bfloat16)
    inverse = 1.0 / math.sqrt(head_size)
    grad_queries = (
        jnp.einsum("ihqk,ikhd->iqhd", grad_scores, key_heads, preferred_element_type=jnp.float32)
        * inverse
    )
    grad_queries = grad_queries.astype(jnp.bfloat16).reshape(item_count, query_len, model_width)
    grad_keys = (
        jnp.einsum("ihqk,iqhd->ikhd", grad_scores, queries, preferred_element_type=jnp.float32)
        * inverse
    )
    grad_keys = grad_keys.astype(jnp.bfloat16).reshape(item_count, key_len, model_width)
    grad_values = grad_values.reshape(item_count, key_len, model_width)
    grad_weights = jnp.stack(
        [
            outer_sum(query_low, grad_queries),
            outer_sum(key_low, grad_keys),
            outer_sum(key_low, grad_values),
            grad_out_weight,
        ]
    )
    grad_vector = jnp.stack(
        [
            row_total(grad_queries),
            row_total(grad_values),
            row_total(grad_branch),
            grad_gain,
            grad_shift,
        ]
    )
    grad_query_low = project_back(grad_queries, weights[0])
    grad_key_low = project_back(grad_keys, weights[1]) + project_back(grad_values, weights[2])
    return (grad_pre, grad_query_low, grad_key_low, grad_weights, grad_vector)


def feed_forward(residual, up_weight, up_bias, down_weight, vector):
    vector = vector.astype(jnp.float32)
    residual_low = residual.astype(jnp.bfloat16)
    hidden = project(residual_low, up_weight) + up_bias.astype(jnp.float32)
    active = gelu_exact(hidden).astype(jnp.bfloat16)
    pre_norm = residual + (project(active, down_weight) + vector[0])
    normed = layer_norm(pre_norm, vector[1], vector[2])
    return (normed, (residual_low, hidden, active, pre_norm))


def feed_backward(grad_out, up_weight, down_weight, vector, kept):
    residual_low, hidden, active, pre_norm = kept
    vector = vector.astype(jnp.float32)
    _, pull_norm = jax.vjp(layer_norm, pre_norm, vector[1], vector[2])
    grad_pre, grad_gain, grad_shift = pull_norm(grad_out)
    grad_branch = grad_pre.astype(jnp.bfloat16)
    grad_down = outer_sum(active, grad_branch)
    grad_active = project_back(grad_branch, down_weight)
    _, pull_gate = jax.vjp(gelu_exact, hidden)
    grad_hidden = pull_gate(grad_active)[0].astype(jnp.bfloat16)
    grad_up = outer_sum(residual_low, grad_hidden)
    grad_up_bias = row_total(grad_hidden)
    grad_residual = grad_pre + project_back(grad_hidden, up_weight)
    grad_vector = jnp.stack([row_total(grad_branch), grad_gain, grad_shift])
    return (grad_residual, grad_up, grad_up_bias, grad_down, grad_vector)


def body(
    language,
    vision,
    lengths,
    attn_weights,
    attn_vectors,
    ffn_up,
    ffn_up_bias,
    ffn_down,
    ffn_vectors,
    language_cot,
    vision_cot,
):
    item_count = lengths.shape[0]
    model_width = language.shape[1]
    word_slots = language.shape[0] // item_count
    region_slots = vision.shape[0] // item_count
    lang_rows = language.reshape(item_count, word_slots, model_width)
    visn_rows = vision.reshape(item_count, region_slots, model_width)
    word_bias = jnp.where(
        jnp.arange(word_slots)[None, :] < lengths[:, None], 0.0, -1000000000.0
    ).astype(jnp.float32)
    region_bias = jnp.zeros((item_count, region_slots), jnp.float32)
    cross_weights, cross_vector = gather_attn(attn_weights, attn_vectors, 0)
    lang_low = lang_rows.astype(jnp.bfloat16)
    visn_low = visn_rows.astype(jnp.bfloat16)
    lang_one = attend_forward(
        lang_rows, lang_low, visn_low, cross_weights, cross_vector, region_bias
    )[0]
    visn_one = attend_forward(
        visn_rows, visn_low, lang_low, cross_weights, cross_vector, word_bias
    )[0]
    lang_self = gather_attn(attn_weights, attn_vectors, 1)
    lang_one_low = lang_one.astype(jnp.bfloat16)
    lang_two, lang_self_kept = attend_forward(
        lang_one, lang_one_low, lang_one_low, lang_self[0], lang_self[1], word_bias
    )
    visn_self = gather_attn(attn_weights, attn_vectors, 2)
    visn_one_low = visn_one.astype(jnp.bfloat16)
    visn_two, visn_self_kept = attend_forward(
        visn_one, visn_one_low, visn_one_low, visn_self[0], visn_self[1], region_bias
    )
    lang_ffn = gather_ffn(ffn_up, ffn_up_bias, ffn_down, ffn_vectors, 0)
    lang_three, lang_ffn_kept = feed_forward(
        lang_two, lang_ffn[0], lang_ffn[1], lang_ffn[2], lang_ffn[3]
    )
    visn_ffn = gather_ffn(ffn_up, ffn_up_bias, ffn_down, ffn_vectors, 1)
    visn_three, visn_ffn_kept = feed_forward(
        visn_two, visn_ffn[0], visn_ffn[1], visn_ffn[2], visn_ffn[3]
    )
    visn_ffn_back = regather_ffn(ffn_up, ffn_up_bias, ffn_down, ffn_vectors, 1)
    visn_back = feed_backward(
        vision_cot.reshape(item_count, region_slots, model_width),
        visn_ffn_back[0],
        visn_ffn_back[2],
        visn_ffn_back[3],
        visn_ffn_kept,
    )
    visn_ffn_grads = settle_ffn(visn_back[1], visn_back[2], visn_back[3], visn_back[4])
    lang_ffn_back = regather_ffn(ffn_up, ffn_up_bias, ffn_down, ffn_vectors, 0)
    lang_back = feed_backward(
        language_cot.reshape(item_count, word_slots, model_width),
        lang_ffn_back[0],
        lang_ffn_back[2],
        lang_ffn_back[3],
        lang_ffn_kept,
    )
    lang_ffn_grads = settle_ffn(lang_back[1], lang_back[2], lang_back[3], lang_back[4])
    visn_self_back = regather_attn(attn_weights, attn_vectors, 2)
    visn_attn = attend_backward(
        visn_back[0],
        visn_one_low,
        visn_one_low,
        visn_self_back[0],
        visn_self_back[1],
        visn_self_kept,
    )
    visn_self_grads = settle_attn(visn_attn[3], visn_attn[4])
    grad_visn_one = visn_attn[0] + visn_attn[1] + visn_attn[2]
    lang_self_back = regather_attn(attn_weights, attn_vectors, 1)
    lang_attn = attend_backward(
        lang_back[0],
        lang_one_low,
        lang_one_low,
        lang_self_back[0],
        lang_self_back[1],
        lang_self_kept,
    )
    lang_self_grads = settle_attn(lang_attn[3], lang_attn[4])
    grad_lang_one = lang_attn[0] + lang_attn[1] + lang_attn[2]
    cross_back = regather_attn(attn_weights, attn_vectors, 0)
    lang_cross_kept = attend_forward(
        lang_rows, lang_low, visn_low, cross_back[0], cross_back[1], region_bias
    )[1]
    visn_cross_kept = attend_forward(
        visn_rows, visn_low, lang_low, cross_back[0], cross_back[1], word_bias
    )[1]
    lang_cross = attend_backward(
        grad_lang_one, lang_low, visn_low, cross_back[0], cross_back[1], lang_cross_kept
    )
    visn_cross = attend_backward(
        grad_visn_one, visn_low, lang_low, cross_back[0], cross_back[1], visn_cross_kept
    )
    cross_grads = settle_attn(lang_cross[3] + visn_cross[3], lang_cross[4] + visn_cross[4])
    grad_language = lang_cross[0] + lang_cross[1] + visn_cross[2]
    grad_vision = visn_cross[0] + visn_cross[1] + lang_cross[2]
    return (
        lang_three.reshape(item_count * word_slots, model_width),
        visn_three.reshape(item_count * region_slots, model_width),
        grad_language.reshape(item_count * word_slots, model_width),
        grad_vision.reshape(item_count * region_slots, model_width),
        jnp.stack([cross_grads[0], lang_self_grads[0], visn_self_grads[0]]),
        jnp.stack([cross_grads[1], lang_self_grads[1], visn_self_grads[1]]),
        jnp.stack([lang_ffn_grads[0], visn_ffn_grads[0]]),
        jnp.stack([lang_ffn_grads[1], visn_ffn_grads[1]]),
        jnp.stack([lang_ffn_grads[2], visn_ffn_grads[2]]),
        jnp.stack([lang_ffn_grads[3], visn_ffn_grads[3]]),
    )


def solution(mesh):
    shape = dict(mesh.shape)
    fast = shape["rep"] == 4 and shape["fsdp"] == 8
    return jax.shard_map(
        fast_body if fast else body,
        mesh=mesh,
        in_specs=(
            P(("rep", "fsdp"), None),
            P(("rep", "fsdp"), None),
            P(("rep", "fsdp")),
            P(None, None, "fsdp", None),
            P(None, None, "fsdp"),
            P(None, "fsdp", None),
            P(None, "fsdp"),
            P(None, "fsdp", None),
            P(None, None, "fsdp"),
            P(("rep", "fsdp"), None),
            P(("rep", "fsdp"), None),
        ),
        out_specs=(
            P(("rep", "fsdp"), None),
            P(("rep", "fsdp"), None),
            P(("rep", "fsdp"), None),
            P(("rep", "fsdp"), None),
            P(None, None, "fsdp", None),
            P(None, None, "fsdp"),
            P(None, "fsdp", None),
            P(None, "fsdp"),
            P(None, "fsdp", None),
            P(None, None, "fsdp"),
        ),
        check_vma=False,
    )
```

```python
import functools
import math

import jax
import jax.numpy as jnp
from jax import lax
from jax.experimental import pallas as pl
from jax.experimental.pallas import tpu as pltpu
from jax.sharding import PartitionSpec as P

HEADS = 12
LOW = jnp.bfloat16
FULL = jnp.float32
VMEM_BYTES = 58 * 1024 * 1024
HBM = pl.BlockSpec(memory_space=pl.ANY)
ONCHIP = pl.BlockSpec(memory_space=pltpu.VMEM)


D = 768
WORDS_HERE = 80
REGIONS_HERE = 144
ROWS = WORDS_HERE + REGIONS_HERE
LANG = slice(0, WORDS_HERE)
VISN = slice(WORDS_HERE, ROWS)
EVERY = slice(0, ROWS)
ITEMS_HERE = 4
FF = 3072
PART = 384
SHARD = 96
Z = 4


def copy_to(src, dst, send, recv, device):
    return pltpu.make_async_remote_copy(
        src_ref=src,
        dst_ref=dst,
        send_sem=send,
        recv_sem=recv,
        device_id=device,
        device_id_type=pl.DeviceIdType.MESH,
    )


class Place:
    def __init__(self):
        rep, spot = lax.axis_index("rep"), lax.axis_index("fsdp")
        z = lax.div(spot, 2)
        core = spot - 2 * z
        y = lax.div(rep, 2)
        x = rep - 2 * y
        self.rep, self.spot, self.z, self.core, self.other = rep, spot, z, core, 1 - core
        along_x, along_y = (1 - x) + 2 * y, x + 2 * (1 - y)
        turn = core * (along_y - along_x)
        self.peers = [along_x + turn, along_y - turn, (1 - x) + 2 * (1 - y)]
        self.sibling = (rep, 2 * z + (1 - core))

    def peer(self, p):
        return (self.peers[p], self.spot)

    def above(self):
        return (self.rep, self.spot + 2)

    def below(self):
        return (self.rep, self.spot - 2)

    def column(self, s):
        return (self.rep, 2 * s + self.core)

    def enter(self, line):
        barrier = pltpu.get_barrier_semaphore()

        def greet(device):
            pl.semaphore_signal(
                barrier, inc=1, device_id=device, device_id_type=pl.DeviceIdType.MESH
            )

        for p in range(3):
            greet(self.peer(p))
        greet(self.sibling)
        number = 4
        if line == 1:

            @pl.when(self.z > 0)
            def _():
                greet(self.below())

            @pl.when(self.z < Z - 1)
            def _():
                greet(self.above())

            number = 4 + jnp.minimum(self.z, 1) + jnp.minimum(Z - 1 - self.z, 1)
        if line == 2:
            self.others(lambda s: greet(self.column(s)))
            number = 4 + Z - 1
        pl.semaphore_wait(barrier, number)

    def others(self, act):
        for s in (0, 3, 1, 2):

            @pl.when(s != self.z)
            def _():
                act(s)


class Chain:
    def __init__(self, at, units, slot, own, send, recv):
        self.at, self.units, self.slot, self.own = at, units, slot, own
        self.send, self.recv = send, recv

    def copy(self, index, s, source, upward):
        return copy_to(
            source, self.slot(self.units[index], s),
            self.send.at[index, s, 0 if upward else 1], self.recv.at[index, s],
            self.at.above() if upward else self.at.below(),
        )

    def send_step(self, index, k):
        z, unit = self.at.z, self.units[index]

        @pl.when((z - k >= 0) & (z < Z - 1))
        def _():
            source = self.own(unit) if k == 0 else self.slot(unit, z - k)
            self.copy(index, z - k, source, True).start()

        @pl.when((z + k <= Z - 1) & (z > 0))
        def _():
            source = self.own(unit) if k == 0 else self.slot(unit, z + k)
            self.copy(index, z + k, source, False).start()

    def come(self, k):
        z = self.at.z
        return ((z - 1 - k, z - 1 - k >= 0), (z + 1 + k, z + 1 + k <= Z - 1))

    def wait_step(self, index, k):
        for upward, (s, there) in zip((True, False), self.come(k)):

            @pl.when(there)
            def _():
                ref = self.slot(self.units[index], s)
                self.copy(index, s, ref, not upward).wait_recv()

    def finish(self):
        z = self.at.z
        for index, unit in enumerate(self.units):
            for s in range(Z):

                @pl.when((s <= z) & (z < Z - 1))
                def _():
                    self.copy(index, s, self.slot(unit, s), True).wait_send()

                @pl.when((s >= z) & (z > 0))
                def _():
                    self.copy(index, s, self.slot(unit, s), False).wait_send()


class FeedWeights:
    def __init__(self, at, up, down, dst, uf, df, sems):
        self.at, self.up, self.down = at, up, down
        self.dst, self.uf, self.df = dst, uf, df
        (
            self.usend, self.urecv, self.dsend, self.drecv, self.ulocal, self.dlocal,
            self.xsend, self.xrecv,
        ) = sems
        self.columns = pl.ds(pl.multiple_of(D * at.rep, D), D)

    def rows(self, rep):
        return pl.ds(pl.multiple_of(PART * self.at.core + SHARD * rep, SHARD), SHARD)

    def slot(self, kind, s):
        return self.uf.at[2 * s + self.at.core] if kind == "u" else self.dst.at[s]

    def own(self, kind):
        if kind == "u":
            return self.up.at[:, self.columns]
        return self.down.at[pl.ds(pl.multiple_of(SHARD * self.at.rep, SHARD), SHARD)]

    def up_across(self, s, source):
        target = self.uf.at[2 * s + self.at.core]
        return copy_to(source, target, self.usend.at[s], self.urecv.at[s], self.at.sibling)

    def up_here(self):
        target = self.uf.at[2 * self.at.z + self.at.core]
        return pltpu.make_async_copy(self.up.at[:, self.columns], target, self.ulocal)

    def down_there(self, s, source):
        return copy_to(
            source, self.df.at[self.rows(self.at.rep)],
            self.dsend.at[s], self.drecv.at[self.at.rep], (s, self.at.spot),
        )

    def down_here(self, source):
        return pltpu.make_async_copy(source, self.df.at[self.rows(self.at.rep)], self.dlocal)

    def down_across(self):
        ref = self.df.at[pl.ds(pl.multiple_of(PART * self.at.core, PART), PART)]
        return copy_to(ref, ref, self.xsend, self.xrecv, self.at.sibling)

    def pass_on(self, kind, s, source):
        if kind == "u":
            self.up_across(s, source).start()
        else:

            @pl.when(s != self.at.rep)
            def _():
                self.down_there(s, source).start()

            @pl.when(s == self.at.rep)
            def _():
                self.down_here(source).start()

    def own_start(self, kind):
        if kind == "u":
            self.up_here().start()
        self.pass_on(kind, self.at.z, self.own(kind))

    def collect(self):
        for p in range(3):
            there = self.at.peers[p]
            copy_to(
                self.dst.at[0], self.df.at[self.rows(there)],
                self.dsend.at[0], self.drecv.at[there], self.at.peer(p),
            ).wait_recv()
        self.down_here(self.dst.at[0]).wait()
        self.down_across().start()

    def finish(self):
        self.up_here().wait()
        for s in range(Z):
            self.up_across(s, self.uf.at[2 * s + self.at.core]).wait()

            @pl.when(s != self.at.rep)
            def _():
                self.down_there(s, self.dst.at[s]).wait_send()

        self.down_across().wait()


def feed_sems():
    dma = pltpu.SemaphoreType.DMA
    return [dma((Z,)), dma((Z,)), dma((Z,)), dma((Z,)), dma, dma, dma, dma]


UNITS = [("a", 0), ("s", 0), ("a", 1), ("a", 2), ("u", 1), ("d", 1)]


def gather_kernel(
    aw, up, down, small, language, vision, lengths,
    wf, uf, df, vec, ub, xlow, onelow, two, q0, k0, v0, m0, z0, q1, k1, v1, m1, z1,
    wv, dst, sf, x, one,
    zsend, zrecv, psend, precv, asend, arecv, ssend, srecv,
    alocal, slocal, wlocal, xlocal, *fsems,
):
    at = Place()
    rep, z, core = at.rep, at.z, at.core
    rows_in = [
        pltpu.make_async_copy(ref, x.at[rows], xlocal.at[i])
        for i, (ref, rows) in enumerate(
            ((language, pl.ds(0, WORDS_HERE)), (vision, pl.ds(WORDS_HERE, REGIONS_HERE)))
        )
    ]
    for copy in rows_in:
        copy.start()
    at.enter(1)
    feed_weights = FeedWeights(at, up.at[1], down.at[1], dst, uf, df, fsems)

    def slot(unit, s):
        kind, i = unit
        if kind == "a":
            return wv.at[i, rep, 2 * s + core]
        return sf.at[2 * s + core] if kind == "s" else feed_weights.slot(kind, s)

    def own(unit):
        kind, i = unit
        if kind == "a":
            return aw.at[i, rep]
        return small if kind == "s" else feed_weights.own(kind)

    chain = Chain(at, UNITS, slot, own, zsend, zrecv)

    def plane_copy(layer, s, i):
        ref = wv.at[layer, at.peers[0] if i == 2 else rep, 2 * s + core]
        there = at.peer(1) if i == 2 else at.peer(i)
        return copy_to(ref, ref, psend.at[layer, s, i], precv.at[layer, s, i], there)

    def plane_arrival(layer, s, i):
        ref = wv.at[layer, at.peers[i], 2 * s + core]
        return copy_to(ref, ref, psend.at[layer, s, i], precv.at[layer, s, i], at.peer(i))

    def small_copy(s, source):
        return copy_to(source, sf.at[2 * s + core], ssend.at[s], srecv.at[s], at.sibling)

    def pass_on(unit, s, source):
        kind, i = unit
        if kind == "a":
            for p in range(2):
                plane_copy(i, s, p).start()
        elif kind == "s":
            small_copy(s, source).start()
        else:
            feed_weights.pass_on(kind, s, source)

    def shard_here(layer):
        return pltpu.make_async_copy(aw.at[layer], wv.at[layer, :, 2 * z + core], alocal.at[layer])

    def small_here():
        return pltpu.make_async_copy(small, sf.at[2 * z + core], slocal)

    def own_start(unit):
        kind, i = unit
        if kind == "a":
            shard_here(i).start()
            copy_to(
                aw.at[i], wv.at[i, :, 2 * z + core], asend.at[i, z], arecv.at[i, z], at.sibling
            ).start()
        elif kind == "s":
            small_here().start()
            pass_on(unit, z, small)
        else:
            feed_weights.own_start(kind)

    def line_send_step(index, k):
        chain.send_step(index, k)
        if k == 0:
            own_start(UNITS[index])

    def pass_step(index, k):
        unit = UNITS[index]
        for s, there in chain.come(k):

            @pl.when(there)
            def _():
                pass_on(unit, s, slot(unit, s))

    def core_copy(layer, s):
        ref = wv.at[layer, :, 2 * s + core]
        return copy_to(ref, ref, asend.at[layer, s], arecv.at[layer, s], at.sibling)

    def core_arrival(layer, s):
        ref = wv.at[layer, :, 2 * s + at.other]
        return copy_to(ref, ref, asend.at[layer, s], arecv.at[layer, s], at.sibling)

    def relay_step(layer, k):
        for s, there in chain.come(k):

            @pl.when(there)
            def _():
                plane_arrival(layer, s, 0).wait_recv()
                plane_copy(layer, s, 2).start()

    def plane_step(layer, k):
        for s, there in chain.come(k):

            @pl.when(there)
            def _():
                plane_arrival(layer, s, 1).wait_recv()
                plane_arrival(layer, s, 2).wait_recv()
                core_copy(layer, s).start()

    count = len(UNITS)

    def exchange():
        line_send_step(0, 0)
        for time in range(count + 6):
            if time + 1 < count:
                line_send_step(time + 1, 0)
            for index, unit in enumerate(UNITS):
                k = time - index
                if 1 <= k <= 3:
                    chain.wait_step(index, k - 1)
                    if k <= 2:
                        line_send_step(index, k)
                    pass_step(index, k - 1)
                    yield time
                if unit[0] == "a" and 0 <= k - 2 <= 2:
                    relay_step(unit[1], k - 2)
                    yield time
                if unit[0] == "a" and 0 <= k - 3 <= 2:
                    plane_step(unit[1], k - 3)
                    yield time
            yield time + 1

    steps = exchange()
    clock = [0]

    def pump(times=1):
        for _ in range(times):
            clock[0] = next(steps, 99)

    def until(time):
        while clock[0] < time:
            pump()

    def ready(layer):
        until(UNITS.index(("a", layer)) + 6)
        shard_here(layer).wait()
        for s in range(Z):
            core_arrival(layer, s).wait_recv()
        pltpu.make_async_copy(wv.at[layer], wf.at[layer], wlocal.at[layer]).start()

    for copy in rows_in:
        copy.wait()
    xlow[...] = x[...].astype(LOW)
    until(UNITS.index(("s", 0)) + 4)
    small_here().wait()
    for s in range(Z):
        copy_to(
            small, sf.at[2 * s + at.other], ssend.at[s], srecv.at[s], at.sibling
        ).wait_recv()
    line = lax.broadcasted_iota(jnp.int32, (128, D), 0)
    lane = lax.broadcasted_iota(jnp.int32, (128, D), 1)
    vectors = jnp.zeros((32, D), FULL)
    for d in range(8):
        pick = ((lane == line + SHARD * d) & (line < SHARD)).astype(FULL).astype(LOW)
        vectors = vectors + dot(sf[d, :, :128], pick)
    vec[...] = vectors
    ub[...] = jnp.zeros_like(ub)
    for c in range(2):
        ub[0:2, PART * c : PART * c + PART] = sf[2 * rep + c].astype(FULL)[21:23, :]

    word_bias = length_bias(lengths, (1, WORDS_HERE), 1)
    ready(0)
    attend(
        x, xlow, wv, vec, 0, EVERY,
        [
            (LANG, VISN, pair_bias(WORDS_EACH, REGIONS_EACH, None)),
            (VISN, LANG, pair_bias(REGIONS_EACH, WORDS_EACH, word_bias)),
        ],
        q0, k0, v0, m0, z0, one, pump,
    )
    onelow[...] = one[...].astype(LOW)
    ready(1)
    attend(
        one, onelow, wv, vec, 1, LANG,
        [(LANG, LANG, pair_bias(WORDS_EACH, WORDS_EACH, word_bias))],
        q1, k1, v1, m1, z1, two, pump,
    )
    ready(2)
    attend(
        one, onelow, wv, vec, 2, VISN,
        [(VISN, VISN, pair_bias(REGIONS_EACH, REGIONS_EACH, None))],
        q1, k1, v1, m1, z1, two, pump,
    )
    until(99)
    feed_weights.collect()

    for layer in range(3):
        pltpu.make_async_copy(wv.at[layer], wf.at[layer], wlocal.at[layer]).wait()
        for s in range(Z):
            core_copy(layer, s).wait_send()

            @pl.when(s != z)
            def _():
                for i in range(3):
                    plane_copy(layer, s, i).wait_send()

    for s in range(Z):
        small_copy(s, small).wait_send()
    chain.finish()
    feed_weights.finish()


def gather(aw, up, down, small, language, vision, lengths):
    dma = pltpu.SemaphoreType.DMA
    count = len(UNITS)
    full = jax.ShapeDtypeStruct((ROWS, D), FULL)
    low = jax.ShapeDtypeStruct((ROWS, D), LOW)
    return pl.pallas_call(
        gather_kernel,
        out_shape=(
            jax.ShapeDtypeStruct((3, 4, 8, SHARD, D), LOW),
            jax.ShapeDtypeStruct((8, SHARD, D), LOW),
            jax.ShapeDtypeStruct((D, D), LOW),
            jax.ShapeDtypeStruct((32, D), FULL),
            jax.ShapeDtypeStruct((8, D), FULL),
            low, low, full,
            low, low, low, low, full,
            low, low, low, low, full,
        ),
        in_specs=[HBM] * 6 + [pl.BlockSpec(memory_space=pltpu.SMEM)],
        out_specs=(HBM,) * 3 + (ONCHIP,) * 15,
        scratch_shapes=[
            pltpu.VMEM((3, 4, 8, SHARD, D), LOW),
            pltpu.VMEM((Z, SHARD, D), LOW),
            pltpu.VMEM((8, 32, PART), LOW),
            pltpu.VMEM((ROWS, D), FULL),
            pltpu.VMEM((ROWS, D), FULL),
            dma((count, Z, 2)), dma((count, Z)),
            dma((3, Z, 3)), dma((3, Z, 3)),
            dma((3, Z)), dma((3, Z)),
            dma((Z,)), dma((Z,)),
            dma((3,)), dma, dma((3,)), dma((2,)),
            *feed_sems(),
        ],
        compiler_params=pltpu.CompilerParams(
            collective_id=0, has_side_effects=True, vmem_limit_bytes=VMEM_BYTES
        ),
        cost_estimate=pl.CostEstimate(
            flops=2_200_000_000, bytes_accessed=40_000_000, transcendentals=500_000
        ),
        name="gather_attention",
    )(aw, up, down, small, language, vision, lengths)


def dot(a, b):
    return jnp.dot(a, b, preferred_element_type=FULL)


def dot_t(a, b):
    return lax.dot_general(a, b, (((1,), (1,)), ((), ())), preferred_element_type=FULL)


def t_dot(a, b):
    return lax.dot_general(a, b, (((0,), (0,)), ((), ())), preferred_element_type=FULL)


def column_sum(a):
    return jnp.sum(a.astype(FULL), axis=0, keepdims=True)


def norm_stats(pre):
    mean = jnp.mean(pre, axis=-1, keepdims=True)
    centred = pre - mean
    spread = jnp.mean(centred * centred, axis=-1, keepdims=True)
    scale = lax.rsqrt(spread + 1e-06)
    return centred * scale, scale


def norm_back(grad, unit, scale, gain):
    flow = grad * (1.0 + gain)
    return (
        flow
        - jnp.mean(flow, axis=-1, keepdims=True)
        - unit * jnp.mean(flow * unit, axis=-1, keepdims=True)
    ) * scale


def item_of(index, size):
    return sum((index >= size * k).astype(jnp.int32) for k in range(1, ITEMS_HERE))


def pair_bias(query_size, key_size, key_bias):
    shape = (query_size * ITEMS_HERE, key_size * ITEMS_HERE)
    query_item = item_of(lax.broadcasted_iota(jnp.int32, shape, 0), query_size)
    key_item = item_of(lax.broadcasted_iota(jnp.int32, shape, 1), key_size)
    bias = jnp.where(query_item == key_item, 0.0, -1e30)
    return bias if key_bias is None else bias + key_bias


GROUP = 4


def head_masks(dtype):
    lane = lax.broadcasted_iota(jnp.int32, (1, 64 * GROUP), 1)
    return [
        ((lane >= 64 * i) & (lane < 64 * i + 64)).astype(FULL).astype(dtype) for i in range(GROUP)
    ]


def stacked(value):
    return jnp.concatenate([value * mask for mask in head_masks(LOW)], axis=0)


def unstacked(value, rows):
    value = value.reshape(GROUP, rows, 64 * GROUP)
    return sum(value[i] * mask for i, mask in enumerate(head_masks(FULL)))


def mix_heads(q_ref, k_ref, v_ref, m_ref, qrows, krows, bias, pump):
    nq, nk = qrows.stop - qrows.start, krows.stop - krows.start
    for group in range(HEADS // GROUP):
        lanes = slice(256 * group, 256 * group + 256)
        query, keys, values = q_ref[qrows, lanes], k_ref[krows, lanes], v_ref[krows, lanes]
        scores = dot_t(stacked(query), keys).reshape(GROUP, nq, nk) * 0.125 + bias[None]
        exponent = jnp.exp(scores - jnp.max(scores, axis=-1, keepdims=True))
        probs = exponent / jnp.sum(exponent, axis=-1, keepdims=True)
        mixed = dot(probs.astype(LOW).reshape(GROUP * nq, nk), values)
        m_ref[qrows, lanes] = unstacked(mixed, nq).astype(LOW)
        pump()


def head_back(q_ref, k_ref, v_ref, dm_ref, dq_ref, dk_ref, dv_ref, qrows, krows, bias, group, base):
    nq, nk = qrows.stop - qrows.start, krows.stop - krows.start
    lanes = slice(256 * group, 256 * group + 256)
    query, keys, values = q_ref[qrows, lanes], k_ref[krows, lanes], v_ref[krows, lanes]
    grad = dm_ref[qrows, lanes]
    keys = stacked(keys)
    scores = dot_t(keys, query).reshape(GROUP, nk, nq) * 0.125 + bias[None]
    exponent = jnp.exp(scores - jnp.max(scores, axis=1, keepdims=True))
    probs = exponent / jnp.sum(exponent, axis=1, keepdims=True)
    dp = dot_t(stacked(values), grad).reshape(GROUP, nk, nq)
    ds = probs * (dp - jnp.sum(probs * dp, axis=1, keepdims=True))
    ds = ds.astype(LOW).reshape(GROUP * nk, nq)
    dv = unstacked(dot(probs.astype(LOW).reshape(GROUP * nk, nq), grad), nk)
    dk = unstacked(dot(ds, query), nk) * 0.125
    dq = t_dot(ds, keys) * 0.125
    qhere = slice(qrows.start - base, qrows.stop - base)
    khere = slice(krows.start - base, krows.stop - base)
    dq_ref[qhere, lanes] = dq.astype(LOW)
    dk_ref[khere, lanes] = dk.astype(LOW)
    dv_ref[khere, lanes] = dv.astype(LOW)


def row_of(ref, i):
    return ref[i : i + 1, :]


def attend(
    x_ref, low_ref, w_ref, vec_ref, layer, rows, parts, q_ref, k_ref, v_ref, m_ref, z_ref, out_ref, pump
):
    low = low_ref[rows, :]
    vec = [row_of(vec_ref, 5 * layer + i) for i in range(5)]

    def matrix(m):
        return w_ref[layer, m].reshape(D, D)

    q_ref[rows, :] = (dot(low, matrix(0)) + vec[0]).astype(LOW)
    k_ref[rows, :] = dot(low, matrix(1)).astype(LOW)
    pump()
    v_ref[rows, :] = (dot(low, matrix(2)) + vec[1]).astype(LOW)
    for qrows, krows, bias in parts:
        mix_heads(q_ref, k_ref, v_ref, m_ref, qrows, krows, bias, pump)
    pre = x_ref[rows, :] + (dot(m_ref[rows, :], matrix(3)) + vec[2])
    z_ref[rows, :] = pre
    unit, _ = norm_stats(pre)
    out_ref[rows, :] = unit * (1.0 + vec[3]) + vec[4]
    pump()


WORDS_EACH = WORDS_HERE // ITEMS_HERE
REGIONS_EACH = REGIONS_HERE // ITEMS_HERE


def length_bias(lengths, shape, axis):
    index = lax.broadcasted_iota(jnp.int32, shape, axis)
    item = item_of(index, WORDS_EACH)
    real = sum(jnp.where(item == i, lengths[i], 0) for i in range(ITEMS_HERE))
    return jnp.where(index - WORDS_EACH * item < real, 0.0, -1000000000.0)


STREAMS = (1, 0)
CHUNKS = ((1, WORDS_HERE, 64), (1, WORDS_HERE + 64, 80), (0, 0, WORDS_HERE))
SELF_ROWS = (pl.ds(0, WORDS_HERE), pl.ds(WORDS_HERE, REGIONS_HERE))
PIECES = ((0, 0, 48), (0, 48, 32), (1, 0, 48), (1, 48, 48), (1, 96, 48))


def ffn_kernel(
    x2, lang_cot, visn_cot, uw1, dw1, vec, ub, onelow, m1, up, down,
    lang_out, visn_out, d2, gu, gd, gv, gb, ax1, ax2, bx1, bx2,
    *scratch,
):
    at = Place()
    rep, z, core = at.rep, at.z, at.core
    scratch = list(scratch)

    def take(count):
        some, scratch[:] = scratch[:count], scratch[count:]
        return some

    many = len(CHUNKS)
    xg, bg, ht, gt, hd, mine, dz = [take(many) for _ in range(7)]
    stage, land = [[take(many) for _ in range(2)] for _ in range(2)]
    uw0, dw0, dst = take(3)
    psend, precv, osend, orecv, olocal, bsend, brecv = take(7)
    zsend, zrecv = take(2)
    at.enter(1)
    feed_weights = FeedWeights(at, up.at[0], down.at[0], dst, uw0, dw0, scratch)

    chain = Chain(at, "ud", feed_weights.slot, feed_weights.own, zsend, zrecv)

    def weights_step(k):
        for index, kind in enumerate("ud"):
            if k > 0:
                chain.wait_step(index, k - 1)
            if k < 3:
                chain.send_step(index, k)
            if k == 0:
                feed_weights.own_start(kind)
            else:
                for s, there in chain.come(k - 1):

                    @pl.when(there)
                    def _():
                        feed_weights.pass_on(kind, s, feed_weights.slot(kind, s))

    def up_weight(t, lanes=slice(0, D)):
        return uw1[:, lanes] if t else uw0[:, :, lanes].reshape(D, lanes.stop - lanes.start)

    def down_weight(t, rows=slice(0, D)):
        return (dw1 if t else dw0)[rows, :]

    def plane_copy(which, i, hop, buffer):
        ref = buffer.at[at.peers[0] if hop == 2 else rep]
        there = at.peer(1) if hop == 2 else at.peer(hop)
        return copy_to(ref, ref, psend.at[which, i, hop], precv.at[which, i, hop], there)

    def plane_arrival(which, i, hop, buffer):
        ref = buffer.at[at.peers[hop]]
        return copy_to(ref, ref, psend.at[which, i, hop], precv.at[which, i, hop], at.peer(hop))

    def gather_start(which, i, buffer):
        for hop in range(2):
            plane_copy(which, i, hop, buffer).start()

    def gather_relay(which, i, buffer):
        plane_arrival(which, i, 0, buffer).wait_recv()
        plane_copy(which, i, 2, buffer).start()

    def gather_rest(which, i, buffer):
        for hop in (1, 2):
            plane_arrival(which, i, hop, buffer).wait_recv()

    def gather_sent(which, i, buffer):
        for hop in range(3):
            plane_copy(which, i, hop, buffer).wait_send()

    def first_copy(turn, i):
        return copy_to(
            stage[turn][i].at[pl.ds(0, 2)], land[turn][i].at[pl.ds(0, 2)],
            psend.at[2 * turn + 1, i, 0], precv.at[2 * turn + 1, i, 0], at.peer(0),
        )

    def second_copy(turn, i):
        return copy_to(
            stage[turn][i].at[2], land[turn][i].at[2],
            psend.at[2 * turn + 1, i, 1], precv.at[2 * turn + 1, i, 1], at.peer(1),
        )

    def return_first(turn, i):
        for hop, p in enumerate((0, 2)):
            stage[turn][i][hop] = mine[i][at.peers[p]].astype(LOW)
        first_copy(turn, i).start()

    def return_second(turn, i):
        first_copy(turn, i).wait_recv()
        passed = land[turn][i][1].astype(FULL)
        stage[turn][i][2] = (mine[i][at.peers[1]] + passed).astype(LOW)
        second_copy(turn, i).start()

    def summed(turn, i):
        second_copy(turn, i).wait_recv()
        passed = land[turn][i][0].astype(FULL) + land[turn][i][2].astype(FULL)
        return mine[i][rep] + passed

    def flat(ref):
        value = ref[...]
        return value.reshape(value.shape[0] * value.shape[1], value.shape[2])

    blocks = [slice(256 * k, 256 * k + 256) for k in range(3)]

    def up_and_down(i):
        t, _, count = CHUNKS[i]
        rows = flat(xg[i])
        hidden = dot(rows, up_weight(t, blocks[0]))
        for k, block in enumerate(blocks):
            ahead = dot(rows, up_weight(t, blocks[k + 1])) if k < 2 else None
            hidden = hidden + ub[t : t + 1, block]
            below = 0.5 * (1.0 + lax.erf(hidden * (1.0 / math.sqrt(2.0))))
            gt[i][:, block] = (hidden * below).astype(LOW)
            ht[i][:, block] = below + hidden * (
                jnp.exp(-0.5 * hidden * hidden) * (1.0 / math.sqrt(2.0 * math.pi))
            )
            hidden = ahead
        mine[i][...] = dot(gt[i][...], down_weight(t)).reshape(4, count, D)

    def rows_back(i):
        t, _, count = CHUNKS[i]
        rows = flat(bg[i])
        for block in blocks:
            grad = dot_t(rows, down_weight(t, block)) * ht[i][:, block]
            hd[i][:, block] = grad.astype(LOW)
        mine[i][...] = dot_t(hd[i][...], up_weight(t)).reshape(4, count, D)

    def weights_back(t):
        pieces = [i for i in range(many) if CHUNKS[i][0] == t]
        for block in blocks:
            gd[t, block, :] = sum(t_dot(gt[i][:, block], flat(bg[i])) for i in pieces).astype(LOW)
            gu[t, block, :] = sum(t_dot(flat(xg[i])[:, block], hd[i][...]) for i in pieces).astype(LOW)
        total = sum(column_sum(hd[i][...]) for i in pieces)
        row = lax.broadcasted_iota(jnp.int32, (Z, D), 0)
        gb[Z * t : Z * t + Z, :] = jnp.where(row == rep, jnp.broadcast_to(total, (Z, D)), 0.0)

    def chunk_rows(i):
        t, start, count = CHUNKS[i]
        here = start - WORDS_HERE * t
        return slice(start, start + count), slice(here, here + count)

    def norm_turn(i):
        t = CHUNKS[i][0]
        rows, here = chunk_rows(i)
        bias, gain, shift = [row_of(vec, 15 + 3 * t + k) for k in range(3)]
        pre = x2[rows, :] + (summed(0, i) + bias)
        unit, scale = norm_stats(pre)
        (lang_out, visn_out)[t][here, :] = unit * (1.0 + gain) + shift
        grad = (lang_cot, visn_cot)[t][here, :]
        dz[i][...] = norm_back(grad, unit, scale, gain)
        branch = dz[i][...].astype(LOW)
        bg[i][rep] = branch
        gather_start(2, i, bg[i])
        for k, value in enumerate((column_sum(branch), column_sum(grad * unit), column_sum(grad))):
            gv[3 * t + k : 3 * t + k + 1, :] += value

    landed, across = (ax1, ax2), (bx1, bx2)

    def operand_copy(source, piece, p):
        k, first, count = PIECES[piece]
        return copy_to(
            source.at[pl.ds(WORDS_HERE * k + first, count)],
            landed[k].at[rep, pl.ds(first, count)],
            osend.at[piece, p], orecv.at[piece, p], at.peer(p),
        )

    def operand_here(source, k):
        return pltpu.make_async_copy(source.at[SELF_ROWS[k]], landed[k].at[rep], olocal.at[k])

    def across_copy(k):
        return copy_to(landed[k], across[k], bsend.at[k], brecv.at[k], at.sibling)

    def operand_send(piece, p):
        @pl.when(at.peers[p] != 3)
        def _():
            operand_copy(onelow, piece, p).start()

        @pl.when(at.peers[p] == 3)
        def _():
            operand_copy(m1, piece, p).start()

    def operands_start():
        for k in range(2):

            @pl.when(rep != 3)
            def _():
                operand_here(onelow, k).start()

            @pl.when(rep == 3)
            def _():
                operand_here(m1, k).start()

    def operands_across(k):
        operand_here(m1, k).wait()
        for piece, (which, first, count) in enumerate(PIECES):
            if which == k:
                for p in range(3):
                    ref = landed[k].at[at.peers[p], pl.ds(first, count)]
                    copy_to(
                        ref, ref, osend.at[piece, p], orecv.at[piece, p], at.peer(p)
                    ).wait_recv()
        across_copy(k).start()

    gv[...] = jnp.zeros_like(gv)
    for i in range(many):
        xg[i][rep] = x2[chunk_rows(i)[0], :].astype(LOW)
        gather_start(0, i, xg[i])
    weights_step(0)
    operands_start()
    gather_relay(0, 0, xg[0])
    gather_rest(0, 0, xg[0])
    gather_relay(0, 1, xg[1])
    up_and_down(0)
    return_first(0, 0)
    weights_step(1)
    gather_relay(0, 2, xg[2])
    gather_rest(0, 1, xg[1])
    operand_send(0, 0)
    operand_send(0, 1)
    up_and_down(1)
    return_second(0, 0)
    return_first(0, 1)
    weights_step(2)
    gather_rest(0, 2, xg[2])
    norm_turn(0)
    weights_step(3)
    return_second(0, 1)
    feed_weights.collect()
    feed_weights.finish()
    operand_send(0, 2)
    operand_send(1, 0)
    operand_send(1, 1)
    up_and_down(2)
    return_first(0, 2)
    gather_relay(2, 0, bg[0])
    norm_turn(1)
    return_second(0, 2)
    gather_rest(2, 0, bg[0])
    operand_send(1, 2)
    operand_send(2, 0)
    operand_send(2, 1)
    rows_back(0)
    return_first(1, 0)
    gather_relay(2, 1, bg[1])
    norm_turn(2)
    gather_rest(2, 1, bg[1])
    operand_send(2, 2)
    operand_send(3, 0)
    operand_send(3, 1)
    rows_back(1)
    return_second(1, 0)
    return_first(1, 1)
    gather_relay(2, 2, bg[2])
    gather_rest(2, 2, bg[2])
    operand_send(3, 2)
    operand_send(4, 0)
    operand_send(4, 1)
    rows_back(2)
    return_second(1, 1)
    return_first(1, 2)
    operand_send(4, 2)
    operands_across(0)
    weights_back(1)
    return_second(1, 2)
    operands_across(1)
    weights_back(0)
    for i in range(many):
        d2[chunk_rows(i)[0], :] = dz[i][...] + summed(1, i)
    chain.finish()
    for k in range(2):
        across_copy(k).wait()
    for k in range(2):
        for p in range(3):
            for piece, (which, _, _) in enumerate(PIECES):
                if which == k:
                    operand_copy(m1, piece, p).wait_send()
    for i in range(many):
        gather_sent(0, i, xg[i])
        gather_sent(2, i, bg[i])
        for turn in range(2):
            first_copy(turn, i).wait_send()
            second_copy(turn, i).wait_send()


def feed(x2, lang_cot, visn_cot, uw1, dw1, vec, ub, onelow, m1, up, down):
    dma = pltpu.SemaphoreType.DMA
    many = len(CHUNKS)

    def each(lead, width, dtype):
        return [pltpu.VMEM((*lead, chunk[2], width), dtype) for chunk in CHUNKS]

    def each_flat(width, dtype):
        return [pltpu.VMEM((4 * chunk[2], width), dtype) for chunk in CHUNKS]

    def rows_of_plane(count):
        return jax.ShapeDtypeStruct((4, count, D), LOW)

    return pl.pallas_call(
        ffn_kernel,
        out_shape=(
            jax.ShapeDtypeStruct((WORDS_HERE, D), FULL),
            jax.ShapeDtypeStruct((REGIONS_HERE, D), FULL),
            jax.ShapeDtypeStruct((ROWS, D), FULL),
            jax.ShapeDtypeStruct((2, D, D), LOW),
            jax.ShapeDtypeStruct((2, D, D), LOW),
            jax.ShapeDtypeStruct((8, D), FULL),
            jax.ShapeDtypeStruct((8, D), FULL),
            rows_of_plane(WORDS_HERE), rows_of_plane(REGIONS_HERE),
            rows_of_plane(WORDS_HERE), rows_of_plane(REGIONS_HERE),
        ),
        in_specs=[ONCHIP] * 7 + [HBM] * 4,
        out_specs=(ONCHIP,) * 7 + (HBM,) * 4,
        scratch_shapes=each((4,), D, LOW)
        + each((4,), D, LOW)
        + each_flat(D, FULL)
        + each_flat(D, LOW)
        + each_flat(D, LOW)
        + each((4,), D, FULL)
        + each((), D, FULL)
        + each((3,), D, LOW) * 2
        + each((3,), D, LOW) * 2
        + [
            pltpu.VMEM((8, SHARD, D), LOW),
            pltpu.VMEM((D, D), LOW),
            pltpu.VMEM((Z, SHARD, D), LOW),
            dma((4, many, 3)), dma((4, many, 3)),
            dma((5, 3)), dma((5, 3)), dma((2,)), dma((2,)), dma((2,)),
            dma((2, Z, 2)), dma((2, Z)), *feed_sems(),
        ],
        compiler_params=pltpu.CompilerParams(
            collective_id=1, has_side_effects=True, vmem_limit_bytes=VMEM_BYTES
        ),
        cost_estimate=pl.CostEstimate(
            flops=6_400_000_000, bytes_accessed=12_000_000, transcendentals=1_400_000
        ),
        name="feed_forward",
    )(x2, lang_cot, visn_cot, uw1, dw1, vec, ub, onelow, m1, up, down)


def turned_bias(query_size, key_size, key_bias):
    shape = (key_size * ITEMS_HERE, query_size * ITEMS_HERE)
    key_item = item_of(lax.broadcasted_iota(jnp.int32, shape, 0), key_size)
    query_item = item_of(lax.broadcasted_iota(jnp.int32, shape, 1), query_size)
    bias = jnp.where(query_item == key_item, 0.0, -1e30)
    return bias if key_bias is None else bias + key_bias


LAYER_ROWS = (EVERY, LANG, VISN)
WIDE_UNITS = 5


def backward_kernel(
    d2, lengths, vec, w, q0, k0, v0, z0, q1, k1, v1, z1, gu, gd, gv, gb,
    xlow, m0, ax1, ax2, bx1, bx2,
    dx, oa, ou, od, os,
    wbuf, xa0, xa1, xa2, ys0, ys1, ys2, ya0, ya1, ya2, yb0, yb1, yb2,
    share, gou, gsu, god, gsd, dland, zwide, zlow, rwide, rlow, edge, wide, final, d1, dm, gs, s0, s1, s2, s3, s4, scol,
    wsem, asem, ysend, yrecv, yfsend, yfrecv,
    dsend, drecv, dlocal, wsend, wrecv, lsend, lrecv, rsend, rrecv, esend, erecv,
    gsend, grecv, glocal, ssend, srecv, osend, orecv, olocal, bsend, brecv, hsend, hrecv, hlocal,
):
    at = Place()
    rep, z, core, other = at.rep, at.z, at.core, at.other
    own_half = pl.ds(pl.multiple_of(PART * core, PART), PART)
    other_half = pl.ds(pl.multiple_of(PART * other, PART), PART)
    xa, xin = (xa0, xa1, xa2), (None, (ax1, bx1), (ax2, bx2))
    ys, ya, yb = (ys0, ys1, ys2), (ya0, ya1, ya2), (yb0, yb1, yb2)

    def load(layer):
        return pltpu.make_async_copy(w.at[layer], wbuf.at[layer], wsem.at[layer])

    def load_rows(layer, side):
        return pltpu.make_async_copy(
            xin[layer][side], xa[layer].at[side], asem.at[layer, side]
        )

    for layer in (1, 2, 0):
        load(layer).start()
    for layer in (1, 2):
        for side in range(2):
            load_rows(layer, side).start()
    at.enter(2)

    def operand_copy(source, p):
        return copy_to(source, xa0.at[0, rep], osend.at[p], orecv.at[p], at.peer(p))

    def operand_across():
        return copy_to(xa0.at[0], xa0.at[1], bsend, brecv, at.sibling)

    def operand_flow():
        for p in (2, 0, 1):

            @pl.when(at.peers[p] != 3)
            def _():
                operand_copy(xlow, p).start()

            @pl.when(at.peers[p] == 3)
            def _():
                operand_copy(m0, p).start()

        @pl.when(rep != 3)
        def _():
            pltpu.make_async_copy(xlow, xa0.at[0, rep], olocal).start()

        @pl.when(rep == 3)
        def _():
            pltpu.make_async_copy(m0, xa0.at[0, rep], olocal).start()

        yield
        pltpu.make_async_copy(m0, xa0.at[0, rep], olocal).wait()
        for p in range(3):
            copy_to(
                m0, xa0.at[0, at.peers[p]], osend.at[p], orecv.at[p], at.peer(p)
            ).wait_recv()
        operand_across().start()

    def y_copy(layer, p):
        return copy_to(
            ys[layer].at[at.peers[p]], ya[layer].at[rep],
            ysend.at[layer, p], yrecv.at[layer, p], at.peer(p),
        )

    def y_forward(layer, i):
        there = rep if i == 3 else at.peers[i]
        return copy_to(
            ya[layer].at[there, :, other_half], yb[layer].at[there],
            yfsend.at[layer, i], yfrecv.at[layer, i], at.sibling,
        )

    def y_arrival(layer, p):
        return copy_to(
            ys[layer].at[0], ya[layer].at[at.peers[p]],
            ysend.at[layer, p], yrecv.at[layer, p], at.peer(p),
        )

    def share_of(unit, s):
        if unit < 3:
            return share.at[unit, s]
        return gou.at[unit - 3, s] if unit < 5 else dland.at[unit - 5, s]

    def slot_of(unit, s):
        return zwide.at[unit, s] if unit < 5 else zlow.at[unit - 5, s]

    def stop_of(unit):
        return rwide.at[unit] if unit < 5 else rlow.at[unit - 5]

    def column_copy(unit, s, source):
        return copy_to(source, slot_of(unit, z), wsend.at[unit, s], wrecv.at[unit, z], at.column(s))

    def column_arrival(unit, s):
        ref = slot_of(unit, s)
        return copy_to(ref, ref, wsend.at[unit, s], wrecv.at[unit, s], at.column(s))

    def stop_copy(unit):
        far = lax.div(z, 3)
        return copy_to(
            share_of(unit, 2 - far), stop_of(unit),
            rsend.at[unit], rrecv.at[unit], at.column(1 + far),
        )

    def stop_arrival(unit):
        ref = stop_of(unit)
        return copy_to(ref, ref, rsend.at[unit], rrecv.at[unit], at.column(3 * (z - 1)))

    is_end = (z == 0) | (z == Z - 1)
    is_middle = (z > 0) & (z < Z - 1)
    straight = (z > 0, z == 0, z == Z - 1, z < Z - 1)

    def from_layer(s):
        return ((z != s) & is_end) | (is_middle & ((z == s + 1) | (z == s - 1)))

    def column_start(unit):
        @pl.when(is_end)
        def _():
            stop_copy(unit).start()

        for s in (3, 0, 1, 2):

            @pl.when(straight[s])
            def _():
                column_copy(unit, s, share_of(unit, s)).start()

        slot_of(unit, z)[...] = share_of(unit, z)[...]

    def column_stop(unit):
        @pl.when(is_middle)
        def _():
            stop_arrival(unit).wait_recv()
            ref = stop_of(unit)
            ref[...] = (ref[...].astype(FULL) + share_of(unit, 3 - z)[...].astype(FULL)).astype(LOW)
            column_copy(unit, 3 - z, ref).start()

    def column_sum_of(unit):
        for s in range(Z):

            @pl.when(from_layer(s))
            def _():
                column_arrival(unit, s).wait_recv()

        total = slot_of(unit, 0)[...].astype(FULL)
        for s in range(1, Z):
            total = total + slot_of(unit, s)[...].astype(FULL)
        return total.astype(LOW)

    for edge_z, s in ((1, 3), (2, 0)):

        @pl.when(z == edge_z)
        def _():
            for unit in range(7):
                ref = slot_of(unit, s)
                ref[...] = jnp.zeros_like(ref)

    def landing(unit, there):
        if unit < 3:
            return oa.at[unit, there]
        if unit < 5:
            return ou.at[unit - 3, :, pl.ds(pl.multiple_of(D * there, D), D)]
        return od.at[unit - 5, pl.ds(pl.multiple_of(SHARD * there, SHARD), SHARD)]

    def source_of(unit):
        return wide.at[unit] if unit < 5 else final.at[unit - 5]

    def share_copy(unit, i):
        there = at.peers[0] if i == 2 else rep
        return copy_to(
            landing(unit, there) if i == 2 else source_of(unit), landing(unit, there),
            gsend.at[unit, i], grecv.at[unit, i], at.peer(1) if i == 2 else at.peer(i),
        )

    def share_arrival(unit, i):
        ref = landing(unit, at.peers[i])
        return copy_to(ref, ref, gsend.at[unit, i], grecv.at[unit, i], at.peer(i))

    def share_out(unit):
        for i in range(2):
            share_copy(unit, i).start()
        pltpu.make_async_copy(source_of(unit), landing(unit, rep), glocal.at[unit]).start()
        yield
        share_arrival(unit, 0).wait_recv()
        share_copy(unit, 2).start()

    def edge_copy(unit):
        return copy_to(
            edge.at[unit, pl.ds(pl.multiple_of(SHARD * other, SHARD), SHARD)],
            wide.at[unit, :, own_half], esend.at[unit], erecv.at[unit], at.sibling,
        )

    def wide_end(unit):
        column_stop(unit)
        yield
        edge[unit] = column_sum_of(unit)
        edge_copy(unit).start()
        wide[unit, :, own_half] = edge[unit, pl.ds(pl.multiple_of(SHARD * core, SHARD), SHARD), :]
        yield
        edge_copy(unit).wait_recv()
        yield from share_out(unit)

    def half_of(kind, t, side):
        if kind:
            return gd.at[t, side]
        return gu.at[t, :, :, pl.ds(pl.multiple_of(PART * side, PART), PART)]

    def half_across(kind, t):
        return copy_to(
            half_of(kind, t, other), (gsu, gsd)[kind].at[t],
            hsend.at[kind, t], hrecv.at[kind, t], at.sibling,
        )

    def half_here(kind, t):
        return pltpu.make_async_copy(
            half_of(kind, t, core), (gou, god)[kind].at[t], hlocal.at[kind, t]
        )

    def half_start(kind, t):
        half_across(kind, t).start()
        half_here(kind, t).start()

    def half_sum(kind, t):
        half_across(kind, t).wait_recv()
        half_here(kind, t).wait()
        ours, theirs = ((gou, gsu), (god, gsd))[kind]
        ours[t] = (ours[t].astype(FULL) + theirs[t].astype(FULL)).astype(LOW)

    def up_flow(t):
        half_start(0, t)
        yield
        half_sum(0, t)
        column_start(3 + t)
        yield
        yield from wide_end(3 + t)

    def down_copy(t, p):
        return copy_to(
            god.at[t, at.peers[p]], dland.at[t, rep], dsend.at[t, p], drecv.at[t, p], at.peer(p)
        )

    def down_arrival(t, p):
        return copy_to(
            god.at[t, rep], dland.at[t, at.peers[p]], dsend.at[t, p], drecv.at[t, p], at.peer(p)
        )

    def down_here(t):
        return pltpu.make_async_copy(god.at[t, rep], dland.at[t, rep], dlocal.at[t])

    def down_flow(t):
        half_start(1, t)
        yield
        half_sum(1, t)
        for p in range(3):
            down_copy(t, p).start()
        down_here(t).start()
        yield
        for p in range(3):
            down_arrival(t, p).wait_recv()
        down_here(t).wait()
        column_start(5 + t)
        yield
        column_stop(5 + t)
        yield
        final[t] = column_sum_of(5 + t)
        yield from share_out(5 + t)

    def flat(value):
        return value.reshape(value.shape[0] * value.shape[1], value.shape[2])

    words, regions = pl.ds(0, WORDS_HERE), pl.ds(WORDS_HERE, REGIONS_HERE)
    pieces = (
        ((0, words), (1, regions), (2, regions), (3, pl.ds(0, ROWS))),
        ((0, regions), (1, words), (2, words)),
    )

    def piece_each(turn, act):
        for p in (2, 0, 1):
            for m, rows in pieces[turn]:

                @pl.when(at.peers[p] == m)
                def _():
                    act(
                        copy_to(
                            ys0.at[m, rows], ya0.at[rep, rows],
                            ysend.at[3 * turn, p], yrecv.at[3 * turn, p], at.peer(p),
                        )
                    )

    def piece_arrivals(p):
        for turn in range(2):
            for m, rows in pieces[turn]:

                @pl.when(rep == m)
                def _():
                    ref = ya0.at[at.peers[p], rows]
                    copy_to(
                        ref, ref, ysend.at[3 * turn, p], yrecv.at[3 * turn, p], at.peer(p)
                    ).wait_recv()

    def y_flow(layer):
        if layer == 0:
            piece_each(0, lambda copy: copy.start())
            yield
            piece_each(1, lambda copy: copy.start())
        else:
            for p in (2, 0, 1):
                y_copy(layer, p).start()
        ya[layer][rep] = ys[layer][rep]
        y_forward(layer, 3).start()
        yield
        for p in range(3):
            if layer == 0:
                piece_arrivals(p)
            else:
                y_arrival(layer, p).wait_recv()
            y_forward(layer, p).start()
        yield
        if layer > 0:
            for side in range(2):
                load_rows(layer, side).wait()
        else:
            operand_across().wait_recv()
        grad = t_dot(flat(xa[layer][0]), flat(ya[layer][:, :, own_half]))
        for i in range(4):
            y_forward(layer, i).wait_recv()
        grad = grad + t_dot(flat(xa[layer][1]), flat(yb[layer][...]))
        share[layer] = grad.astype(LOW).reshape(Z, 2 * SHARD, PART)
        column_start(layer)
        yield
        yield from wide_end(layer)

    small_ways = (at.sibling, at.peer(0), at.peer(1))
    small_from = (gs, s1, s2)
    small_land = (s0, s3, s4)

    def small_copy(i):
        return copy_to(small_from[i], small_land[i], ssend.at[i], srecv.at[i], small_ways[i])

    def small_line(s):
        return copy_to(scol.at[z], scol.at[z], ssend.at[3 + s], srecv.at[3 + z], at.column(s))

    def small_arrival(s):
        return copy_to(scol.at[s], scol.at[s], ssend.at[3 + s], srecv.at[3 + s], at.column(s))

    def small_flow():
        small_copy(0).start()
        yield
        small_copy(0).wait_recv()
        s1[...] = gs[...] + s0[...]
        small_copy(1).start()
        yield
        small_copy(1).wait_recv()
        s2[...] = s1[...] + s3[...]
        small_copy(2).start()
        yield
        small_copy(2).wait_recv()
        scol[z] = s2[...] + s4[...]
        for s in range(Z):

            @pl.when(s != z)
            def _():
                small_line(s).start()

        yield
        for s in range(Z):

            @pl.when(s != z)
            def _():
                small_arrival(s).wait_recv()

        os[...] = (scol[0] + scol[1]) + (scol[2] + scol[3])

    u0, u1, w0, w1, y0, y1, y2, sm, xm = range(9)
    flows = [
        up_flow(0), up_flow(1), down_flow(0), down_flow(1),
        y_flow(0), y_flow(1), y_flow(2), small_flow(), operand_flow(),
    ]

    def go(*names):
        for name in names:
            next(flows[name], None)

    gs[...] = jnp.zeros_like(gs)
    gs[15:21, :] = gv[0:6, :]
    gs[21:29, :] = gb[...]

    def attend_back(grad, layer, parts, q, k, v, zs, dx_ref, marks):
        rows = LAYER_ROWS[layer]
        vecs = [row_of(vec, 5 * layer + i) for i in range(5)]
        unit, scale = norm_stats(zs[rows, :])
        dz = norm_back(grad, unit, scale, vecs[3])
        branch = dz.astype(LOW)
        out = ys[layer]
        out[3] = branch
        for i, value in enumerate(
            (column_sum(branch), column_sum(grad * unit), column_sum(grad))
        ):
            gs[5 * layer + 2 + i : 5 * layer + 3 + i, :] = value
        dx_ref[rows, :] = dz
        load(layer).wait()
        dm[rows, :] = dot_t(branch, wbuf[layer, 3]).astype(LOW)
        go(*marks[0])
        for (qrows, krows, pair_mask), mark in zip(parts, marks[1]):
            for group in range(HEADS // GROUP):
                head_back(
                    q, k, v, dm, out.at[0], out.at[1], out.at[2],
                    qrows, krows, pair_mask, group, rows.start,
                )
            go(*mark)
        gs[5 * layer : 5 * layer + 1, :] = column_sum(out[0])
        gs[5 * layer + 1 : 5 * layer + 2, :] = column_sum(out[2])
        go(*marks[2])
        dx_ref[rows, :] += (
            dot_t(out[0], wbuf[layer, 0])
            + (dot_t(out[1], wbuf[layer, 1]) + dot_t(out[2], wbuf[layer, 2]))
        )
        go(*marks[3])

    word_bias = length_bias(lengths, (WORDS_HERE, 1), 0)
    go(w1, u1, w0, u0)
    attend_back(
        d2[LANG, :], 1,
        [(LANG, LANG, turned_bias(WORDS_EACH, WORDS_EACH, word_bias))], q1, k1, v1, z1, d1,
        ([w1, u1, w0, u0, xm], [[y1]], [], [u1]),
    )
    attend_back(
        d2[VISN, :], 2,
        [(VISN, VISN, turned_bias(REGIONS_EACH, REGIONS_EACH, None))], q1, k1, v1, z1, d1,
        ([u0], [[y2]], [w1, w0], [u1, y1]),
    )
    attend_back(
        d1[...], 0,
        [
            (LANG, VISN, turned_bias(WORDS_EACH, REGIONS_EACH, None)),
            (VISN, LANG, turned_bias(REGIONS_EACH, WORDS_EACH, word_bias)),
        ],
        q0, k0, v0, z0, dx,
        ([u1, u0, y1], [[y0, u0, w1, w0, y1, y2, xm], [y0]], [sm], [u1, y2, u0]),
    )
    go(sm, y0, y2, y0, sm, w1, w0, y1, y0, y1, sm, y2, w1, w0, y2, y1, sm, y0, y2, y0, y0)
    for flow in range(9):
        for _ in range(9):
            go(flow)

    for unit in range(7):
        pltpu.make_async_copy(source_of(unit), landing(unit, rep), glocal.at[unit]).wait()
        for i in (1, 2):
            share_arrival(unit, i).wait_recv()
        for i in range(3):
            share_copy(unit, i).wait_send()
        for s in range(Z):

            @pl.when(straight[s])
            def _():
                column_copy(unit, s, share_of(unit, s)).wait_send()

        @pl.when(is_end)
        def _():
            stop_copy(unit).wait_send()

        @pl.when(is_middle)
        def _():
            column_copy(unit, 3 - z, stop_of(unit)).wait_send()

    for p in range(3):
        operand_copy(m0, p).wait_send()
    operand_across().wait_send()
    for t in range(2):
        for kind in range(2):
            half_across(kind, t).wait_send()
    for turn in range(2):
        piece_each(turn, lambda copy: copy.wait_send())
    for layer in range(3):
        if layer > 0:
            for p in range(3):
                y_copy(layer, p).wait_send()
        for i in range(4):
            y_forward(layer, i).wait_send()
    for t in range(2):
        for p in range(3):
            down_copy(t, p).wait_send()
    for unit in range(WIDE_UNITS):
        edge_copy(unit).wait_send()
    for i in range(3):
        small_copy(i).wait_send()
    for s in range(Z):

        @pl.when(s != z)
        def _():
            small_line(s).wait_send()


def backward(d2, lengths, vec, w, kept, gu, gd, gv, gb, rows):
    dma = pltpu.SemaphoreType.DMA
    sizes = [layer_rows.stop - layer_rows.start for layer_rows in LAYER_ROWS]

    def each(lead, width):
        return [pltpu.VMEM((*lead, n, width), LOW) for n in sizes]

    return pl.pallas_call(
        backward_kernel,
        out_shape=(
            jax.ShapeDtypeStruct((ROWS, D), FULL),
            jax.ShapeDtypeStruct((3, 4, SHARD, D), LOW),
            jax.ShapeDtypeStruct((2, SHARD, FF), LOW),
            jax.ShapeDtypeStruct((2, PART, D), LOW),
            jax.ShapeDtypeStruct((32, D), FULL),
        ),
        in_specs=[ONCHIP, pl.BlockSpec(memory_space=pltpu.SMEM), ONCHIP, HBM]
        + [ONCHIP] * 8
        + [HBM, HBM, ONCHIP, ONCHIP]
        + [HBM] * 6,
        out_specs=(ONCHIP, HBM, HBM, HBM, ONCHIP),
        scratch_shapes=[
            pltpu.VMEM((3, 4, D, D), LOW),
            *each((2, 4), D), *each((4,), D), *each((4,), D), *each((4,), PART),
            pltpu.VMEM((3, Z, 2 * SHARD, PART), LOW),
            pltpu.VMEM((2, Z, 2 * SHARD, PART), LOW),
            pltpu.VMEM((2, Z, 2 * SHARD, PART), LOW),
            pltpu.VMEM((2, 4, SHARD, D), LOW),
            pltpu.VMEM((2, 4, SHARD, D), LOW),
            pltpu.VMEM((2, Z, SHARD, D), LOW),
            pltpu.VMEM((WIDE_UNITS, Z, 2 * SHARD, PART), LOW),
            pltpu.VMEM((2, Z, SHARD, D), LOW),
            pltpu.VMEM((WIDE_UNITS, 2 * SHARD, PART), LOW),
            pltpu.VMEM((2, SHARD, D), LOW),
            pltpu.VMEM((WIDE_UNITS, 2 * SHARD, PART), LOW),
            pltpu.VMEM((WIDE_UNITS, SHARD, D), LOW),
            pltpu.VMEM((2, SHARD, D), LOW),
            pltpu.VMEM((ROWS, D), FULL),
            pltpu.VMEM((ROWS, D), LOW),
            *[pltpu.VMEM((32, D), FULL)] * 6,
            pltpu.VMEM((Z, 32, D), FULL),
            dma((3,)), dma((3, 2)),
            dma((4, 3)), dma((4, 3)), dma((3, 4)), dma((3, 4)),
            dma((2, 3)), dma((2, 3)), dma((2,)),
            dma((7, Z)), dma((7, Z)), dma((2, Z)), dma((2, Z)),
            dma((7,)), dma((7,)),
            dma((WIDE_UNITS,)), dma((WIDE_UNITS,)),
            dma((7, 3)), dma((7, 3)), dma((7,)),
            dma((3 + Z,)), dma((3 + Z,)),
            dma((3,)), dma((3,)), dma, dma, dma, dma((2, 2)), dma((2, 2)), dma((2, 2)),
        ],
        compiler_params=pltpu.CompilerParams(
            collective_id=2, has_side_effects=True, vmem_limit_bytes=VMEM_BYTES
        ),
        cost_estimate=pl.CostEstimate(
            flops=4_400_000_000, bytes_accessed=30_000_000, transcendentals=500_000
        ),
        name="attention_backward",
    )(d2, lengths, vec, w, *kept, gu, gd, gv, gb, *rows)


def finish_kernel(
    oa, ou, od, os, dx, lo, vo,
    wa, wu, wd, va, vf, vu, lang_grad, visn_grad, lang_out, visn_out,
):
    wa[...] = oa[...].astype(FULL)
    wu[...] = ou[...].astype(FULL)
    wd[...] = od[...].astype(FULL)

    @pl.when(pl.program_id(0) == 0)
    def _():
        lang_grad[...] = dx[LANG, :]
        visn_grad[...] = dx[VISN, :]
        lang_out[...] = lo[...]
        visn_out[...] = vo[...]
        spot = lax.axis_index("fsdp")
        z = lax.div(spot, 2)
        own = jnp.zeros((32, SHARD), FULL)
        for d in range(8):
            own = jnp.where(spot == d, os[:, SHARD * d : SHARD * d + SHARD], own)
        for i in range(5):
            for layer in range(3):
                va[i, layer : layer + 1, :] = own[5 * layer + i : 5 * layer + i + 1, :]
        for i in range(3):
            for t in range(2):
                vf[i, t : t + 1, :] = own[15 + 3 * t + i : 16 + 3 * t + i, :]
        for t in range(2):
            row = os[pl.ds(21 + 4 * t + z, 1), :]
            vu[t : t + 1, :] = jnp.where(spot == 2 * z, row[:, :PART], row[:, PART:])


def finish(oa, ou, od, os, dx, lo, vo):
    def whole(shape):
        return pl.BlockSpec(shape, lambda i: (0,) * len(shape))

    parts = [
        pl.BlockSpec((3, 1, SHARD, D), lambda i: (0, i, 0, 0)),
        pl.BlockSpec((2, SHARD, D), lambda i: (0, 0, i)),
        pl.BlockSpec((2, SHARD, D), lambda i: (0, i, 0)),
    ]
    words, regions = (WORDS_HERE, D), (REGIONS_HERE, D)
    smalls = [(5, 3, SHARD), (3, 2, SHARD), (2, PART)]
    singles = [*smalls, words, regions, words, regions]
    return pl.pallas_call(
        finish_kernel,
        grid=(4,),
        out_shape=tuple(jax.ShapeDtypeStruct(ref.shape, FULL) for ref in (oa, ou, od))
        + tuple(jax.ShapeDtypeStruct(shape, FULL) for shape in singles),
        in_specs=[*parts, whole((32, D)), whole((ROWS, D)), whole(words), whole(regions)],
        out_specs=(*parts, *[whole(shape) for shape in singles]),
        compiler_params=pltpu.CompilerParams(vmem_limit_bytes=VMEM_BYTES),
        cost_estimate=pl.CostEstimate(flops=0, bytes_accessed=15_000_000, transcendentals=0),
        name="widen_outputs",
    )(oa, ou, od, os, dx, lo, vo)


def fast_body(
    language, vision, lengths, attn_weights, attn_vectors, ffn_up, ffn_up_bias, ffn_down, ffn_vectors,
    language_cot, vision_cot,
):
    wide = ((0, 0), (0, PART - SHARD))
    vectors = [attn_vectors[i] for i in range(3)] + [ffn_vectors[i] for i in range(2)]
    small = jnp.concatenate([jnp.pad(piece, wide) for piece in vectors] + [ffn_up_bias])
    small = jnp.pad(small, ((0, 9), (0, 0)))
    wf, uf, df, vec, ub, xlow, onelow, two, *kept = gather(
        attn_weights, ffn_up, ffn_down, small, language, vision, lengths
    )
    q0, k0, v0, m0, z0, q1, k1, v1, m1, z1 = kept
    lo, vo, d2, gu, gd, gv, gb, ax1, ax2, bx1, bx2 = feed(
        two, language_cot, vision_cot, uf.reshape(D, D), df, vec, ub, onelow, m1,
        ffn_up, ffn_down,
    )
    dx, oa, ou, od, os = backward(
        d2, lengths, vec, wf.reshape(3, 4, D, D), (q0, k0, v0, z0, q1, k1, v1, z1),
        gu.reshape(2, Z, 2 * SHARD, D), gd.reshape(2, 2, 4, SHARD, D), gv, gb,
        (xlow, m0, ax1, ax2, bx1, bx2),
    )
    wa, wu, wd, va, vf, vu, lang_grad, visn_grad, lang_out, visn_out = finish(
        oa, ou, od, os, dx, lo, vo
    )
    va, vf = va.transpose(1, 0, 2), vf.transpose(1, 0, 2)
    return (lang_out, visn_out, lang_grad, visn_grad, wa, va, wu, vu, wd, vf)


def layer_norm(values, gain, shift):
    mean = jnp.mean(values, axis=-1, keepdims=True)
    centred = values - mean
    spread = jnp.mean(centred * centred, axis=-1, keepdims=True)
    return centred * jax.lax.rsqrt(spread + 1e-06) * (1.0 + gain) + shift


def gelu_exact(values):
    return jax.nn.gelu(values, approximate=False)


def project(inputs, matrix):
    return jnp.einsum("isd,de->ise", inputs, matrix, preferred_element_type=jnp.float32)


def project_back(grads, matrix):
    return jnp.einsum("ise,de->isd", grads, matrix, preferred_element_type=jnp.float32)


def outer_sum(inputs, grads):
    return jnp.einsum("isd,ise->de", inputs, grads, preferred_element_type=jnp.float32)


def row_total(grads):
    return jnp.sum(grads.astype(jnp.float32), axis=(0, 1))


def gather_attn(attn_weights, attn_vectors, layer_index):
    return (
        lax.all_gather(attn_weights[layer_index], "fsdp", axis=1, tiled=True),
        lax.all_gather(attn_vectors[layer_index], "fsdp", axis=1, tiled=True),
    )


def regather_attn(attn_weights, attn_vectors, layer_index):
    return (
        lax.all_gather(attn_weights[layer_index], "fsdp", axis=1, tiled=True),
        lax.all_gather(attn_vectors[layer_index], "fsdp", axis=1, tiled=True),
    )


def gather_ffn(ffn_up, ffn_up_bias, ffn_down, ffn_vectors, layer_index):
    return (
        lax.all_gather(ffn_up[layer_index], "fsdp", axis=0, tiled=True),
        lax.all_gather(ffn_up_bias[layer_index], "fsdp", axis=0, tiled=True),
        lax.all_gather(ffn_down[layer_index], "fsdp", axis=0, tiled=True),
        lax.all_gather(ffn_vectors[layer_index], "fsdp", axis=1, tiled=True),
    )


def regather_ffn(ffn_up, ffn_up_bias, ffn_down, ffn_vectors, layer_index):
    return (
        lax.all_gather(ffn_up[layer_index], "fsdp", axis=0, tiled=True),
        lax.all_gather(ffn_up_bias[layer_index], "fsdp", axis=0, tiled=True),
        lax.all_gather(ffn_down[layer_index], "fsdp", axis=0, tiled=True),
        lax.all_gather(ffn_vectors[layer_index], "fsdp", axis=1, tiled=True),
    )


def settle_attn(grad_weights, grad_vector):
    shards = (
        lax.psum_scatter(grad_weights, "fsdp", scatter_dimension=1, tiled=True),
        lax.psum_scatter(grad_vector, "fsdp", scatter_dimension=1, tiled=True),
    )
    quarter = lax.psum_scatter(
        shards[0].astype(jnp.bfloat16), "rep", scatter_dimension=2, tiled=True
    ).astype(jnp.float32)
    vector_sum = lax.psum(shards[1], "rep")
    whole = lax.all_gather(quarter.astype(jnp.bfloat16), "rep", axis=2, tiled=True).astype(
        quarter.dtype
    )
    return (whole, vector_sum)


def settle_ffn(grad_up, grad_up_bias, grad_down, grad_vector):
    shards = (
        lax.psum_scatter(grad_up, "fsdp", scatter_dimension=0, tiled=True),
        lax.psum_scatter(grad_up_bias, "fsdp", scatter_dimension=0, tiled=True),
        lax.psum_scatter(grad_down, "fsdp", scatter_dimension=0, tiled=True),
        lax.psum_scatter(grad_vector, "fsdp", scatter_dimension=1, tiled=True),
    )
    quarters = (
        lax.psum_scatter(
            shards[0].astype(jnp.bfloat16), "rep", scatter_dimension=1, tiled=True
        ).astype(jnp.float32),
        lax.psum_scatter(
            shards[2].astype(jnp.bfloat16), "rep", scatter_dimension=1, tiled=True
        ).astype(jnp.float32),
    )
    smalls = lax.psum((shards[1], shards[3]), "rep")
    wholes = (
        lax.all_gather(quarters[0].astype(jnp.bfloat16), "rep", axis=1, tiled=True).astype(
            jnp.float32
        ),
        lax.all_gather(quarters[1].astype(jnp.bfloat16), "rep", axis=1, tiled=True).astype(
            jnp.float32
        ),
    )
    return (wholes[0], smalls[0], wholes[1], smalls[1])


def attend_forward(residual, query_low, key_low, weights, vector, key_bias):
    item_count, query_len, model_width = residual.shape
    key_len = key_low.shape[1]
    head_size = model_width // HEADS
    vector = vector.astype(jnp.float32)
    queries = (project(query_low, weights[0]) + vector[0]).astype(jnp.bfloat16)
    key_heads = project(key_low, weights[1]).astype(jnp.bfloat16)
    values = (project(key_low, weights[2]) + vector[1]).astype(jnp.bfloat16)
    queries = queries.reshape(item_count, query_len, HEADS, head_size)
    key_heads = key_heads.reshape(item_count, key_len, HEADS, head_size)
    values = values.reshape(item_count, key_len, HEADS, head_size)
    scores = jnp.einsum(
        "iqhd,ikhd->ihqk", queries, key_heads, preferred_element_type=jnp.float32
    ) / math.sqrt(head_size)
    scores = scores + key_bias[:, None, None, :]
    highest = jnp.max(scores, axis=-1, keepdims=True)
    exponent = jnp.exp(scores - highest)
    attn_probs = exponent / jnp.sum(exponent, axis=-1, keepdims=True)
    mixed_heads = jnp.einsum(
        "ihqk,ikhd->iqhd",
        attn_probs.astype(jnp.bfloat16),
        values,
        preferred_element_type=jnp.float32,
    )
    mixed_heads = mixed_heads.astype(jnp.bfloat16).reshape(item_count, query_len, model_width)
    pre_norm = residual + (project(mixed_heads, weights[3]) + vector[2])
    normed = layer_norm(pre_norm, vector[3], vector[4])
    return (normed, (queries, key_heads, values, attn_probs, mixed_heads, pre_norm))


def attend_backward(grad_out, query_low, key_low, weights, vector, kept):
    queries, key_heads, values, attn_probs, mixed_heads, pre_norm = kept
    item_count, query_len, head_count, head_size = queries.shape
    key_len = key_heads.shape[1]
    model_width = head_count * head_size
    vector = vector.astype(jnp.float32)
    _, pull_norm = jax.vjp(layer_norm, pre_norm, vector[3], vector[4])
    grad_pre, grad_gain, grad_shift = pull_norm(grad_out)
    grad_branch = grad_pre.astype(jnp.bfloat16)
    grad_out_weight = outer_sum(mixed_heads, grad_branch)
    grad_mixed = project_back(grad_branch, weights[3]).astype(jnp.bfloat16)
    grad_mixed = grad_mixed.reshape(item_count, query_len, head_count, head_size)
    grad_probs = jnp.einsum(
        "iqhd,ikhd->ihqk", grad_mixed, values, preferred_element_type=jnp.float32
    )
    grad_values = jnp.einsum(
        "ihqk,iqhd->ikhd",
        attn_probs.astype(jnp.bfloat16),
        grad_mixed,
        preferred_element_type=jnp.float32,
    ).astype(jnp.bfloat16)
    grad_scores = attn_probs * (
        grad_probs - jnp.sum(attn_probs * grad_probs, axis=-1, keepdims=True)
    )
    grad_scores = grad_scores.astype(jnp.bfloat16)
    inverse = 1.0 / math.sqrt(head_size)
    grad_queries = (
        jnp.einsum("ihqk,ikhd->iqhd", grad_scores, key_heads, preferred_element_type=jnp.float32)
        * inverse
    )
    grad_queries = grad_queries.astype(jnp.bfloat16).reshape(item_count, query_len, model_width)
    grad_keys = (
        jnp.einsum("ihqk,iqhd->ikhd", grad_scores, queries, preferred_element_type=jnp.float32)
        * inverse
    )
    grad_keys = grad_keys.astype(jnp.bfloat16).reshape(item_count, key_len, model_width)
    grad_values = grad_values.reshape(item_count, key_len, model_width)
    grad_weights = jnp.stack(
        [
            outer_sum(query_low, grad_queries),
            outer_sum(key_low, grad_keys),
            outer_sum(key_low, grad_values),
            grad_out_weight,
        ]
    )
    grad_vector = jnp.stack(
        [
            row_total(grad_queries),
            row_total(grad_values),
            row_total(grad_branch),
            grad_gain,
            grad_shift,
        ]
    )
    grad_query_low = project_back(grad_queries, weights[0])
    grad_key_low = project_back(grad_keys, weights[1]) + project_back(grad_values, weights[2])
    return (grad_pre, grad_query_low, grad_key_low, grad_weights, grad_vector)


def feed_forward(residual, up_weight, up_bias, down_weight, vector):
    vector = vector.astype(jnp.float32)
    residual_low = residual.astype(jnp.bfloat16)
    hidden = project(residual_low, up_weight) + up_bias.astype(jnp.float32)
    active = gelu_exact(hidden).astype(jnp.bfloat16)
    pre_norm = residual + (project(active, down_weight) + vector[0])
    normed = layer_norm(pre_norm, vector[1], vector[2])
    return (normed, (residual_low, hidden, active, pre_norm))


def feed_backward(grad_out, up_weight, down_weight, vector, kept):
    residual_low, hidden, active, pre_norm = kept
    vector = vector.astype(jnp.float32)
    _, pull_norm = jax.vjp(layer_norm, pre_norm, vector[1], vector[2])
    grad_pre, grad_gain, grad_shift = pull_norm(grad_out)
    grad_branch = grad_pre.astype(jnp.bfloat16)
    grad_down = outer_sum(active, grad_branch)
    grad_active = project_back(grad_branch, down_weight)
    _, pull_gate = jax.vjp(gelu_exact, hidden)
    grad_hidden = pull_gate(grad_active)[0].astype(jnp.bfloat16)
    grad_up = outer_sum(residual_low, grad_hidden)
    grad_up_bias = row_total(grad_hidden)
    grad_residual = grad_pre + project_back(grad_hidden, up_weight)
    grad_vector = jnp.stack([row_total(grad_branch), grad_gain, grad_shift])
    return (grad_residual, grad_up, grad_up_bias, grad_down, grad_vector)


def body(
    language,
    vision,
    lengths,
    attn_weights,
    attn_vectors,
    ffn_up,
    ffn_up_bias,
    ffn_down,
    ffn_vectors,
    language_cot,
    vision_cot,
):
    item_count = lengths.shape[0]
    model_width = language.shape[1]
    word_slots = language.shape[0] // item_count
    region_slots = vision.shape[0] // item_count
    lang_rows = language.reshape(item_count, word_slots, model_width)
    visn_rows = vision.reshape(item_count, region_slots, model_width)
    word_bias = jnp.where(
        jnp.arange(word_slots)[None, :] < lengths[:, None], 0.0, -1000000000.0
    ).astype(jnp.float32)
    region_bias = jnp.zeros((item_count, region_slots), jnp.float32)
    cross_weights, cross_vector = gather_attn(attn_weights, attn_vectors, 0)
    lang_low = lang_rows.astype(jnp.bfloat16)
    visn_low = visn_rows.astype(jnp.bfloat16)
    lang_one = attend_forward(
        lang_rows, lang_low, visn_low, cross_weights, cross_vector, region_bias
    )[0]
    visn_one = attend_forward(
        visn_rows, visn_low, lang_low, cross_weights, cross_vector, word_bias
    )[0]
    lang_self = gather_attn(attn_weights, attn_vectors, 1)
    lang_one_low = lang_one.astype(jnp.bfloat16)
    lang_two, lang_self_kept = attend_forward(
        lang_one, lang_one_low, lang_one_low, lang_self[0], lang_self[1], word_bias
    )
    visn_self = gather_attn(attn_weights, attn_vectors, 2)
    visn_one_low = visn_one.astype(jnp.bfloat16)
    visn_two, visn_self_kept = attend_forward(
        visn_one, visn_one_low, visn_one_low, visn_self[0], visn_self[1], region_bias
    )
    lang_ffn = gather_ffn(ffn_up, ffn_up_bias, ffn_down, ffn_vectors, 0)
    lang_three, lang_ffn_kept = feed_forward(
        lang_two, lang_ffn[0], lang_ffn[1], lang_ffn[2], lang_ffn[3]
    )
    visn_ffn = gather_ffn(ffn_up, ffn_up_bias, ffn_down, ffn_vectors, 1)
    visn_three, visn_ffn_kept = feed_forward(
        visn_two, visn_ffn[0], visn_ffn[1], visn_ffn[2], visn_ffn[3]
    )
    visn_ffn_back = regather_ffn(ffn_up, ffn_up_bias, ffn_down, ffn_vectors, 1)
    visn_back = feed_backward(
        vision_cot.reshape(item_count, region_slots, model_width),
        visn_ffn_back[0],
        visn_ffn_back[2],
        visn_ffn_back[3],
        visn_ffn_kept,
    )
    visn_ffn_grads = settle_ffn(visn_back[1], visn_back[2], visn_back[3], visn_back[4])
    lang_ffn_back = regather_ffn(ffn_up, ffn_up_bias, ffn_down, ffn_vectors, 0)
    lang_back = feed_backward(
        language_cot.reshape(item_count, word_slots, model_width),
        lang_ffn_back[0],
        lang_ffn_back[2],
        lang_ffn_back[3],
        lang_ffn_kept,
    )
    lang_ffn_grads = settle_ffn(lang_back[1], lang_back[2], lang_back[3], lang_back[4])
    visn_self_back = regather_attn(attn_weights, attn_vectors, 2)
    visn_attn = attend_backward(
        visn_back[0],
        visn_one_low,
        visn_one_low,
        visn_self_back[0],
        visn_self_back[1],
        visn_self_kept,
    )
    visn_self_grads = settle_attn(visn_attn[3], visn_attn[4])
    grad_visn_one = visn_attn[0] + visn_attn[1] + visn_attn[2]
    lang_self_back = regather_attn(attn_weights, attn_vectors, 1)
    lang_attn = attend_backward(
        lang_back[0],
        lang_one_low,
        lang_one_low,
        lang_self_back[0],
        lang_self_back[1],
        lang_self_kept,
    )
    lang_self_grads = settle_attn(lang_attn[3], lang_attn[4])
    grad_lang_one = lang_attn[0] + lang_attn[1] + lang_attn[2]
    cross_back = regather_attn(attn_weights, attn_vectors, 0)
    lang_cross_kept = attend_forward(
        lang_rows, lang_low, visn_low, cross_back[0], cross_back[1], region_bias
    )[1]
    visn_cross_kept = attend_forward(
        visn_rows, visn_low, lang_low, cross_back[0], cross_back[1], word_bias
    )[1]
    lang_cross = attend_backward(
        grad_lang_one, lang_low, visn_low, cross_back[0], cross_back[1], lang_cross_kept
    )
    visn_cross = attend_backward(
        grad_visn_one, visn_low, lang_low, cross_back[0], cross_back[1], visn_cross_kept
    )
    cross_grads = settle_attn(lang_cross[3] + visn_cross[3], lang_cross[4] + visn_cross[4])
    grad_language = lang_cross[0] + lang_cross[1] + visn_cross[2]
    grad_vision = visn_cross[0] + visn_cross[1] + lang_cross[2]
    return (
        lang_three.reshape(item_count * word_slots, model_width),
        visn_three.reshape(item_count * region_slots, model_width),
        grad_language.reshape(item_count * word_slots, model_width),
        grad_vision.reshape(item_count * region_slots, model_width),
        jnp.stack([cross_grads[0], lang_self_grads[0], visn_self_grads[0]]),
        jnp.stack([cross_grads[1], lang_self_grads[1], visn_self_grads[1]]),
        jnp.stack([lang_ffn_grads[0], visn_ffn_grads[0]]),
        jnp.stack([lang_ffn_grads[1], visn_ffn_grads[1]]),
        jnp.stack([lang_ffn_grads[2], visn_ffn_grads[2]]),
        jnp.stack([lang_ffn_grads[3], visn_ffn_grads[3]]),
    )


def solution(mesh):
    shape = dict(mesh.shape)
    fast = shape["rep"] == 4 and shape["fsdp"] == 8
    return jax.shard_map(
        fast_body if fast else body,
        mesh=mesh,
        in_specs=(
            P(("rep", "fsdp"), None),
            P(("rep", "fsdp"), None),
            P(("rep", "fsdp")),
            P(None, None, "fsdp", None),
            P(None, None, "fsdp"),
            P(None, "fsdp", None),
            P(None, "fsdp"),
            P(None, "fsdp", None),
            P(None, None, "fsdp"),
            P(("rep", "fsdp"), None),
            P(("rep", "fsdp"), None),
        ),
        out_specs=(
            P(("rep", "fsdp"), None),
            P(("rep", "fsdp"), None),
            P(("rep", "fsdp"), None),
            P(("rep", "fsdp"), None),
            P(None, None, "fsdp", None),
            P(None, None, "fsdp"),
            P(None, "fsdp", None),
            P(None, "fsdp"),
            P(None, "fsdp", None),
            P(None, None, "fsdp"),
        ),
        check_vma=False,
    )
```
